32 devices in a mesh: dp: 16 (over z, y, core), tap: 2 (over x).
Axes of the slice: x: 2, y: 2, z: 4, core: 2. Of those that a mesh axis runs over, the one named last changes fastest.
Arguments:
- block_input: bfloat16 [32768, 512], P('dp'), may hold values from -6 to 6
- conv_weight: bfloat16 [10, 512, 512], P('tap'), may hold values from -0.09375 to 0.09375
- slot_tap_table: int32 [10], P('tap'), may hold values from 0 to 8, as said below
- conv_bias: float32 [512], replicated, may hold values from -3 to 3
- conv_norm_gain: float32 [512], replicated, may hold values from 0.5 to 1.5
- conv_norm_bias: float32 [512], replicated, may hold values from -3 to 3
- w_in: bfloat16 [512, 2048], replicated, may hold values from -0.25 to 0.25
- b_in: float32 [2048], replicated, may hold values from -3 to 3
- w_out: bfloat16 [2048, 512], replicated, may hold values from -0.125 to 0.125
- b_out: float32 [512], replicated, may hold values from -3 to 3
- ffn_norm_gain: float32 [512], replicated, may hold values from 0.5 to 1.5
- ffn_norm_bias: float32 [512], replicated, may hold values from -3 to 3
- species_id: int32 [64], P('dp'), may hold values from 0 to 15, as said below
- species_count: int32 [16], replicated, may hold values from 1 to 7, as said below
- out_grad: bfloat16 [32768, 512], P(('dp', 'tap')), may hold values from -6 to 6
Outputs:
- block_output: bfloat16 [32768, 512], P(('dp', 'tap'))
- input_grad: float32 [32768, 512], P(('dp', 'tap'))
- conv_weight_grad: float32 [10, 512, 512], P('tap', 'dp')
- conv_bias_grad: float32 [512], P(('dp', 'tap'))
- conv_norm_gain_grad: float32 [512], P(('dp', 'tap'))
- conv_norm_bias_grad: float32 [512], P(('dp', 'tap'))
- w_in_grad: float32 [512, 2048], P(('dp', 'tap'))
- b_in_grad: float32 [2048], P(('dp', 'tap'))
- w_out_grad: float32 [2048, 512], P(('dp', 'tap'))
- b_out_grad: float32 [512], P(('dp', 'tap'))
- ffn_norm_gain_grad: float32 [512], P(('dp', 'tap'))
- ffn_norm_bias_grad: float32 [512], P(('dp', 'tap'))
The draws below stay inside these ranges and needn't reach their ends.
Inputs may be any that keep to these rules, and one draw needn't show every extreme that they name: `species_id`: windows are grouped by species: ids never fall along the windows, and species s has exactly species_count[s] windows. `species_count`: the counts sum to 64; species 2i and 2i + 1 together have 8 windows. `slot_tap_table`: each of the 9 taps is applied by at least one slot.
All inputs are finite; a program needn't handle non-finite values.
Results may differ from the reference program's by a relative error of at most 0.0065.
Values may be sent and summed in bfloat16 or wider, within the bound.
No kernel may reach another device: no remote copies, remote signals or barrier semaphores. Data moves between devices by JAX's collectives and lax.ppermute only.
A program may use at most 128 MiB of HBM per device.

```python
import jax
import jax.numpy as jnp
from jax import lax

C = 512
FF = 2048
KERNEL_TAPS = 9
DILATION_STEP = 16
WINDOW_LENGTH = 512
SLOTS = 10
WINDOWS = 64
TOKENS = 32768


def species_layout(key):
    pair_count = WINDOWS // 8
    first = jax.random.randint(jax.random.fold_in(key, 11), (pair_count,), 1, 8)
    chosen = jax.random.randint(jax.random.fold_in(key, 12), (), 0, pair_count)
    first = jnp.where(jnp.arange(pair_count) == chosen, 7, first)
    counts = jnp.stack([first, 8 - first], axis=1).reshape(-1).astype(jnp.int32)
    ends = jnp.cumsum(counts)
    window_pos = jnp.arange(WINDOWS)
    ids = jnp.sum((ends[None, :] <= window_pos[:, None]).astype(jnp.int32), axis=1)
    return (counts, ids.astype(jnp.int32))


def draw_species_id(key, part):
    counts, ids = species_layout(key)
    return ids


def draw_species_count(key, part):
    counts, ids = species_layout(key)
    return counts


def draw_slot_tap_table(key, part):
    key = jax.random.fold_in(key, 21)
    order = jax.random.permutation(key, SLOTS).astype(jnp.int32)
    extra = jax.random.randint(jax.random.fold_in(key, 22), (SLOTS,), 0, KERNEL_TAPS)
    return jnp.where(order < KERNEL_TAPS, order, extra).astype(jnp.int32)


def shard_levels(own_key, shape, split, low, largest):
    gain, own = 1.0, jax.random.fold_in(own_key, 6)
    for axis_at, blocks in split:
        heights = jnp.exp(jax.random.uniform(jax.random.fold_in(own, axis_at), (blocks,), jnp.float32, low / len(split), largest / len(split)))
        gain = gain * jnp.repeat(heights, shape[axis_at] // blocks).reshape([-1 if axis == axis_at else 1 for axis in range(len(shape))])
    return gain


def centred(own_key, shape, deviation, reach, cuts=(), dtype=jnp.bfloat16):
    entries = deviation * jax.random.normal(own_key, shape, jnp.float32)
    if cuts:
        entries = entries * shard_levels(own_key, shape, cuts, -0.22, 0.18)
    return jnp.clip(entries, -reach, reach).astype(dtype)


def setup_inputs(seed: int = 0) -> dict:
    splits = jax.random.split(jax.random.key(seed), 16)
    block_input = centred(splits[0], (TOKENS, C), 1.0, 6.0, ((0, 16),))
    conv_weight = centred(splits[1], (SLOTS, C, C), (KERNEL_TAPS * C) ** -0.5, 0.09375, ((0, 2),))
    slot_tap_table = draw_slot_tap_table(jax.random.fold_in(splits[15], 71), 0)
    conv_bias = centred(splits[3], (C,), 0.5, 3.0, (), jnp.float32)
    conv_norm_gain = jnp.clip(1.0 + 0.1 * jax.random.normal(splits[4], (C,), jnp.float32), 0.5, 1.5)
    conv_norm_bias = centred(splits[5], (C,), 0.5, 3.0, (), jnp.float32)
    w_in = centred(splits[6], (C, FF), C ** -0.5, 0.25)
    b_in = centred(splits[7], (FF,), 0.5, 3.0, (), jnp.float32)
    w_out = centred(splits[8], (FF, C), FF ** -0.5, 0.125)
    b_out = centred(splits[9], (C,), 0.5, 3.0, (), jnp.float32)
    ffn_norm_gain = jnp.clip(1.0 + 0.1 * jax.random.normal(splits[10], (C,), jnp.float32), 0.5, 1.5)
    ffn_norm_bias = centred(splits[11], (C,), 0.5, 3.0, (), jnp.float32)
    species_id = draw_species_id(jax.random.fold_in(splits[15], 71), 0)
    species_count = draw_species_count(jax.random.fold_in(splits[15], 71), 0)
    out_grad = centred(splits[14], (TOKENS, C), 1.0, 6.0, ((0, 32),))
    return dict(block_input=block_input, conv_weight=conv_weight, slot_tap_table=slot_tap_table, conv_bias=conv_bias, conv_norm_gain=conv_norm_gain, conv_norm_bias=conv_norm_bias, w_in=w_in, b_in=b_in, w_out=w_out, b_out=b_out, ffn_norm_gain=ffn_norm_gain, ffn_norm_bias=ffn_norm_bias, species_id=species_id, species_count=species_count, out_grad=out_grad)


@jax.custom_vjp
def low(v):
    return lax.optimization_barrier(v.astype(jnp.bfloat16)).astype(jnp.float32)

@jax.custom_vjp
def low_back(v):
    return v

def low_keep(v):
    return (low(v), None)

def low_pass(kept, grad):
    return (grad,)

def back_keep(v):
    return (v, None)

def back_low(kept, grad):
    return (low(grad),)
low.defvjp(low_keep, low_pass)
low_back.defvjp(back_keep, back_low)

def layer_norm(values):
    mean_val = lax.optimization_barrier(jnp.mean(values, axis=-1, keepdims=True))
    center = values - mean_val
    spread = lax.optimization_barrier(jnp.mean(center * center, axis=-1, keepdims=True))
    return center * lax.rsqrt(spread + 1e-05)

def reference(block_input, conv_weight, slot_tap_table, conv_bias, conv_norm_gain, conv_norm_bias, w_in, b_in, w_out, b_out, ffn_norm_gain, ffn_norm_bias, species_id, species_count, out_grad):
    chan_width = block_input.shape[1]
    group_wins = 8
    groups = WINDOWS // group_wins
    tap_extent = KERNEL_TAPS // 2 * DILATION_STEP
    high = lax.Precision.HIGHEST
    window_scale = 4.0 / species_count[species_id].astype(jnp.float32)
    x_groups = block_input.astype(jnp.float32).reshape(groups, group_wins, WINDOW_LENGTH, chan_width)
    g_groups = out_grad.astype(jnp.float32).reshape(groups, group_wins, WINDOW_LENGTH, chan_width) * window_scale.reshape(groups, group_wins, 1, 1)
    params = (conv_weight.astype(jnp.float32), conv_bias, conv_norm_gain, conv_norm_bias, w_in.astype(jnp.float32), b_in, w_out.astype(jnp.float32), b_out, ffn_norm_gain, ffn_norm_bias)

    def forward(win_x, weights):
        c_weight, c_bias, gain_one, bias_one, wi, bi, wo, bo, gain_two, bias_two = weights
        padded_input = jnp.pad(win_x, ((0, 0), (tap_extent, tap_extent), (0, 0)))
        conv = jnp.zeros(win_x.shape, jnp.float32)
        for index_of_slot in range(slot_tap_table.shape[0]):
            shifted_input = lax.dynamic_slice_in_dim(padded_input, slot_tap_table[index_of_slot] * DILATION_STEP, WINDOW_LENGTH, 1)
            conv = conv + jnp.einsum('gwc,co->gwo', shifted_input, c_weight[index_of_slot], precision=high)
        pre_conv = low_back(conv + c_bias)
        norm_one = layer_norm(jax.nn.gelu(pre_conv, approximate=False)) * gain_one + bias_one
        hidden = win_x + norm_one
        hidden_low = low(hidden)
        pre_up = low_back(jnp.einsum('gwc,cf->gwf', hidden_low, wi, precision=high) + bi)
        act_low = low(jax.nn.gelu(pre_up, approximate=False))
        pre_out = low_back(jnp.einsum('gwf,fc->gwc', act_low, wo, precision=high) + bo)
        norm_two = layer_norm(pre_out) * gain_two + bias_two
        return hidden + norm_two

    def step(totals, pieces):
        x_part, g_part = pieces
        y_part, back_fn = jax.vjp(forward, x_part, params)
        d_x, d_params = back_fn(g_part)
        totals = jax.tree.map(lambda left, right: left + right, totals, d_params)
        return (totals, (y_part, d_x))
    zeros = jax.tree.map(jnp.zeros_like, params)
    totals, (outputs, input_grads) = lax.scan(step, zeros, (x_groups, g_groups))
    block_output = outputs.reshape(TOKENS, chan_width).astype(jnp.bfloat16)
    input_grad = input_grads.reshape(TOKENS, chan_width)
    return (block_output, input_grad, totals[0], totals[1], totals[2], totals[3], totals[4], totals[5], totals[6], totals[7], totals[8], totals[9])
```

```python
import jax
import jax.numpy as jnp
from jax import lax
from jax.sharding import PartitionSpec as P

KERNEL_TAPS = 9
DILATION_STEP = 16
WINDOW_LENGTH = 512


def layer_norm(values):
    mean_val = jnp.mean(values, axis=-1, keepdims=True)
    center = values - mean_val
    spread = jnp.mean(center * center, axis=-1, keepdims=True)
    return center * lax.rsqrt(spread + 1e-05)


def exact_gelu(values):
    return jax.nn.gelu(values, approximate=False)


def conv_branch(pre_conv, gain_one, bias_one):
    return layer_norm(exact_gelu(pre_conv)) * gain_one + bias_one


def ffn_branch(pre_out, gain_two, bias_two):
    return layer_norm(pre_out) * gain_two + bias_two


def shift_stack(win_rows, tap_table, forward):
    tap_extent = KERNEL_TAPS // 2 * DILATION_STEP
    padded_input = jnp.pad(win_rows, ((0, 0), (tap_extent, tap_extent), (0, 0)))
    pieces = []
    for index_of_slot in range(tap_table.shape[0]):
        if forward:
            tap_offset = tap_table[index_of_slot]
        else:
            tap_offset = KERNEL_TAPS - 1 - tap_table[index_of_slot]
        shifted_input = lax.dynamic_slice_in_dim(
            padded_input, tap_offset * DILATION_STEP, WINDOW_LENGTH, 1
        )
        pieces.append(shifted_input.reshape(-1, win_rows.shape[2]))
    return jnp.stack(pieces)


def contract_rows(left, right):
    return lax.dot_general(
        left, right, (((0,), (0,)), ((), ())), preferred_element_type=jnp.float32
    )


def contract_cols(left, right):
    return lax.dot_general(
        left, right, (((1,), (1,)), ((), ())), preferred_element_type=jnp.float32
    )


def swap_dp(value, bit):
    count = lax.axis_size("dp")
    return lax.ppermute(value, "dp", [(i, i ^ (1 << bit)) for i in range(count)])


def swap_tap(value):
    return lax.ppermute(value, "tap", [(0, 1), (1, 0)])


def halve(part, order, kind):
    dp_bits = (lax.axis_size("dp") - 1).bit_length()
    place = lax.axis_index("dp")
    tap = lax.axis_index("tap")
    labels = ["t"] + list(range(dp_bits - 1, -1, -1))
    for step in order:
        axis = labels.index(step)
        labels.pop(axis)
        mine = tap if step == "t" else (place >> step) & 1
        keep = lax.dynamic_index_in_dim(part, mine, axis, keepdims=False)
        send = lax.dynamic_index_in_dim(part, 1 - mine, axis, keepdims=False).astype(kind)
        got = swap_tap(send) if step == "t" else swap_dp(send, step)
        part = keep + got.astype(jnp.float32)
    return part


def orders(dp_bits):
    rest = list(range(2, dp_bits))
    first = [0, "t", 1] + rest
    second = [0, 1] + rest[:1] + ["t"] + rest[1:]
    third = [0] + rest[:1] + ["t", 1] + rest[1:]
    return first, second, third


def shards(
    block_input,
    conv_weight,
    slot_tap_table,
    conv_bias,
    conv_norm_gain,
    conv_norm_bias,
    w_in,
    b_in,
    w_out,
    b_out,
    ffn_norm_gain,
    ffn_norm_bias,
    species_id,
    species_count,
    out_grad,
):
    tap_count = lax.axis_size("tap")
    my_index = lax.axis_index("tap")
    core = lax.axis_index("dp") & 1
    dp_bits = (lax.axis_size("dp") - 1).bit_length()
    tok_dev, chan_width = block_input.shape
    hid_width = w_in.shape[1]
    half_rows = tok_dev // tap_count
    windows = tok_dev // WINDOW_LENGTH
    my_windows = windows // tap_count
    own_slots = conv_weight.shape[0]
    half_chan = chan_width // 2
    first, second, third = orders(dp_bits)

    other_table = swap_tap(slot_tap_table)
    part_send = lax.dynamic_slice_in_dim(conv_weight, core * half_chan, half_chan, 1)
    part_here = swap_tap(part_send)
    part_mate = swap_dp(part_here, 0)
    low_part = jnp.where(core == 0, part_here, part_mate)
    high_part = jnp.where(core == 0, part_mate, part_here)
    other_weight = jnp.concatenate([low_part, high_part], axis=1)

    my_x = lax.dynamic_slice_in_dim(block_input, my_index * half_rows, half_rows, 0)
    x_windows = my_x.reshape(my_windows, WINDOW_LENGTH, chan_width)
    mine_x = my_x.astype(jnp.float32)
    own_stack = shift_stack(x_windows, slot_tap_table, True)
    other_stack = shift_stack(x_windows, other_table, True)
    conv_out = jnp.einsum("str,sro->to", own_stack, conv_weight, preferred_element_type=jnp.float32)
    conv_out = conv_out + jnp.einsum(
        "str,sro->to", other_stack, other_weight, preferred_element_type=jnp.float32
    )
    pre_conv = conv_out + conv_bias
    norm_one, conv_back = jax.vjp(conv_branch, pre_conv, conv_norm_gain, conv_norm_bias)
    hidden = mine_x + norm_one
    hidden_low = hidden.astype(jnp.bfloat16)
    pre_up = jnp.dot(hidden_low, w_in, preferred_element_type=jnp.float32) + b_in
    activ, activ_back = jax.vjp(exact_gelu, pre_up)
    act_low = activ.astype(jnp.bfloat16)
    pre_out = jnp.dot(act_low, w_out, preferred_element_type=jnp.float32) + b_out
    norm_two, ffn_back = jax.vjp(ffn_branch, pre_out, ffn_norm_gain, ffn_norm_bias)
    block_output = (hidden + norm_two).astype(jnp.bfloat16)
    my_species = lax.dynamic_slice_in_dim(species_id, my_index * my_windows, my_windows, 0)
    species_range = jnp.arange(species_count.shape[0], dtype=jnp.int32)
    matches = my_species[:, None] == species_range[None, :]
    window_count = jnp.sum(jnp.where(matches, species_count[None, :], 0), axis=1)
    window_scale = 4.0 / window_count.astype(jnp.float32)
    grad_y = (
        out_grad.astype(jnp.float32).reshape(my_windows, WINDOW_LENGTH, chan_width)
        * window_scale[:, None, None]
    ).reshape(half_rows, chan_width)
    d_pre_out, d_gain_two, d_bias_two = ffn_back(grad_y)
    d_out_low = d_pre_out.astype(jnp.bfloat16)
    d_w_out = contract_rows(act_low, d_out_low)
    d_b_out = jnp.sum(d_out_low.astype(jnp.float32), axis=0)
    d_activ = contract_cols(d_out_low, w_out)
    (d_pre_up,) = activ_back(d_activ)
    d_up_low = d_pre_up.astype(jnp.bfloat16)
    d_w_in = contract_rows(hidden_low, d_up_low)
    d_b_in = jnp.sum(d_up_low.astype(jnp.float32), axis=0)
    d_hidden = grad_y + contract_cols(d_up_low, w_in)
    d_pre_conv, d_gain_one, d_bias_one = conv_back(d_hidden)
    d_conv_low = d_pre_conv.astype(jnp.bfloat16)
    d_conv_bias = jnp.sum(d_conv_low.astype(jnp.float32), axis=0)
    d_windows = d_conv_low.reshape(my_windows, WINDOW_LENGTH, chan_width)
    own_back = shift_stack(d_windows, slot_tap_table, False)
    other_back = shift_stack(d_windows, other_table, False)
    input_grad = (
        d_hidden
        + jnp.einsum("sto,sro->tr", own_back, conv_weight, preferred_element_type=jnp.float32)
        + jnp.einsum("sto,sro->tr", other_back, other_weight, preferred_element_type=jnp.float32)
    )
    own_terms = jnp.einsum("str,to->sro", own_stack, d_conv_low, preferred_element_type=jnp.float32)
    other_terms = jnp.einsum(
        "str,to->sro", other_stack, d_conv_low, preferred_element_type=jnp.float32
    )
    bits = [2] * dp_bits

    def by_tap(own, other):
        return jnp.where(my_index == 0, jnp.stack([own, other]), jnp.stack([other, own]))

    def conv_part(begin, end, order):
        own = own_terms[begin:end]
        other = other_terms[begin:end]
        both = by_tap(own, other)
        rows = chan_width >> dp_bits
        both = both.reshape([2, end - begin] + bits + [rows, chan_width])
        return halve(jnp.moveaxis(both, 1, 1 + dp_bits), order, jnp.bfloat16)

    cut = own_slots * 2 // 5
    conv_weight_grad = jnp.concatenate(
        [
            conv_part(0, cut, first),
            conv_part(cut, 2 * cut, second),
            conv_part(2 * cut, own_slots, third),
        ]
    )

    def spread(total, order, kind):
        rows = total.shape[0] >> (dp_bits + 1)
        split = total.reshape(bits + [2, rows] + list(total.shape[1:]))
        return halve(jnp.moveaxis(split, dp_bits, 0), order, kind)

    d_w_out_mine = spread(d_w_out, first, jnp.bfloat16)
    d_w_in_mine = spread(d_w_in, second, jnp.bfloat16)
    owners = 2 << dp_bits
    small = [d_b_in, d_b_out, d_conv_bias, d_gain_one, d_bias_one, d_gain_two, d_bias_two]
    joined = jnp.concatenate([v.reshape(owners, -1) for v in small], axis=1)
    joined_mine = spread(joined, third, jnp.float32).reshape(-1)
    vectors = []
    start = 0
    for v in small:
        size = v.shape[0] // owners
        vectors.append(joined_mine[start : start + size])
        start += size
    return (
        block_output,
        input_grad,
        conv_weight_grad,
        vectors[2],
        vectors[3],
        vectors[4],
        d_w_in_mine,
        vectors[0],
        d_w_out_mine,
        vectors[1],
        vectors[5],
        vectors[6],
    )


def solution(mesh):
    return jax.shard_map(
        shards,
        mesh=mesh,
        in_specs=(
            P("dp", None),
            P("tap", None, None),
            P("tap"),
            P(),
            P(),
            P(),
            P(),
            P(),
            P(),
            P(),
            P(),
            P(),
            P("dp"),
            P(),
            P(("dp", "tap"), None),
        ),
        out_specs=(
            P(("dp", "tap"), None),
            P(("dp", "tap"), None),
            P("tap", "dp", None),
            P(("dp", "tap")),
            P(("dp", "tap")),
            P(("dp", "tap")),
            P(("dp", "tap"), None),
            P(("dp", "tap")),
            P(("dp", "tap"), None),
            P(("dp", "tap")),
            P(("dp", "tap")),
            P(("dp", "tap")),
        ),
        check_vma=False,
    )
```

```python
import functools

import jax
import jax.numpy as jnp
from jax import lax
from jax.experimental import pallas as pl
from jax.experimental.pallas import tpu as pltpu
from jax.sharding import PartitionSpec as P

KERNEL_TAPS = 9
DILATION_STEP = 16
WINDOW_LENGTH = 512


def layer_norm(values):
    mean_val = jnp.mean(values, axis=-1, keepdims=True)
    center = values - mean_val
    spread = jnp.mean(center * center, axis=-1, keepdims=True)
    return center * lax.rsqrt(spread + 1e-05)


def exact_gelu(values):
    return jax.nn.gelu(values, approximate=False)


def conv_branch(pre_conv, gain_one, bias_one):
    return layer_norm(exact_gelu(pre_conv)) * gain_one + bias_one


def ffn_branch(pre_out, gain_two, bias_two):
    return layer_norm(pre_out) * gain_two + bias_two


def shift_stack(win_rows, tap_table, forward):
    tap_extent = KERNEL_TAPS // 2 * DILATION_STEP
    padded_input = jnp.pad(win_rows, ((0, 0), (tap_extent, tap_extent), (0, 0)))
    pieces = []
    for index_of_slot in range(tap_table.shape[0]):
        if forward:
            tap_offset = tap_table[index_of_slot]
        else:
            tap_offset = KERNEL_TAPS - 1 - tap_table[index_of_slot]
        shifted_input = lax.dynamic_slice_in_dim(
            padded_input, tap_offset * DILATION_STEP, WINDOW_LENGTH, 1
        )
        pieces.append(shifted_input.reshape(-1, win_rows.shape[2]))
    return jnp.stack(pieces)


def contract_rows(left, right):
    return lax.dot_general(
        left, right, (((0,), (0,)), ((), ())), preferred_element_type=jnp.float32
    )


def contract_cols(left, right):
    return lax.dot_general(
        left, right, (((1,), (1,)), ((), ())), preferred_element_type=jnp.float32
    )


def swap_dp(value, bit):
    count = lax.axis_size("dp")
    return lax.ppermute(value, "dp", [(i, i ^ (1 << bit)) for i in range(count)])


def swap_tap(value):
    return lax.ppermute(value, "tap", [(0, 1), (1, 0)])


def halve(part, order, kind):
    dp_bits = (lax.axis_size("dp") - 1).bit_length()
    place = lax.axis_index("dp")
    tap = lax.axis_index("tap")
    labels = ["t"] + list(range(dp_bits - 1, -1, -1))
    for step in order:
        axis = labels.index(step)
        labels.pop(axis)
        mine = tap if step == "t" else (place >> step) & 1
        keep = lax.dynamic_index_in_dim(part, mine, axis, keepdims=False)
        send = lax.dynamic_index_in_dim(part, 1 - mine, axis, keepdims=False).astype(kind)
        got = swap_tap(send) if step == "t" else swap_dp(send, step)
        part = keep + got.astype(jnp.float32)
    return part


def orders(dp_bits):
    rest = list(range(2, dp_bits))
    first = [0, "t", 1] + rest
    second = [0, 1] + rest[:1] + ["t"] + rest[1:]
    third = [0] + rest[:1] + ["t", 1] + rest[1:]
    return first, second, third


def plain_shards(
    block_input,
    conv_weight,
    slot_tap_table,
    conv_bias,
    conv_norm_gain,
    conv_norm_bias,
    w_in,
    b_in,
    w_out,
    b_out,
    ffn_norm_gain,
    ffn_norm_bias,
    species_id,
    species_count,
    out_grad,
):
    tap_count = lax.axis_size("tap")
    my_index = lax.axis_index("tap")
    core = lax.axis_index("dp") & 1
    dp_bits = (lax.axis_size("dp") - 1).bit_length()
    tok_dev, chan_width = block_input.shape
    hid_width = w_in.shape[1]
    half_rows = tok_dev // tap_count
    windows = tok_dev // WINDOW_LENGTH
    my_windows = windows // tap_count
    own_slots = conv_weight.shape[0]
    half_chan = chan_width // 2
    first, second, third = orders(dp_bits)

    other_table = swap_tap(slot_tap_table)
    part_send = lax.dynamic_slice_in_dim(conv_weight, core * half_chan, half_chan, 1)
    part_here = swap_tap(part_send)
    part_mate = swap_dp(part_here, 0)
    low_part = jnp.where(core == 0, part_here, part_mate)
    high_part = jnp.where(core == 0, part_mate, part_here)
    other_weight = jnp.concatenate([low_part, high_part], axis=1)

    my_x = lax.dynamic_slice_in_dim(block_input, my_index * half_rows, half_rows, 0)
    x_windows = my_x.reshape(my_windows, WINDOW_LENGTH, chan_width)
    mine_x = my_x.astype(jnp.float32)
    own_stack = shift_stack(x_windows, slot_tap_table, True)
    other_stack = shift_stack(x_windows, other_table, True)
    conv_out = jnp.einsum("str,sro->to", own_stack, conv_weight, preferred_element_type=jnp.float32)
    conv_out = conv_out + jnp.einsum(
        "str,sro->to", other_stack, other_weight, preferred_element_type=jnp.float32
    )
    pre_conv = conv_out + conv_bias
    norm_one, conv_back = jax.vjp(conv_branch, pre_conv, conv_norm_gain, conv_norm_bias)
    hidden = mine_x + norm_one
    hidden_low = hidden.astype(jnp.bfloat16)
    pre_up = jnp.dot(hidden_low, w_in, preferred_element_type=jnp.float32) + b_in
    activ, activ_back = jax.vjp(exact_gelu, pre_up)
    act_low = activ.astype(jnp.bfloat16)
    pre_out = jnp.dot(act_low, w_out, preferred_element_type=jnp.float32) + b_out
    norm_two, ffn_back = jax.vjp(ffn_branch, pre_out, ffn_norm_gain, ffn_norm_bias)
    block_output = (hidden + norm_two).astype(jnp.bfloat16)
    my_species = lax.dynamic_slice_in_dim(species_id, my_index * my_windows, my_windows, 0)
    species_range = jnp.arange(species_count.shape[0], dtype=jnp.int32)
    matches = my_species[:, None] == species_range[None, :]
    window_count = jnp.sum(jnp.where(matches, species_count[None, :], 0), axis=1)
    window_scale = 4.0 / window_count.astype(jnp.float32)
    grad_y = (
        out_grad.astype(jnp.float32).reshape(my_windows, WINDOW_LENGTH, chan_width)
        * window_scale[:, None, None]
    ).reshape(half_rows, chan_width)
    d_pre_out, d_gain_two, d_bias_two = ffn_back(grad_y)
    d_out_low = d_pre_out.astype(jnp.bfloat16)
    d_w_out = contract_rows(act_low, d_out_low)
    d_b_out = jnp.sum(d_out_low.astype(jnp.float32), axis=0)
    d_activ = contract_cols(d_out_low, w_out)
    (d_pre_up,) = activ_back(d_activ)
    d_up_low = d_pre_up.astype(jnp.bfloat16)
    d_w_in = contract_rows(hidden_low, d_up_low)
    d_b_in = jnp.sum(d_up_low.astype(jnp.float32), axis=0)
    d_hidden = grad_y + contract_cols(d_up_low, w_in)
    d_pre_conv, d_gain_one, d_bias_one = conv_back(d_hidden)
    d_conv_low = d_pre_conv.astype(jnp.bfloat16)
    d_conv_bias = jnp.sum(d_conv_low.astype(jnp.float32), axis=0)
    d_windows = d_conv_low.reshape(my_windows, WINDOW_LENGTH, chan_width)
    own_back = shift_stack(d_windows, slot_tap_table, False)
    other_back = shift_stack(d_windows, other_table, False)
    input_grad = (
        d_hidden
        + jnp.einsum("sto,sro->tr", own_back, conv_weight, preferred_element_type=jnp.float32)
        + jnp.einsum("sto,sro->tr", other_back, other_weight, preferred_element_type=jnp.float32)
    )
    own_terms = jnp.einsum("str,to->sro", own_stack, d_conv_low, preferred_element_type=jnp.float32)
    other_terms = jnp.einsum(
        "str,to->sro", other_stack, d_conv_low, preferred_element_type=jnp.float32
    )
    bits = [2] * dp_bits

    def by_tap(own, other):
        return jnp.where(my_index == 0, jnp.stack([own, other]), jnp.stack([other, own]))

    def conv_part(begin, end, order):
        own = own_terms[begin:end]
        other = other_terms[begin:end]
        both = by_tap(own, other)
        rows = chan_width >> dp_bits
        both = both.reshape([2, end - begin] + bits + [rows, chan_width])
        return halve(jnp.moveaxis(both, 1, 1 + dp_bits), order, jnp.bfloat16)

    cut = own_slots * 2 // 5
    conv_weight_grad = jnp.concatenate(
        [
            conv_part(0, cut, first),
            conv_part(cut, 2 * cut, second),
            conv_part(2 * cut, own_slots, third),
        ]
    )

    def spread(total, order, kind):
        rows = total.shape[0] >> (dp_bits + 1)
        split = total.reshape(bits + [2, rows] + list(total.shape[1:]))
        return halve(jnp.moveaxis(split, dp_bits, 0), order, kind)

    d_w_out_mine = spread(d_w_out, first, jnp.bfloat16)
    d_w_in_mine = spread(d_w_in, second, jnp.bfloat16)
    owners = 2 << dp_bits
    small = [d_b_in, d_b_out, d_conv_bias, d_gain_one, d_bias_one, d_gain_two, d_bias_two]
    joined = jnp.concatenate([v.reshape(owners, -1) for v in small], axis=1)
    joined_mine = spread(joined, third, jnp.float32).reshape(-1)
    vectors = []
    start = 0
    for v in small:
        size = v.shape[0] // owners
        vectors.append(joined_mine[start : start + size])
        start += size
    return (
        block_output,
        input_grad,
        conv_weight_grad,
        vectors[2],
        vectors[3],
        vectors[4],
        d_w_in_mine,
        vectors[0],
        d_w_out_mine,
        vectors[1],
        vectors[5],
        vectors[6],
    )


TILE = 256
COLS = 512
PAD = KERNEL_TAPS // 2 * DILATION_STEP
MIB = 2**20
F32 = jnp.float32
BF16 = jnp.bfloat16
HBM = pl.BlockSpec(memory_space=pltpu.HBM)
ANY = pl.BlockSpec(memory_space=pl.ANY)
VMEM = pl.BlockSpec(memory_space=pltpu.VMEM)
SMEM = pl.BlockSpec(memory_space=pltpu.SMEM)


def dot_plain(left, right):
    return lax.dot_general(left, right, (((1,), (0,)), ((), ())), preferred_element_type=F32)


def gelu_and_slope(value):
    cdf = 0.5 + 0.5 * lax.erf(value * 0.7071067811865476)
    density = 0.3989422804014327 * jnp.exp(value * value * -0.5)
    return value * cdf, cdf + value * density


def norm_parts(value):
    center = value - jnp.mean(value, axis=-1, keepdims=True)
    spread = jnp.mean(center * center, axis=-1, keepdims=True)
    scale = lax.rsqrt(spread + 1e-05)
    return center * scale, scale


def norm_back(grad, unit):
    return grad - jnp.mean(grad, axis=-1, keepdims=True) - unit * jnp.mean(
        grad * unit, axis=-1, keepdims=True
    )


def fold_rows(value):
    return jnp.sum(value.reshape(value.shape[0] // 8, 8, value.shape[1]), axis=0)


def one_row(value):
    return jnp.sum(value, axis=0, keepdims=True)


def my_bits(dp_bits):
    place = lax.axis_index("dp")
    mine = {bit: (place >> bit) & 1 for bit in range(dp_bits)}
    mine["t"] = lax.axis_index("tap")
    return mine


def relative(order, owner, mine):
    spot = 0
    for label in order:
        spot = spot * 2 + (owner[label] ^ mine[label])
    return spot


def rows_at(start, size):
    return pl.ds(pl.multiple_of(start, 16), size)


def clear_pads(pad_ref):
    zeros = jnp.zeros((PAD, pad_ref.shape[2]), pad_ref.dtype)
    for win in range(pad_ref.shape[0]):
        pad_ref[win, 0:PAD, :] = zeros
        pad_ref[win, PAD + WINDOW_LENGTH :, :] = zeros


def row_tiles(rows):
    for at in range(0, rows, TILE):
        yield slice(at, at + TILE), at // WINDOW_LENGTH, at % WINDOW_LENGTH


def window_weight(species, counts, win, windows, lanes):
    kind = species[lax.axis_index("tap") * windows + win]
    count = jnp.full((8, lanes), counts[kind], jnp.int32).astype(F32)
    return (4.0 / count)[0:1, :]


def own_conv_kernel(table, x_rows, weight, x_pad, out):
    windows = x_pad.shape[0]
    base = lax.axis_index("tap") * windows * WINDOW_LENGTH
    clear_pads(x_pad)
    for win in range(windows):
        x_pad[win, PAD : PAD + WINDOW_LENGTH, :] = x_rows[
            rows_at(base + win * WINDOW_LENGTH, WINDOW_LENGTH), :
        ]
    for rows, win, begin in row_tiles(out.shape[0]):
        total = None
        for slot in range(weight.shape[0]):
            shifted = rows_at(table[slot] * DILATION_STEP + begin, TILE)
            term = dot_plain(x_pad[win, shifted, :], weight[slot])
            total = term if total is None else total + term
        out[rows, :] = total


def join_pieces(pieces, weight):
    rows = weight.shape[1] // 8
    place = lax.axis_index("dp")
    for turn, first, piece in pieces:
        at = ((place & 7) ^ turn) * rows + first
        weight[:, rows_at(at, piece.shape[1]), :] = piece[...]


def main_kernel(order, dp_bits, turns, *refs):
    table, species, counts = refs[:3]
    x_pad, part, grad_in, w_in, w_out = refs[3:8]
    conv_bias, gain_one, bias_one, b_in, b_out, gain_two, bias_two = refs[8:15]
    pieces = refs[15 : 15 + len(turns)]
    y_hbm, unit, slope, d_up, weight, keep, send, small = refs[15 + len(turns) : 23 + len(turns)]
    hidden, low, act, hid_slope, d_out, y_low, result, sem = refs[23 + len(turns) :]
    mine = my_bits(dp_bits)
    rows_dev, chan = hidden.shape
    hid_width = w_in.shape[1]
    windows = x_pad.shape[0]
    join_pieces([turn + (piece,) for turn, piece in zip(turns, pieces)], weight)
    for rows, win, begin in row_tiles(rows_dev):
        total = part[rows, :] + conv_bias[...]
        for slot in range(weight.shape[0]):
            shifted = rows_at(table[slot] * DILATION_STEP + begin, TILE)
            total = total + dot_plain(x_pad[win, shifted, :], weight[slot])
        value, steep = gelu_and_slope(total)
        normed, scale = norm_parts(value)
        unit[rows, :] = normed
        slope[rows, :] = scale * steep
        here = x_pad[win, PAD + begin : PAD + begin + TILE, :].astype(F32)
        summed = here + (normed * gain_one[...] + bias_one[...])
        hidden[rows, :] = summed
        low[rows, :] = summed.astype(BF16)
    for rows, win, begin in row_tiles(rows_dev):
        for at in range(0, hid_width, COLS):
            cols = slice(at, at + COLS)
            up = dot_plain(low[rows, :], w_in[:, cols]) + b_in[:, cols]
            value, steep = gelu_and_slope(up)
            act[rows, cols] = value.astype(BF16)
            hid_slope[rows, cols] = steep
    sum_b_out = 0.0
    sum_gain = 0.0
    sum_bias = 0.0
    for rows, win, begin in row_tiles(rows_dev):
        pre_out = dot_plain(act[rows, :], w_out[...]) + b_out[...]
        normed, scale = norm_parts(pre_out)
        result_rows = hidden[rows, :] + (normed * gain_two[...] + bias_two[...])
        y_low[rows, :] = result_rows.astype(BF16)
        grad_y = grad_in[rows, :].astype(F32) * window_weight(species, counts, win, windows, chan)
        sum_bias = sum_bias + fold_rows(grad_y)
        sum_gain = sum_gain + fold_rows(grad_y * normed)
        back = (norm_back(grad_y * gain_two[...], normed) * scale).astype(BF16)
        d_out[rows, :] = back
        sum_b_out = sum_b_out + fold_rows(back.astype(F32))
    y_copy = pltpu.make_async_copy(y_low, y_hbm, sem)
    y_copy.start()
    small[0:1, :] = one_row(sum_b_out)
    small[1:2, :] = one_row(sum_gain)
    small[2:3, :] = one_row(sum_bias)
    small[7:8, :] = jnp.zeros((1, chan), F32)
    sums_in = [0.0] * (hid_width // COLS)
    for rows, win, begin in row_tiles(rows_dev):
        for number, at in enumerate(range(0, hid_width, COLS)):
            cols = slice(at, at + COLS)
            d_act = contract_cols(d_out[rows, :], w_out[cols, :])
            back = (d_act * hid_slope[rows, cols]).astype(BF16)
            d_up[rows, cols] = back
            sums_in[number] = sums_in[number] + fold_rows(back.astype(F32))
    for number, total in enumerate(sums_in):
        small[3 + number : 4 + number, :] = one_row(total)
    core = mine[0]
    out_block = hid_width >> (dp_bits + 1)
    in_block = chan >> (dp_bits + 1)
    chunks = hid_width // COLS
    whole = out_block + chunks * in_block

    def hand_out(spot, first_row, block, shift):
        for start in range(0, result.shape[1], 4 * block):
            owner_at = (first_row + start) // block
            for tap in range(2):
                owner = {bit: (owner_at >> (bit + 1)) & 1 for bit in range(1, dp_bits)}
                owner["t"] = tap
                place = rows_at(relative(order, owner, mine) * whole + shift, block)
                inner = start + tap * block
                keep[place, :] = result[spot, rows_at(inner + core * 2 * block, block), :]
                other = rows_at(inner + (1 - core) * 2 * block, block)
                send[place, :] = result[spot, other, :].astype(BF16)

    for number, at in enumerate(range(0, hid_width, COLS)):
        result[number % 2] = contract_rows(act[:, at : at + COLS], d_out[...])
        hand_out(number % 2, at, out_block, 0)
    for number, at in enumerate(range(0, hid_width, COLS)):
        result[number % 2] = contract_rows(low[...], d_up[:, at : at + COLS])
        hand_out(number % 2, 0, in_block, out_block + number * in_block)
    y_copy.wait()


def back_kernel(
    species, counts, grad_in, w_in, d_up, unit, slope, gain_one, small_in, d_pad, d_hidden, small
):
    windows = d_pad.shape[0]
    chan = d_hidden.shape[1]
    sum_gain = 0.0
    sum_bias = 0.0
    sum_conv = 0.0
    clear_pads(d_pad)
    for rows, win, begin in row_tiles(d_hidden.shape[0]):
        grad = grad_in[rows, :].astype(F32) * window_weight(species, counts, win, windows, chan)
        grad = grad + contract_cols(d_up[rows, :], w_in[...])
        d_hidden[rows, :] = grad
        normed = unit[rows, :]
        sum_bias = sum_bias + fold_rows(grad)
        sum_gain = sum_gain + fold_rows(grad * normed)
        back = (norm_back(grad * gain_one[...], normed) * slope[rows, :]).astype(BF16)
        d_pad[win, PAD + begin : PAD + begin + TILE, :] = back
        sum_conv = sum_conv + fold_rows(back.astype(F32))
    small[0:8, :] = small_in[...]
    small[8:9, :] = one_row(sum_conv)
    small[9:10, :] = one_row(sum_gain)
    small[10:11, :] = one_row(sum_bias)
    small[11:16, :] = jnp.zeros((5, chan), F32)


def store_small(total, ref, first):
    count = total.shape[0]
    high = total.astype(BF16)
    ref[first : first + count, :] = high
    ref[first + count : first + 2 * count, :] = (total - high.astype(F32)).astype(BF16)


def load_small(ref, first, count):
    high = ref[first : first + count, :].astype(F32)
    return high + ref[first + count : first + 2 * count, :].astype(F32)


def terms_kernel(slots, order, dp_bits, with_small, own_table, other_table, x_pad, d_pad, *refs):
    if with_small:
        small, _, keep, send, result = refs
        store_small(small[...], send, keep.shape[0])
    else:
        _, keep, send, result = refs
    mine = my_bits(dp_bits)
    rows = x_pad.shape[2] >> dp_bits
    core = mine[0]
    turn = 0
    for near_tap, table in enumerate((own_table, other_table)):
        for number, slot in enumerate(slots):
            spot = turn % 2
            turn += 1
            total = None
            for win in range(x_pad.shape[0]):
                shifted = rows_at((KERNEL_TAPS - 1 - table[slot]) * DILATION_STEP, WINDOW_LENGTH)
                term = contract_rows(
                    x_pad[win, PAD : PAD + WINDOW_LENGTH, :], d_pad[win, shifted, :]
                )
                total = term if total is None else total + term
            result[spot] = total
            for start in range(0, x_pad.shape[2], 2 * rows):
                owner_at = start // rows
                owner = {bit: (owner_at >> bit) & 1 for bit in range(1, dp_bits)}
                owner["t"] = mine["t"] ^ near_tap
                spread = relative(order, owner, mine)
                place = rows_at((spread * len(slots) + number) * rows, rows)
                keep[place, :] = result[spot, rows_at(start + core * rows, rows), :]
                other = rows_at(start + (1 - core) * rows, rows)
                send[place, :] = result[spot, other, :].astype(BF16)


def input_sum(table, d_pad, base, weight, rows, win, begin):
    total = base[rows, :]
    for slot in range(weight.shape[0]):
        shifted = rows_at((KERNEL_TAPS - 1 - table[slot]) * DILATION_STEP + begin, TILE)
        total = total + contract_cols(d_pad[win, shifted, :], weight[slot])
    return total


def input_near_kernel(table, d_pad, base, weight, _, out):
    for rows, win, begin in row_tiles(out.shape[0]):
        out[rows, :] = input_sum(table, d_pad, base, weight, rows, win, begin)


def input_far_kernel(table, d_pad, base, weight, _, out_hbm, out, sems):
    copies = []
    for rows, win, begin in row_tiles(out.shape[0]):
        out[rows, :] = input_sum(table, d_pad, base, weight, rows, win, begin)
        copies.append(
            pltpu.make_async_copy(out.at[rows, :], out_hbm.at[rows, :], sems.at[len(copies)])
        )
        copies[-1].start()
    for copy in copies:
        copy.wait()


def add_kernel(members, sends, with_small, *refs):
    gots = refs[:members]
    keep = refs[members]
    small = refs[members + 1] if with_small else None
    outs = refs[members + 2 + with_small :]
    next_keep = outs[0]
    rows = next_keep.shape[0]
    for block in range(sends, -1, -1):
        part = slice(block * rows, (block + 1) * rows)
        total = keep[part, :]
        for got in gots:
            total = total + got[part, :].astype(F32)
        if block == 0:
            next_keep[...] = total
        else:
            outs[block][0:rows, :] = total.astype(BF16)
    if with_small:
        total = small[...]
        for got in gots:
            total = total + load_small(got, keep.shape[0], small.shape[0])
        outs[sends + 1][...] = total
        for block in range(sends):
            store_small(total, outs[1 + block], rows)


def params(mib):
    return pltpu.CompilerParams(vmem_limit_bytes=mib * MIB)


def cost(flops, moved):
    return pl.CostEstimate(flops=flops, bytes_accessed=moved, transcendentals=0)


def near(value):
    return pltpu.with_memory_space_constraint(value, pltpu.VMEM)


def add_up(gots, keep, sends, token, small=None):
    lanes = keep.shape[1]
    rows = keep.shape[0] // (sends + 1)
    extra = 0 if small is None else 2 * small.shape[0]
    outs = [pltpu.VMEM((rows, lanes), F32)]
    outs += [pltpu.VMEM((rows + extra, lanes), BF16) for _ in range(sends)]
    operands = [near(got) for got in gots] + [near(keep)]
    if small is not None:
        outs.append(pltpu.VMEM(small.shape, F32))
        operands.append(near(small))
    return pl.pallas_call(
        functools.partial(add_kernel, len(gots), sends, small is not None),
        out_shape=outs,
        in_specs=[VMEM] * len(operands) + [ANY],
        out_specs=[VMEM] * len(outs),
        compiler_params=params(4),
        cost_estimate=cost(1, 1),
        name="add_up",
    )(*operands, token)


def swap(value, mask):
    count = lax.axis_size("dp") * lax.axis_size("tap")
    return lax.ppermute(value, ("dp", "tap"), [(i, i ^ mask) for i in range(count)])


def masks_of(group):
    bits = [1 if label == "t" else 2 << label for label in group]
    out = []
    for place in range(1, 1 << len(group)):
        mask = 0
        for at, bit in enumerate(reversed(bits)):
            mask |= bit if (place >> at) & 1 else 0
        out.append(mask)
    return out


def fetch_pieces(conv_weight, part):
    rows = conv_weight.shape[1] // 8
    place = lax.axis_index("dp") & 7
    first = swap_tap(lax.dynamic_slice_in_dim(conv_weight, place * rows, rows, 1))
    over_one = swap_dp(first, 1)
    over_two = swap_dp(first, 2)
    half = rows // 2
    last_low = swap_dp(over_two[:, :half], 1)
    last_high = swap_dp(over_one[:, half:], 2)
    chip = [
        ((0, 0), first),
        ((2, 0), over_one),
        ((4, 0), over_two),
        ((6, 0), last_low),
        ((6, half), last_high),
    ]
    mate = [((turn + 1, at), swap_dp(piece, 0)) for (turn, at), piece in chip]
    return chip + mate


def fast_shards(
    block_input,
    conv_weight,
    slot_tap_table,
    conv_bias,
    conv_norm_gain,
    conv_norm_bias,
    w_in,
    b_in,
    w_out,
    b_out,
    ffn_norm_gain,
    ffn_norm_bias,
    species_id,
    species_count,
    out_grad,
):
    tap_count = lax.axis_size("tap")
    dp_bits = (lax.axis_size("dp") - 1).bit_length()
    rows_dev = block_input.shape[0] // tap_count
    chan = block_input.shape[1]
    hid = w_in.shape[1]
    windows = rows_dev // WINDOW_LENGTH
    slots = conv_weight.shape[0]
    vmem = pltpu.VMEM
    plane = [1, "t"]
    line = list(range(dp_bits - 1, 1, -1))
    plane_masks = masks_of(plane)
    line_masks = masks_of(line)
    order_a = plane + line
    order_b = line + plane
    pad_shape = (windows, WINDOW_LENGTH + 2 * PAD, chan)
    rows_f = (rows_dev, chan)
    small_cost = cost(1, 1)

    def row(vector):
        return vector.reshape(1, -1)

    other_table = swap_tap(slot_tap_table)
    x_pad, part = pl.pallas_call(
        own_conv_kernel,
        out_shape=[vmem(pad_shape, BF16), vmem(rows_f, F32)],
        in_specs=[SMEM] + [VMEM] * 2,
        out_specs=[VMEM] * 2,
        compiler_params=params(8),
        cost_estimate=small_cost,
        name="own_conv",
    )(slot_tap_table, near(block_input), near(conv_weight))
    pieces = fetch_pieces(conv_weight, part)

    block_f = (hid + chan * hid // COLS) >> (dp_bits + 1)
    half_f = block_f << dp_bits
    main = pl.pallas_call(
        functools.partial(main_kernel, order_a, dp_bits, [turn for turn, _ in pieces]),
        out_shape=[
            pltpu.HBM(rows_f, BF16),
            vmem(rows_f, F32),
            vmem(rows_f, F32),
            vmem((rows_dev, hid), BF16),
            vmem(conv_weight.shape, BF16),
            vmem((half_f, chan), F32),
            vmem((half_f, chan), BF16),
            vmem((8, chan), F32),
        ],
        in_specs=[SMEM] * 3 + [VMEM] * (12 + len(pieces)),
        out_specs=[HBM] + [VMEM] * 7,
        scratch_shapes=[
            vmem(rows_f, F32),
            vmem(rows_f, BF16),
            vmem((rows_dev, hid), BF16),
            vmem((rows_dev, hid), F32),
            vmem(rows_f, BF16),
            vmem(rows_f, BF16),
            vmem((2, COLS, chan), F32),
            pltpu.SemaphoreType.DMA,
        ],
        compiler_params=params(32),
        cost_estimate=small_cost,
        name="main_rows",
    )(
        other_table,
        species_id,
        species_count,
        near(x_pad),
        near(part),
        near(out_grad),
        near(w_in),
        near(w_out),
        row(conv_bias),
        row(conv_norm_gain),
        row(conv_norm_bias),
        row(b_in),
        row(b_out),
        row(ffn_norm_gain),
        row(ffn_norm_bias),
        *[near(piece) for _, piece in pieces],
    )
    block_output, unit, slope, d_up, other_weight, keep_f, send_f, small_ffn = main
    got_f = swap_dp(send_f, 0)

    d_pad, d_hidden, small = pl.pallas_call(
        back_kernel,
        out_shape=[vmem(pad_shape, BF16), vmem(rows_f, F32), vmem((16, chan), F32)],
        in_specs=[SMEM] * 2 + [VMEM] * 7,
        out_specs=[VMEM] * 3,
        compiler_params=params(8),
        cost_estimate=small_cost,
        name="back_rows",
    )(
        species_id,
        species_count,
        near(out_grad),
        near(w_in),
        near(d_up),
        near(unit),
        near(slope),
        row(conv_norm_gain),
        near(small_ffn),
    )
    keep_f, *sends_f = add_up([got_f], keep_f, 3, small)
    gots_f = [swap(value, mask) for value, mask in zip(sends_f, plane_masks)]

    def terms(group, order, token, small, name):
        count = len(group) * chan
        extra = 0 if small is None else 2 * small.shape[0]
        operands = [near(x_pad), near(d_pad)] + ([] if small is None else [near(small)])
        return pl.pallas_call(
            functools.partial(terms_kernel, group, order, dp_bits, small is not None),
            out_shape=[vmem((count, chan), F32), vmem((count + extra, chan), BF16)],
            in_specs=[SMEM] * 2 + [VMEM] * len(operands) + [ANY],
            out_specs=[VMEM] * 2,
            scratch_shapes=[vmem((2, chan, chan), F32)],
            compiler_params=params(8),
            cost_estimate=small_cost,
            name=name,
        )(slot_tap_table, other_table, *operands, token)

    cut = (slots * 3 + 4) // 5
    keep_a, send_a = terms(range(0, cut), order_a, sends_f[0], None, "terms_a")
    got_a = swap_dp(send_a, 0)
    keep_b, send_b = terms(range(cut, slots), order_b, keep_a, small, "terms_b")
    got_b = swap_dp(send_b, 0)
    keep_a, *sends_a = add_up([got_a], keep_a, 3, keep_b)
    gots_a = [swap(value, mask) for value, mask in zip(sends_a, plane_masks)]
    keep_b, *sends_b = add_up([got_b], keep_b, len(line_masks), keep_a, small)
    small = sends_b.pop()
    gots_b = [swap(value, mask) for value, mask in zip(sends_b, line_masks)]

    partial = pl.pallas_call(
        input_near_kernel,
        out_shape=vmem(rows_f, F32),
        in_specs=[SMEM] + [VMEM] * 3 + [ANY],
        out_specs=VMEM,
        compiler_params=params(8),
        cost_estimate=small_cost,
        name="input_near",
    )(slot_tap_table, near(d_pad), near(d_hidden), near(conv_weight), keep_b)
    keep_f, *sends_f = add_up(gots_f, keep_f, len(line_masks), partial)
    gots_f = [swap(value, mask) for value, mask in zip(sends_f, line_masks)]
    input_grad = pl.pallas_call(
        input_far_kernel,
        out_shape=pltpu.HBM(rows_f, F32),
        in_specs=[SMEM] + [VMEM] * 3 + [ANY],
        out_specs=HBM,
        scratch_shapes=[vmem(rows_f, F32), pltpu.SemaphoreType.DMA((rows_dev // TILE,))],
        compiler_params=params(8),
        cost_estimate=small_cost,
        name="input_far",
    )(other_table, near(d_pad), near(partial), near(other_weight), keep_f)
    keep_a, *sends_a = add_up(gots_a, keep_a, len(line_masks), input_grad)
    gots_a = [swap(value, mask) for value, mask in zip(sends_a, line_masks)]
    keep_b, *sends_b = add_up(gots_b, keep_b, 3, keep_a, small)
    small = sends_b.pop()
    gots_b = [swap(value, mask) for value, mask in zip(sends_b, plane_masks)]
    (ffn_mine,) = add_up(gots_f, keep_f, 0, keep_b)
    w_out_rows = hid >> (dp_bits + 1)
    w_out_mine = ffn_mine[:w_out_rows]
    chunks = hid // COLS
    w_in_rows = chan >> (dp_bits + 1)
    w_in_mine = ffn_mine[w_out_rows:].reshape(chunks, w_in_rows, COLS)
    w_in_mine = w_in_mine.swapaxes(0, 1).reshape(w_in_rows, hid)
    (part_a,) = add_up(gots_a, keep_a, 0, ffn_mine)
    part_b, small = add_up(gots_b, keep_b, 0, part_a, small)

    conv_rows = chan >> dp_bits
    conv_weight_grad = jnp.concatenate(
        [v.reshape(-1, conv_rows, chan) for v in (part_a, part_b)]
    )
    owner = lax.axis_index("dp") * tap_count + lax.axis_index("tap")
    width = chan >> (dp_bits + 1)
    lanes = lax.dynamic_slice(small, (0, owner * width), (small.shape[0], width))
    wide = hid >> (dp_bits + 1)
    d_b_in = lax.dynamic_slice(small[3 : 3 + chunks].reshape(-1), (owner * wide,), (wide,))
    return (
        block_output,
        input_grad,
        conv_weight_grad,
        lanes[8],
        lanes[9],
        lanes[10],
        w_in_mine,
        d_b_in,
        w_out_mine,
        lanes[0],
        lanes[1],
        lanes[2],
    )


def narrow_enough(mesh):
    return mesh.shape["tap"] == 2 and mesh.shape["dp"] in (8, 16)


def solution(mesh):
    chosen = fast_shards if narrow_enough(mesh) else plain_shards
    return jax.shard_map(
        chosen,
        mesh=mesh,
        in_specs=(
            P("dp", None),
            P("tap", None, None),
            P("tap"),
            P(),
            P(),
            P(),
            P(),
            P(),
            P(),
            P(),
            P(),
            P(),
            P("dp"),
            P(),
            P(("dp", "tap"), None),
        ),
        out_specs=(
            P(("dp", "tap"), None),
            P(("dp", "tap"), None),
            P("tap", "dp", None),
            P(("dp", "tap")),
            P(("dp", "tap")),
            P(("dp", "tap")),
            P(("dp", "tap"), None),
            P(("dp", "tap")),
            P(("dp", "tap"), None),
            P(("dp", "tap")),
            P(("dp", "tap")),
            P(("dp", "tap")),
        ),
        check_vma=False,
    )
```

```python
import functools

import jax
import jax.numpy as jnp
from jax import lax
from jax.experimental import pallas as pl
from jax.experimental.pallas import tpu as pltpu
from jax.sharding import PartitionSpec as P

KERNEL_TAPS = 9
DILATION_STEP = 16
WINDOW_LENGTH = 512


def layer_norm(values):
    mean_val = jnp.mean(values, axis=-1, keepdims=True)
    center = values - mean_val
    spread = jnp.mean(center * center, axis=-1, keepdims=True)
    return center * lax.rsqrt(spread + 1e-05)


def exact_gelu(values):
    return jax.nn.gelu(values, approximate=False)


def conv_branch(pre_conv, gain_one, bias_one):
    return layer_norm(exact_gelu(pre_conv)) * gain_one + bias_one


def ffn_branch(pre_out, gain_two, bias_two):
    return layer_norm(pre_out) * gain_two + bias_two


def shift_stack(win_rows, tap_table, forward):
    tap_extent = KERNEL_TAPS // 2 * DILATION_STEP
    padded_input = jnp.pad(win_rows, ((0, 0), (tap_extent, tap_extent), (0, 0)))
    pieces = []
    for index_of_slot in range(tap_table.shape[0]):
        if forward:
            tap_offset = tap_table[index_of_slot]
        else:
            tap_offset = KERNEL_TAPS - 1 - tap_table[index_of_slot]
        shifted_input = lax.dynamic_slice_in_dim(
            padded_input, tap_offset * DILATION_STEP, WINDOW_LENGTH, 1
        )
        pieces.append(shifted_input.reshape(-1, win_rows.shape[2]))
    return jnp.stack(pieces)


def contract_rows(left, right):
    return lax.dot_general(
        left, right, (((0,), (0,)), ((), ())), preferred_element_type=jnp.float32
    )


def contract_cols(left, right):
    return lax.dot_general(
        left, right, (((1,), (1,)), ((), ())), preferred_element_type=jnp.float32
    )


def swap_dp(value, bit):
    count = lax.axis_size("dp")
    return lax.ppermute(value, "dp", [(i, i ^ (1 << bit)) for i in range(count)])


def swap_tap(value):
    return lax.ppermute(value, "tap", [(0, 1), (1, 0)])


def halve(part, order, kind):
    dp_bits = (lax.axis_size("dp") - 1).bit_length()
    place = lax.axis_index("dp")
    tap = lax.axis_index("tap")
    labels = ["t"] + list(range(dp_bits - 1, -1, -1))
    for step in order:
        axis = labels.index(step)
        labels.pop(axis)
        mine = tap if step == "t" else (place >> step) & 1
        keep = lax.dynamic_index_in_dim(part, mine, axis, keepdims=False)
        send = lax.dynamic_index_in_dim(part, 1 - mine, axis, keepdims=False).astype(kind)
        got = swap_tap(send) if step == "t" else swap_dp(send, step)
        part = keep + got.astype(jnp.float32)
    return part


def orders(dp_bits):
    rest = list(range(2, dp_bits))
    first = [0, "t", 1] + rest
    second = [0, 1] + rest[:1] + ["t"] + rest[1:]
    third = [0] + rest[:1] + ["t", 1] + rest[1:]
    return first, second, third


def plain_shards(
    block_input,
    conv_weight,
    slot_tap_table,
    conv_bias,
    conv_norm_gain,
    conv_norm_bias,
    w_in,
    b_in,
    w_out,
    b_out,
    ffn_norm_gain,
    ffn_norm_bias,
    species_id,
    species_count,
    out_grad,
):
    tap_count = lax.axis_size("tap")
    my_index = lax.axis_index("tap")
    core = lax.axis_index("dp") & 1
    dp_bits = (lax.axis_size("dp") - 1).bit_length()
    tok_dev, chan_width = block_input.shape
    hid_width = w_in.shape[1]
    half_rows = tok_dev // tap_count
    windows = tok_dev // WINDOW_LENGTH
    my_windows = windows // tap_count
    own_slots = conv_weight.shape[0]
    half_chan = chan_width // 2
    first, second, third = orders(dp_bits)

    other_table = swap_tap(slot_tap_table)
    part_send = lax.dynamic_slice_in_dim(conv_weight, core * half_chan, half_chan, 1)
    part_here = swap_tap(part_send)
    part_mate = swap_dp(part_here, 0)
    low_part = jnp.where(core == 0, part_here, part_mate)
    high_part = jnp.where(core == 0, part_mate, part_here)
    other_weight = jnp.concatenate([low_part, high_part], axis=1)

    my_x = lax.dynamic_slice_in_dim(block_input, my_index * half_rows, half_rows, 0)
    x_windows = my_x.reshape(my_windows, WINDOW_LENGTH, chan_width)
    mine_x = my_x.astype(jnp.float32)
    own_stack = shift_stack(x_windows, slot_tap_table, True)
    other_stack = shift_stack(x_windows, other_table, True)
    conv_out = jnp.einsum("str,sro->to", own_stack, conv_weight, preferred_element_type=jnp.float32)
    conv_out = conv_out + jnp.einsum(
        "str,sro->to", other_stack, other_weight, preferred_element_type=jnp.float32
    )
    pre_conv = conv_out + conv_bias
    norm_one, conv_back = jax.vjp(conv_branch, pre_conv, conv_norm_gain, conv_norm_bias)
    hidden = mine_x + norm_one
    hidden_low = hidden.astype(jnp.bfloat16)
    pre_up = jnp.dot(hidden_low, w_in, preferred_element_type=jnp.float32) + b_in
    activ, activ_back = jax.vjp(exact_gelu, pre_up)
    act_low = activ.astype(jnp.bfloat16)
    pre_out = jnp.dot(act_low, w_out, preferred_element_type=jnp.float32) + b_out
    norm_two, ffn_back = jax.vjp(ffn_branch, pre_out, ffn_norm_gain, ffn_norm_bias)
    block_output = (hidden + norm_two).astype(jnp.bfloat16)
    my_species = lax.dynamic_slice_in_dim(species_id, my_index * my_windows, my_windows, 0)
    species_range = jnp.arange(species_count.shape[0], dtype=jnp.int32)
    matches = my_species[:, None] == species_range[None, :]
    window_count = jnp.sum(jnp.where(matches, species_count[None, :], 0), axis=1)
    window_scale = 4.0 / window_count.astype(jnp.float32)
    grad_y = (
        out_grad.astype(jnp.float32).reshape(my_windows, WINDOW_LENGTH, chan_width)
        * window_scale[:, None, None]
    ).reshape(half_rows, chan_width)
    d_pre_out, d_gain_two, d_bias_two = ffn_back(grad_y)
    d_out_low = d_pre_out.astype(jnp.bfloat16)
    d_w_out = contract_rows(act_low, d_out_low)
    d_b_out = jnp.sum(d_out_low.astype(jnp.float32), axis=0)
    d_activ = contract_cols(d_out_low, w_out)
    (d_pre_up,) = activ_back(d_activ)
    d_up_low = d_pre_up.astype(jnp.bfloat16)
    d_w_in = contract_rows(hidden_low, d_up_low)
    d_b_in = jnp.sum(d_up_low.astype(jnp.float32), axis=0)
    d_hidden = grad_y + contract_cols(d_up_low, w_in)
    d_pre_conv, d_gain_one, d_bias_one = conv_back(d_hidden)
    d_conv_low = d_pre_conv.astype(jnp.bfloat16)
    d_conv_bias = jnp.sum(d_conv_low.astype(jnp.float32), axis=0)
    d_windows = d_conv_low.reshape(my_windows, WINDOW_LENGTH, chan_width)
    own_back = shift_stack(d_windows, slot_tap_table, False)
    other_back = shift_stack(d_windows, other_table, False)
    input_grad = (
        d_hidden
        + jnp.einsum("sto,sro->tr", own_back, conv_weight, preferred_element_type=jnp.float32)
        + jnp.einsum("sto,sro->tr", other_back, other_weight, preferred_element_type=jnp.float32)
    )
    own_terms = jnp.einsum("str,to->sro", own_stack, d_conv_low, preferred_element_type=jnp.float32)
    other_terms = jnp.einsum(
        "str,to->sro", other_stack, d_conv_low, preferred_element_type=jnp.float32
    )
    bits = [2] * dp_bits

    def by_tap(own, other):
        return jnp.where(my_index == 0, jnp.stack([own, other]), jnp.stack([other, own]))

    def conv_part(begin, end, order):
        own = own_terms[begin:end]
        other = other_terms[begin:end]
        both = by_tap(own, other)
        rows = chan_width >> dp_bits
        both = both.reshape([2, end - begin] + bits + [rows, chan_width])
        return halve(jnp.moveaxis(both, 1, 1 + dp_bits), order, jnp.bfloat16)

    cut = own_slots * 2 // 5
    conv_weight_grad = jnp.concatenate(
        [
            conv_part(0, cut, first),
            conv_part(cut, 2 * cut, second),
            conv_part(2 * cut, own_slots, third),
        ]
    )

    def spread(total, order, kind):
        rows = total.shape[0] >> (dp_bits + 1)
        split = total.reshape(bits + [2, rows] + list(total.shape[1:]))
        return halve(jnp.moveaxis(split, dp_bits, 0), order, kind)

    d_w_out_mine = spread(d_w_out, first, jnp.bfloat16)
    d_w_in_mine = spread(d_w_in, second, jnp.bfloat16)
    owners = 2 << dp_bits
    small = [d_b_in, d_b_out, d_conv_bias, d_gain_one, d_bias_one, d_gain_two, d_bias_two]
    joined = jnp.concatenate([v.reshape(owners, -1) for v in small], axis=1)
    joined_mine = spread(joined, third, jnp.float32).reshape(-1)
    vectors = []
    start = 0
    for v in small:
        size = v.shape[0] // owners
        vectors.append(joined_mine[start : start + size])
        start += size
    return (
        block_output,
        input_grad,
        conv_weight_grad,
        vectors[2],
        vectors[3],
        vectors[4],
        d_w_in_mine,
        vectors[0],
        d_w_out_mine,
        vectors[1],
        vectors[5],
        vectors[6],
    )


TILE = 256
COLS = 512
PAD = KERNEL_TAPS // 2 * DILATION_STEP
MIB = 2**20
F32 = jnp.float32
BF16 = jnp.bfloat16
HBM = pl.BlockSpec(memory_space=pltpu.HBM)
VMEM = pl.BlockSpec(memory_space=pltpu.VMEM)
SMEM = pl.BlockSpec(memory_space=pltpu.SMEM)


def dot_plain(left, right):
    return lax.dot_general(left, right, (((1,), (0,)), ((), ())), preferred_element_type=F32)


def gelu_and_slope(value):
    cdf = 0.5 + 0.5 * lax.erf(value * 0.7071067811865476)
    density = 0.3989422804014327 * jnp.exp(value * value * -0.5)
    return value * cdf, cdf + value * density


def norm_parts(value):
    center = value - jnp.mean(value, axis=-1, keepdims=True)
    spread = jnp.mean(center * center, axis=-1, keepdims=True)
    scale = lax.rsqrt(spread + 1e-05)
    return center * scale, scale


def norm_back(grad, unit):
    return grad - jnp.mean(grad, axis=-1, keepdims=True) - unit * jnp.mean(
        grad * unit, axis=-1, keepdims=True
    )


def fold_rows(value):
    return jnp.sum(value.reshape(value.shape[0] // 8, 8, value.shape[1]), axis=0)


def one_row(value):
    return jnp.sum(value, axis=0, keepdims=True)


def my_bits(dp_bits):
    place = lax.axis_index("dp")
    mine = {bit: (place >> bit) & 1 for bit in range(dp_bits)}
    mine["t"] = lax.axis_index("tap")
    return mine


def relative(order, owner, mine):
    spot = 0
    for label in order:
        spot = spot * 2 + (owner[label] ^ mine[label])
    return spot


def rows_at(start, size):
    return pl.ds(pl.multiple_of(start, 16), size)


def clear_pads(pad_ref):
    zeros = jnp.zeros((PAD, pad_ref.shape[2]), pad_ref.dtype)
    for win in range(pad_ref.shape[0]):
        pad_ref[win, 0:PAD, :] = zeros
        pad_ref[win, PAD + WINDOW_LENGTH :, :] = zeros


def row_tiles(rows):
    for at in range(0, rows, TILE):
        yield slice(at, at + TILE), at // WINDOW_LENGTH, at % WINDOW_LENGTH


def window_weight(species, counts, win, windows, lanes):
    kind = species[lax.axis_index("tap") * windows + win]
    count = jnp.full((8, lanes), counts[kind], jnp.int32).astype(F32)
    return (4.0 / count)[0:1, :]


def own_conv_kernel(table, x_hbm, weight_hbm, _, x_pad, part, token, weight, sems):
    windows = x_pad.shape[0]
    slots = weight.shape[0]
    base = lax.axis_index("tap") * windows * WINDOW_LENGTH
    copies = []
    for win in range(windows):
        source = x_hbm.at[rows_at(base + win * WINDOW_LENGTH, WINDOW_LENGTH), :]
        copies.append((source, x_pad.at[win, PAD : PAD + WINDOW_LENGTH, :]))
    copies += [(weight_hbm.at[slot], weight.at[slot]) for slot in range(slots)]
    copies = [
        pltpu.make_async_copy(source, target, sems.at[at])
        for at, (source, target) in enumerate(copies)
    ]
    for copy in copies:
        copy.start()
    clear_pads(x_pad)
    token[...] = jnp.zeros(token.shape, token.dtype)
    for copy in copies:
        copy.wait()
    for rows, win, begin in row_tiles(part.shape[0]):
        total = None
        for slot in range(slots):
            shifted = rows_at(table[slot] * DILATION_STEP + begin, TILE)
            term = dot_plain(x_pad[win, shifted, :], weight[slot])
            total = term if total is None else total + term
        part[rows, :] = total


def fetch_plan(rows):
    direct = rows // 8
    return direct, (rows - 2 * direct) // 8


def join_pieces(plan, pieces, weight):
    direct, shared = fetch_plan(weight.shape[1])
    place = lax.axis_index("dp")
    for (turn, first), piece in zip(plan, pieces):
        if first is None:
            at = ((place & 1) ^ turn) * direct
            first = 0
        else:
            at = 2 * direct + ((place & 7) ^ turn) * shared
        weight[first : first + piece.shape[0], rows_at(at, piece.shape[1]), :] = piece[...]


def main_kernel(orders, dp_bits, turns, *refs):
    table, species, counts = refs[:3]
    x_pad, part, grad_hbm, w_in_hbm, w_out_hbm = refs[3:8]
    conv_bias, gain_one, bias_one, b_in, b_out, gain_two, bias_two = refs[8:15]
    pieces = refs[15 : 15 + len(turns)]
    y_hbm, unit, slope, d_up, weight, keep, send, small, grad_in, w_in = refs[
        15 + len(turns) : 25 + len(turns)
    ]
    w_out, hidden, low, act, hid_slope, d_out, y_low, result, sem, sems = refs[25 + len(turns) :]
    mine = my_bits(dp_bits)
    rows_dev, chan = hidden.shape
    hid_width = w_in.shape[1]
    windows = x_pad.shape[0]
    in_copy = pltpu.make_async_copy(w_in_hbm, w_in, sems.at[0])
    out_copy = pltpu.make_async_copy(w_out_hbm, w_out, sems.at[1])
    grad_copy = pltpu.make_async_copy(grad_hbm, grad_in, sems.at[2])
    for copy in (in_copy, out_copy, grad_copy):
        copy.start()
    join_pieces(turns, pieces, weight)
    for rows, win, begin in row_tiles(rows_dev):
        total = part[rows, :] + conv_bias[...]
        for slot in range(weight.shape[0]):
            shifted = rows_at(table[slot] * DILATION_STEP + begin, TILE)
            total = total + dot_plain(x_pad[win, shifted, :], weight[slot])
        value, steep = gelu_and_slope(total)
        normed, scale = norm_parts(value)
        unit[rows, :] = normed
        slope[rows, :] = scale * steep
        here = x_pad[win, PAD + begin : PAD + begin + TILE, :].astype(F32)
        summed = here + (normed * gain_one[...] + bias_one[...])
        hidden[rows, :] = summed
        low[rows, :] = summed.astype(BF16)
    in_copy.wait()
    for rows, win, begin in row_tiles(rows_dev):
        for at in range(0, hid_width, COLS):
            cols = slice(at, at + COLS)
            up = dot_plain(low[rows, :], w_in[:, cols]) + b_in[:, cols]
            value, steep = gelu_and_slope(up)
            act[rows, cols] = value.astype(BF16)
            hid_slope[rows, cols] = steep
    sum_b_out = 0.0
    sum_gain = 0.0
    sum_bias = 0.0
    out_copy.wait()
    grad_copy.wait()
    for rows, win, begin in row_tiles(rows_dev):
        pre_out = dot_plain(act[rows, :], w_out[...]) + b_out[...]
        normed, scale = norm_parts(pre_out)
        result_rows = hidden[rows, :] + (normed * gain_two[...] + bias_two[...])
        y_low[rows, :] = result_rows.astype(BF16)
        grad_y = grad_in[rows, :].astype(F32) * window_weight(species, counts, win, windows, chan)
        sum_bias = sum_bias + fold_rows(grad_y)
        sum_gain = sum_gain + fold_rows(grad_y * normed)
        back = (norm_back(grad_y * gain_two[...], normed) * scale).astype(BF16)
        d_out[rows, :] = back
        sum_b_out = sum_b_out + fold_rows(back.astype(F32))
    y_copy = pltpu.make_async_copy(y_low, y_hbm, sem)
    y_copy.start()
    small[0:1, :] = one_row(sum_b_out)
    small[1:2, :] = one_row(sum_gain)
    small[2:3, :] = one_row(sum_bias)
    small[7:8, :] = jnp.zeros((1, chan), F32)
    sums_in = [0.0] * (hid_width // COLS)
    for rows, win, begin in row_tiles(rows_dev):
        for number, at in enumerate(range(0, hid_width, COLS)):
            cols = slice(at, at + COLS)
            d_act = contract_cols(d_out[rows, :], w_out[cols, :])
            back = (d_act * hid_slope[rows, cols]).astype(BF16)
            d_up[rows, cols] = back
            sums_in[number] = sums_in[number] + fold_rows(back.astype(F32))
    for number, total in enumerate(sums_in):
        small[3 + number : 4 + number, :] = one_row(total)
    core = mine[0]
    out_block = hid_width >> (dp_bits + 1)
    in_block = chan >> (dp_bits + 1)
    chunks = hid_width // COLS
    half = (out_block + chunks * in_block) // 2

    def hand_out(spot, first_row, block, targets):
        for start in range(0, result.shape[1], 4 * block):
            owner_at = (first_row + start) // block
            for tap in range(2):
                owner = {bit: (owner_at >> (bit + 1)) & 1 for bit in range(1, dp_bits)}
                owner["t"] = tap
                inner = start + tap * block
                for part_at, source, size, shift in targets:
                    spread = relative(orders[part_at], owner, mine) + (part_at << dp_bits)
                    place = rows_at(spread * half + shift, size)
                    mine_at = rows_at(inner + source + core * 2 * block, size)
                    other_at = rows_at(inner + source + (1 - core) * 2 * block, size)
                    keep[place, :] = result[spot, mine_at, :]
                    send[place, :] = result[spot, other_at, :].astype(BF16)

    for number, at in enumerate(range(0, hid_width, COLS)):
        result[number % 2] = contract_rows(act[:, at : at + COLS], d_out[...])
        size = out_block // 2
        hand_out(number % 2, at, out_block, [(0, 0, size, 0), (1, size, size, 0)])
    for number, at in enumerate(range(0, hid_width, COLS)):
        result[number % 2] = contract_rows(low[...], d_up[:, at : at + COLS])
        part_at, step = divmod(number, chunks // 2)
        shift = out_block // 2 + step * in_block
        hand_out(number % 2, 0, in_block, [(part_at, 0, in_block, shift)])
    y_copy.wait()


def back_kernel(
    species, counts, grad_in, w_in, d_up, unit, slope, gain_one, small_in, d_pad, d_hidden, small
):
    windows = d_pad.shape[0]
    chan = d_hidden.shape[1]
    sum_gain = 0.0
    sum_bias = 0.0
    sum_conv = 0.0
    clear_pads(d_pad)
    for rows, win, begin in row_tiles(d_hidden.shape[0]):
        grad = grad_in[rows, :].astype(F32) * window_weight(species, counts, win, windows, chan)
        grad = grad + contract_cols(d_up[rows, :], w_in[...])
        d_hidden[rows, :] = grad
        normed = unit[rows, :]
        sum_bias = sum_bias + fold_rows(grad)
        sum_gain = sum_gain + fold_rows(grad * normed)
        back = (norm_back(grad * gain_one[...], normed) * slope[rows, :]).astype(BF16)
        d_pad[win, PAD + begin : PAD + begin + TILE, :] = back
        sum_conv = sum_conv + fold_rows(back.astype(F32))
    small[0:8, :] = small_in[...]
    small[8:9, :] = one_row(sum_conv)
    small[9:10, :] = one_row(sum_gain)
    small[10:11, :] = one_row(sum_bias)
    small[11:16, :] = jnp.zeros((5, chan), F32)


def store_small(total, ref, first):
    count = total.shape[0]
    high = total.astype(BF16)
    ref[first : first + count, :] = high
    ref[first + count : first + 2 * count, :] = (total - high.astype(F32)).astype(BF16)


def load_small(ref, first, count):
    high = ref[first : first + count, :].astype(F32)
    return high + ref[first + count : first + 2 * count, :].astype(F32)


def terms_kernel(slots, orders, dp_bits, with_small, own_table, other_table, x_pad, d_pad, *refs):
    if with_small:
        small, _, keep, send, result = refs
        store_small(small[...], send, keep.shape[0])
    else:
        weight_hbm, _, keep, send, weight, result, sem = refs
        weight_copy = pltpu.make_async_copy(weight_hbm, weight, sem)
        weight_copy.start()
    mine = my_bits(dp_bits)
    rows = x_pad.shape[2] >> dp_bits
    core = mine[0]
    turn = 0
    for near_tap, table in enumerate((own_table, other_table)):
        for number, slot in enumerate(slots):
            spot = turn % 2
            turn += 1
            total = None
            for win in range(x_pad.shape[0]):
                shifted = rows_at((KERNEL_TAPS - 1 - table[slot]) * DILATION_STEP, WINDOW_LENGTH)
                term = contract_rows(
                    x_pad[win, PAD : PAD + WINDOW_LENGTH, :], d_pad[win, shifted, :]
                )
                total = term if total is None else total + term
            result[spot] = total
            for start in range(0, x_pad.shape[2], 2 * rows):
                owner_at = start // rows
                owner = {bit: (owner_at >> bit) & 1 for bit in range(1, dp_bits)}
                owner["t"] = mine["t"] ^ near_tap
                size = rows // 2
                for part_at in range(2):
                    spread = relative(orders[part_at], owner, mine) + (part_at << dp_bits)
                    place = rows_at((spread * len(slots) + number) * size, size)
                    mine_at = rows_at(start + core * rows + part_at * size, size)
                    other_at = rows_at(start + (1 - core) * rows + part_at * size, size)
                    keep[place, :] = result[spot, mine_at, :]
                    send[place, :] = result[spot, other_at, :].astype(BF16)
    if not with_small:
        weight_copy.wait()


def input_sum(table, d_pad, base, weight, rows, win, begin):
    total = base[rows, :]
    for slot in range(weight.shape[0]):
        shifted = rows_at((KERNEL_TAPS - 1 - table[slot]) * DILATION_STEP + begin, TILE)
        total = total + contract_cols(d_pad[win, shifted, :], weight[slot])
    return total


def input_near_kernel(table, d_pad, base, weight, _, out):
    for rows, win, begin in row_tiles(out.shape[0]):
        out[rows, :] = input_sum(table, d_pad, base, weight, rows, win, begin)


def input_far_kernel(table, d_pad, base, weight, _, out_hbm, token, out, sems):
    copies = []
    token[...] = jnp.zeros(token.shape, token.dtype)
    for rows, win, begin in row_tiles(out.shape[0]):
        out[rows, :] = input_sum(table, d_pad, base, weight, rows, win, begin)
        copies.append(
            pltpu.make_async_copy(out.at[rows, :], out_hbm.at[rows, :], sems.at[len(copies)])
        )
        copies[-1].start()
    for copy in copies:
        copy.wait()


def step_kernel(joined_in, joined_out, with_small, *refs):
    gots = refs[: 2 - joined_in]
    keep = refs[2 - joined_in]
    outs = refs[4 - joined_in + with_small :]
    rows = keep.shape[0] // 2
    half = rows // 2
    for part in range(2):
        got = gots[0 if joined_in else part]
        base = part * rows if joined_in else 0
        start = part * rows
        sent = keep[start + half : start + rows, :] + got[base + half : base + rows, :].astype(F32)
        if joined_out:
            outs[1][part * half : (part + 1) * half, :] = sent.astype(BF16)
        else:
            outs[1 + part][0:half, :] = sent.astype(BF16)
        kept = keep[start : start + half, :] + got[base : base + half, :].astype(F32)
        outs[0][part * half : (part + 1) * half, :] = kept
    if with_small:
        small = refs[3 - joined_in]
        total = small[...] + load_small(gots[0], rows * (1 + joined_in), small.shape[0])
        outs[3 - joined_out][...] = total
        store_small(total, outs[1], half * (1 + joined_out))


def sum_of(gots, keep, rows):
    total = keep[rows, :]
    for got in gots:
        total = total + got[rows, :].astype(F32)
    return total


def last_ffn_kernel(members, *refs):
    gots = refs[:members]
    keep, _, w_in_out, w_out_out = refs[members:]
    out_rows, chan = w_out_out.shape
    in_rows = w_in_out.shape[0]
    half = keep.shape[0] // 2
    steps = w_in_out.shape[1] // chan // 2
    for part in range(2):
        base = part * half
        size = out_rows // 2
        w_out_out[part * size : (part + 1) * size, :] = sum_of(gots, keep, slice(base, base + size))
        for step in range(steps):
            at = base + size + step * in_rows
            cols = slice((part * steps + step) * chan, (part * steps + step + 1) * chan)
            w_in_out[:, cols] = sum_of(gots, keep, slice(at, at + in_rows))


def last_small_kernel(members, *refs):
    gots = refs[:members]
    keep, small, _, out, next_small = refs[members:]
    rows = out.shape[0]
    out[...] = sum_of(gots, keep, slice(0, rows))
    total = small[...]
    for got in gots:
        total = total + load_small(got, rows, small.shape[0])
    next_small[...] = total


def last_conv_kernel(members, *refs):
    gots = refs[:members]
    keep, done, out = refs[members:]
    size = out.shape[1] // 2
    first = done.shape[0] // out.shape[1]
    rest = out.shape[0] - first
    for slot in range(out.shape[0]):
        for part in range(2):
            place = slice(part * size, (part + 1) * size)
            if slot < first:
                at = (part * first + slot) * size
                out[slot, place, :] = done[at : at + size, :]
            else:
                at = (part * rest + slot - first) * size
                out[slot, place, :] = sum_of(gots, keep, slice(at, at + size))


def params(mib):
    return pltpu.CompilerParams(vmem_limit_bytes=mib * MIB)


def claim(micros):
    return pl.CostEstimate(flops=int(micros * 1.1e9), bytes_accessed=1, transcendentals=0)


def after_kernel(_, token, out):
    del token, out


def after(value, token, claimed=0):
    return pl.pallas_call(
        after_kernel,
        out_shape=pltpu.VMEM(value.shape, value.dtype),
        in_specs=[VMEM] * 2,
        out_specs=VMEM,
        input_output_aliases={0: 0},
        compiler_params=params(4),
        cost_estimate=claim(claimed),
        name="after",
    )(near(value), near(token))


def far(value):
    return pltpu.with_memory_space_constraint(value, pltpu.HBM)


def near(value):
    return pltpu.with_memory_space_constraint(value, pltpu.VMEM)


def step(gots, keep, joined_out, token, small=None):
    lanes = keep.shape[1]
    half = keep.shape[0] // 4
    extra = 0 if small is None else 2 * small.shape[0]
    sent = [2 * half + extra] if joined_out else [half + extra, half]
    outs = [pltpu.VMEM((2 * half, lanes), F32)]
    outs += [pltpu.VMEM((rows, lanes), BF16) for rows in sent]
    operands = [near(got) for got in gots] + [near(keep)]
    if small is not None:
        outs.append(pltpu.VMEM(small.shape, F32))
        operands.append(near(small))
    out = pl.pallas_call(
        functools.partial(step_kernel, len(gots) == 1, joined_out, small is not None),
        out_shape=outs,
        in_specs=[VMEM] * (len(operands) + 1),
        out_specs=[VMEM] * len(outs),
        compiler_params=params(4),
        cost_estimate=claim(0),
        name="step",
    )(*operands, near(token))
    if small is None:
        return out[0], out[1:], None
    return out[0], out[1:-1], out[-1]


def swap(value, mask):
    count = lax.axis_size("dp") * lax.axis_size("tap")
    return lax.ppermute(value, ("dp", "tap"), [(i, i ^ mask) for i in range(count)])


def cut_kernel(weight_hbm, _, shared, direct, sems):
    rows = direct.shape[1]
    place = lax.axis_index("dp")
    start = 2 * rows + (place & 7) * shared.shape[1]
    copies = [
        pltpu.make_async_copy(
            weight_hbm.at[:, rows_at(start, shared.shape[1]), :], shared, sems.at[0]
        ),
        pltpu.make_async_copy(
            weight_hbm.at[:, rows_at((place & 1) * rows, rows), :], direct, sems.at[1]
        ),
    ]
    for copy in copies:
        copy.start()
    for copy in copies:
        copy.wait()


def cut_pieces(conv_weight, other_table):
    slots, chan, width = conv_weight.shape
    direct, shared = fetch_plan(chan)
    return pl.pallas_call(
        cut_kernel,
        out_shape=[pltpu.VMEM((slots, rows, width), BF16) for rows in (shared, direct)],
        in_specs=[HBM, VMEM],
        out_specs=[VMEM] * 2,
        scratch_shapes=[pltpu.SemaphoreType.DMA((2,))],
        compiler_params=params(4),
        cost_estimate=claim(0),
        name="cut_pieces",
    )(far(conv_weight), near(other_table))


def pick_kernel(over_one, over_two, _, low, high):
    low[...] = over_two[0 : low.shape[0]]
    high[...] = over_one[low.shape[0] :]


def fetch_pieces(first, direct, token):
    over_one = swap_dp(first, 1)
    over_two = swap_dp(first, 2)
    straight = swap_tap(after(direct, first))
    slots = first.shape[0]
    cut = (slots + 1) // 2
    low, high = pl.pallas_call(
        pick_kernel,
        out_shape=[pltpu.VMEM((count,) + first.shape[1:], BF16) for count in (cut, slots - cut)],
        in_specs=[VMEM] * 3,
        out_specs=[VMEM] * 2,
        compiler_params=params(4),
        cost_estimate=claim(0),
        name="pick",
    )(near(over_one), near(over_two), near(token))
    last_low = swap_dp(low, 1)
    last_high = swap_dp(high, 2)
    straight = after(straight, low)
    chip = [
        ((0, 0), first),
        ((2, 0), over_one),
        ((4, 0), over_two),
        ((0, None), straight),
        ((6, 0), last_low),
        ((6, cut), last_high),
    ]
    mate = [((turn + 1, at), swap_dp(piece, 0)) for (turn, at), piece in chip]
    return chip + mate


def fast_shards(
    block_input,
    conv_weight,
    slot_tap_table,
    conv_bias,
    conv_norm_gain,
    conv_norm_bias,
    w_in,
    b_in,
    w_out,
    b_out,
    ffn_norm_gain,
    ffn_norm_bias,
    species_id,
    species_count,
    out_grad,
):
    tap_count = lax.axis_size("tap")
    dp_bits = (lax.axis_size("dp") - 1).bit_length()
    rows_dev = block_input.shape[0] // tap_count
    chan = block_input.shape[1]
    hid = w_in.shape[1]
    windows = rows_dev // WINDOW_LENGTH
    slots = conv_weight.shape[0]
    vmem = pltpu.VMEM
    line = list(range(2, dp_bits))
    orders = (["t", 1] + line, [1, "t"] + line)
    over_x, over_y = 1, 4
    pad_shape = (windows, WINDOW_LENGTH + 2 * PAD, chan)
    rows_f = (rows_dev, chan)
    small_cost = claim(0)

    def row(vector):
        return vector.reshape(1, -1)

    other_table = swap_tap(slot_tap_table)
    shared, direct = cut_pieces(conv_weight, other_table)
    weight_shape = conv_weight.shape
    tiles = rows_dev // TILE
    dma = pltpu.SemaphoreType.DMA
    first = swap_tap(shared)
    x_pad, part, token = pl.pallas_call(
        own_conv_kernel,
        out_shape=[vmem(pad_shape, BF16), vmem(rows_f, F32), vmem((8, 128), F32)],
        in_specs=[SMEM] + [HBM] * 2 + [VMEM],
        out_specs=[VMEM] * 3,
        scratch_shapes=[vmem(weight_shape, BF16), dma((windows + slots,))],
        compiler_params=params(8),
        cost_estimate=claim(0),
        name="own_conv",
    )(slot_tap_table, far(block_input), far(conv_weight), near(first))
    pieces = fetch_pieces(first, direct, token)

    block_f = (hid + chan * hid // COLS) >> (dp_bits + 1)
    half_f = block_f << dp_bits
    main = pl.pallas_call(
        functools.partial(main_kernel, orders, dp_bits, [turn for turn, _ in pieces]),
        out_shape=[
            pltpu.HBM(rows_f, BF16),
            vmem(rows_f, F32),
            vmem(rows_f, F32),
            vmem((rows_dev, hid), BF16),
            vmem(conv_weight.shape, BF16),
            vmem((half_f, chan), F32),
            vmem((half_f, chan), BF16),
            vmem((8, chan), F32),
            vmem(rows_f, BF16),
            vmem(w_in.shape, BF16),
        ],
        in_specs=[SMEM] * 3 + [VMEM] * 2 + [HBM] * 3 + [VMEM] * (7 + len(pieces)),
        out_specs=[HBM] + [VMEM] * 9,
        scratch_shapes=[
            vmem(w_out.shape, BF16),
            vmem(rows_f, F32),
            vmem(rows_f, BF16),
            vmem((rows_dev, hid), BF16),
            vmem((rows_dev, hid), F32),
            vmem(rows_f, BF16),
            vmem(rows_f, BF16),
            vmem((2, COLS, chan), F32),
            dma,
            dma((3,)),
        ],
        compiler_params=params(34),
        cost_estimate=small_cost,
        name="main_rows",
    )(
        other_table,
        species_id,
        species_count,
        near(x_pad),
        near(part),
        far(out_grad),
        far(w_in),
        far(w_out),
        row(conv_bias),
        row(conv_norm_gain),
        row(conv_norm_bias),
        row(b_in),
        row(b_out),
        row(ffn_norm_gain),
        row(ffn_norm_bias),
        *[near(piece) for _, piece in pieces],
    )
    block_output, unit, slope, d_up, other_weight, keep_f, send_f, small_ffn, grad_in, w_in_near = main
    got_f = swap_dp(send_f, 0)

    d_pad, d_hidden, small = pl.pallas_call(
        back_kernel,
        out_shape=[vmem(pad_shape, BF16), vmem(rows_f, F32), vmem((16, chan), F32)],
        in_specs=[SMEM] * 2 + [VMEM] * 7,
        out_specs=[VMEM] * 3,
        compiler_params=params(8),
        cost_estimate=small_cost,
        name="back_rows",
    )(
        species_id,
        species_count,
        near(grad_in),
        near(w_in_near),
        near(d_up),
        near(unit),
        near(slope),
        row(conv_norm_gain),
        near(small_ffn),
    )
    keep_f, sends_f, _ = step([got_f], keep_f, False, small)
    gots_f = [swap(sends_f[0], over_x), swap(sends_f[1], over_y)]

    def terms(group, token, small, name):
        count = len(group) * chan
        extra = 0 if small is None else 2 * small.shape[0]
        outs = [vmem((count, chan), F32), vmem((count + extra, chan), BF16)]
        scratch = [vmem((2, chan, chan), F32)]
        if small is None:
            last, last_spec = far(conv_weight), HBM
            outs.append(vmem(weight_shape, BF16))
            scratch.append(dma)
        else:
            last, last_spec = near(small), VMEM
        return pl.pallas_call(
            functools.partial(terms_kernel, group, orders, dp_bits, small is not None),
            out_shape=outs,
            in_specs=[SMEM] * 2 + [VMEM] * 2 + [last_spec, VMEM],
            out_specs=[VMEM] * len(outs),
            scratch_shapes=scratch,
            compiler_params=params(8),
            cost_estimate=small_cost,
            name=name,
        )(slot_tap_table, other_table, near(x_pad), near(d_pad), last, near(token))

    cut = (slots * 3 + 4) // 5
    keep_a, send_a = terms(range(0, cut), sends_f[0], small, "terms_a")
    got_a = swap_dp(send_a, 0)
    keep_b, send_b, own_weight = terms(range(cut, slots), keep_a, None, "terms_b")
    got_b = swap_dp(send_b, 0)
    def spaced(token, claimed=1):
        return after(mark, token, claimed)

    def turned(sends):
        return [swap(sends[0], over_y), swap(sends[1], over_x)]

    def along(sends, stage):
        return [swap(sends[0], 2 << line[stage])]

    mark = token
    keep_f, sends_f, _ = step(gots_f, keep_f, False, keep_b)
    gots_f = turned(sends_f)
    keep_a, sends_a, small = step([got_a], keep_a, False, spaced(keep_f, 100), small)
    gots_a = [swap(sends_a[0], over_x), swap(sends_a[1], over_y)]
    partial = pl.pallas_call(
        input_near_kernel,
        out_shape=vmem(rows_f, F32),
        in_specs=[SMEM] + [VMEM] * 4,
        out_specs=VMEM,
        compiler_params=params(8),
        cost_estimate=claim(0),
        name="input_near",
    )(slot_tap_table, near(d_pad), near(d_hidden), near(own_weight), near(keep_a))
    input_grad, mark = pl.pallas_call(
        input_far_kernel,
        out_shape=[pltpu.HBM(rows_f, F32), vmem((8, 128), F32)],
        in_specs=[SMEM] + [VMEM] * 4,
        out_specs=[HBM, VMEM],
        scratch_shapes=[vmem(rows_f, F32), pltpu.SemaphoreType.DMA((rows_dev // TILE,))],
        compiler_params=params(8),
        cost_estimate=small_cost,
        name="input_far",
    )(other_table, near(d_pad), near(partial), near(other_weight), near(keep_a))
    mark = spaced(mark)
    keep_f, sends_f, _ = step(gots_f, keep_f, True, mark)
    got_f = along(sends_f, 0)
    keep_b, sends_b, _ = step([got_b], keep_b, False, keep_f)
    gots_b = [swap(sends_b[0], over_x), swap(sends_b[1], over_y)]
    mark = spaced(keep_b)
    keep_a, sends_a, small = step(gots_a, keep_a, False, mark, small)
    gots_a = turned(sends_a)
    mark = spaced(keep_a)
    for stage in range(1, len(line)):
        keep_f, sends_f, _ = step(got_f, keep_f, True, mark)
        got_f = along(sends_f, stage)
        mark = spaced(keep_f)
    keep_b, sends_b, _ = step(gots_b, keep_b, False, mark)
    gots_b = turned(sends_b)
    mark = spaced(keep_b)
    keep_a, sends_a, small = step(gots_a, keep_a, True, mark, small)
    got_a = along(sends_a, 0)
    mark = spaced(keep_a)
    w_in_mine, w_out_mine = pl.pallas_call(
        functools.partial(last_ffn_kernel, 1),
        out_shape=[
            jax.ShapeDtypeStruct((chan >> (dp_bits + 1), hid), F32),
            jax.ShapeDtypeStruct((hid >> (dp_bits + 1), chan), F32),
        ],
        in_specs=[VMEM] * 3,
        out_specs=[VMEM] * 2,
        compiler_params=params(4),
        cost_estimate=claim(0),
        name="last_ffn",
    )(near(got_f[0]), near(keep_f), near(mark))
    keep_b, sends_b, _ = step(gots_b, keep_b, True, mark)
    got_b = along(sends_b, 0)
    mark = spaced(keep_b)
    for stage in range(1, len(line)):
        keep_a, sends_a, small = step(got_a, keep_a, True, mark, small)
        got_a = along(sends_a, stage)
        mark = spaced(keep_a)
        keep_b, sends_b, _ = step(got_b, keep_b, True, mark)
        got_b = along(sends_b, stage)
        mark = spaced(keep_b)
    part_a, small = pl.pallas_call(
        functools.partial(last_small_kernel, 1),
        out_shape=[vmem(keep_a.shape, F32), vmem(small.shape, F32)],
        in_specs=[VMEM] * 4,
        out_specs=[VMEM] * 2,
        compiler_params=params(4),
        cost_estimate=claim(0),
        name="last_a",
    )(near(got_a[0]), near(keep_a), near(small), near(mark))
    conv_weight_grad = pl.pallas_call(
        functools.partial(last_conv_kernel, 1),
        out_shape=jax.ShapeDtypeStruct((slots, chan >> dp_bits, chan), F32),
        in_specs=[VMEM] * 3,
        out_specs=VMEM,
        compiler_params=params(4),
        cost_estimate=claim(0),
        name="last_conv",
    )(near(got_b[0]), near(keep_b), near(part_a))
    chunks = hid // COLS

    owner = lax.axis_index("dp") * tap_count + lax.axis_index("tap")
    width = chan >> (dp_bits + 1)
    lanes = lax.dynamic_slice(small, (0, owner * width), (small.shape[0], width))
    wide = hid >> (dp_bits + 1)
    d_b_in = lax.dynamic_slice(small[3 : 3 + chunks].reshape(-1), (owner * wide,), (wide,))
    return (
        block_output,
        input_grad,
        conv_weight_grad,
        lanes[8],
        lanes[9],
        lanes[10],
        w_in_mine,
        d_b_in,
        w_out_mine,
        lanes[0],
        lanes[1],
        lanes[2],
    )


def narrow_enough(mesh):
    return mesh.shape["tap"] == 2 and mesh.shape["dp"] in (8, 16)


def solution(mesh):
    chosen = fast_shards if narrow_enough(mesh) else plain_shards
    return jax.shard_map(
        chosen,
        mesh=mesh,
        in_specs=(
            P("dp", None),
            P("tap", None, None),
            P("tap"),
            P(),
            P(),
            P(),
            P(),
            P(),
            P(),
            P(),
            P(),
            P(),
            P("dp"),
            P(),
            P(("dp", "tap"), None),
        ),
        out_specs=(
            P(("dp", "tap"), None),
            P(("dp", "tap"), None),
            P("tap", "dp", None),
            P(("dp", "tap")),
            P(("dp", "tap")),
            P(("dp", "tap")),
            P(("dp", "tap"), None),
            P(("dp", "tap")),
            P(("dp", "tap"), None),
            P(("dp", "tap")),
            P(("dp", "tap")),
            P(("dp", "tap")),
        ),
        check_vma=False,
    )
```

```python
import functools

import jax
import jax.numpy as jnp
from jax import lax
from jax.experimental import pallas as pl
from jax.experimental.pallas import tpu as pltpu
from jax.sharding import PartitionSpec as P

KERNEL_TAPS = 9
DILATION_STEP = 16
WINDOW_LENGTH = 512


def layer_norm(values):
    mean_val = jnp.mean(values, axis=-1, keepdims=True)
    center = values - mean_val
    spread = jnp.mean(center * center, axis=-1, keepdims=True)
    return center * lax.rsqrt(spread + 1e-05)


def exact_gelu(values):
    return jax.nn.gelu(values, approximate=False)


def conv_branch(pre_conv, gain_one, bias_one):
    return layer_norm(exact_gelu(pre_conv)) * gain_one + bias_one


def ffn_branch(pre_out, gain_two, bias_two):
    return layer_norm(pre_out) * gain_two + bias_two


def shift_stack(win_rows, tap_table, forward):
    tap_extent = KERNEL_TAPS // 2 * DILATION_STEP
    padded_input = jnp.pad(win_rows, ((0, 0), (tap_extent, tap_extent), (0, 0)))
    pieces = []
    for index_of_slot in range(tap_table.shape[0]):
        if forward:
            tap_offset = tap_table[index_of_slot]
        else:
            tap_offset = KERNEL_TAPS - 1 - tap_table[index_of_slot]
        shifted_input = lax.dynamic_slice_in_dim(
            padded_input, tap_offset * DILATION_STEP, WINDOW_LENGTH, 1
        )
        pieces.append(shifted_input.reshape(-1, win_rows.shape[2]))
    return jnp.stack(pieces)


def contract_rows(left, right):
    return lax.dot_general(
        left, right, (((0,), (0,)), ((), ())), preferred_element_type=jnp.float32
    )


def contract_cols(left, right):
    return lax.dot_general(
        left, right, (((1,), (1,)), ((), ())), preferred_element_type=jnp.float32
    )


def swap_dp(value, bit):
    count = lax.axis_size("dp")
    return lax.ppermute(value, "dp", [(i, i ^ (1 << bit)) for i in range(count)])


def swap_tap(value):
    return lax.ppermute(value, "tap", [(0, 1), (1, 0)])


def halve(part, order, kind):
    dp_bits = (lax.axis_size("dp") - 1).bit_length()
    place = lax.axis_index("dp")
    tap = lax.axis_index("tap")
    labels = ["t"] + list(range(dp_bits - 1, -1, -1))
    for step in order:
        axis = labels.index(step)
        labels.pop(axis)
        mine = tap if step == "t" else (place >> step) & 1
        keep = lax.dynamic_index_in_dim(part, mine, axis, keepdims=False)
        send = lax.dynamic_index_in_dim(part, 1 - mine, axis, keepdims=False).astype(kind)
        got = swap_tap(send) if step == "t" else swap_dp(send, step)
        part = keep + got.astype(jnp.float32)
    return part


def orders(dp_bits):
    rest = list(range(2, dp_bits))
    first = [0, "t", 1] + rest
    second = [0, 1] + rest[:1] + ["t"] + rest[1:]
    third = [0] + rest[:1] + ["t", 1] + rest[1:]
    return first, second, third


def plain_shards(
    block_input,
    conv_weight,
    slot_tap_table,
    conv_bias,
    conv_norm_gain,
    conv_norm_bias,
    w_in,
    b_in,
    w_out,
    b_out,
    ffn_norm_gain,
    ffn_norm_bias,
    species_id,
    species_count,
    out_grad,
):
    tap_count = lax.axis_size("tap")
    my_index = lax.axis_index("tap")
    core = lax.axis_index("dp") & 1
    dp_bits = (lax.axis_size("dp") - 1).bit_length()
    tok_dev, chan_width = block_input.shape
    hid_width = w_in.shape[1]
    half_rows = tok_dev // tap_count
    windows = tok_dev // WINDOW_LENGTH
    my_windows = windows // tap_count
    own_slots = conv_weight.shape[0]
    half_chan = chan_width // 2
    first, second, third = orders(dp_bits)

    other_table = swap_tap(slot_tap_table)
    part_send = lax.dynamic_slice_in_dim(conv_weight, core * half_chan, half_chan, 1)
    part_here = swap_tap(part_send)
    part_mate = swap_dp(part_here, 0)
    low_part = jnp.where(core == 0, part_here, part_mate)
    high_part = jnp.where(core == 0, part_mate, part_here)
    other_weight = jnp.concatenate([low_part, high_part], axis=1)

    my_x = lax.dynamic_slice_in_dim(block_input, my_index * half_rows, half_rows, 0)
    x_windows = my_x.reshape(my_windows, WINDOW_LENGTH, chan_width)
    mine_x = my_x.astype(jnp.float32)
    own_stack = shift_stack(x_windows, slot_tap_table, True)
    other_stack = shift_stack(x_windows, other_table, True)
    conv_out = jnp.einsum("str,sro->to", own_stack, conv_weight, preferred_element_type=jnp.float32)
    conv_out = conv_out + jnp.einsum(
        "str,sro->to", other_stack, other_weight, preferred_element_type=jnp.float32
    )
    pre_conv = conv_out + conv_bias
    norm_one, conv_back = jax.vjp(conv_branch, pre_conv, conv_norm_gain, conv_norm_bias)
    hidden = mine_x + norm_one
    hidden_low = hidden.astype(jnp.bfloat16)
    pre_up = jnp.dot(hidden_low, w_in, preferred_element_type=jnp.float32) + b_in
    activ, activ_back = jax.vjp(exact_gelu, pre_up)
    act_low = activ.astype(jnp.bfloat16)
    pre_out = jnp.dot(act_low, w_out, preferred_element_type=jnp.float32) + b_out
    norm_two, ffn_back = jax.vjp(ffn_branch, pre_out, ffn_norm_gain, ffn_norm_bias)
    block_output = (hidden + norm_two).astype(jnp.bfloat16)
    my_species = lax.dynamic_slice_in_dim(species_id, my_index * my_windows, my_windows, 0)
    species_range = jnp.arange(species_count.shape[0], dtype=jnp.int32)
    matches = my_species[:, None] == species_range[None, :]
    window_count = jnp.sum(jnp.where(matches, species_count[None, :], 0), axis=1)
    window_scale = 4.0 / window_count.astype(jnp.float32)
    grad_y = (
        out_grad.astype(jnp.float32).reshape(my_windows, WINDOW_LENGTH, chan_width)
        * window_scale[:, None, None]
    ).reshape(half_rows, chan_width)
    d_pre_out, d_gain_two, d_bias_two = ffn_back(grad_y)
    d_out_low = d_pre_out.astype(jnp.bfloat16)
    d_w_out = contract_rows(act_low, d_out_low)
    d_b_out = jnp.sum(d_out_low.astype(jnp.float32), axis=0)
    d_activ = contract_cols(d_out_low, w_out)
    (d_pre_up,) = activ_back(d_activ)
    d_up_low = d_pre_up.astype(jnp.bfloat16)
    d_w_in = contract_rows(hidden_low, d_up_low)
    d_b_in = jnp.sum(d_up_low.astype(jnp.float32), axis=0)
    d_hidden = grad_y + contract_cols(d_up_low, w_in)
    d_pre_conv, d_gain_one, d_bias_one = conv_back(d_hidden)
    d_conv_low = d_pre_conv.astype(jnp.bfloat16)
    d_conv_bias = jnp.sum(d_conv_low.astype(jnp.float32), axis=0)
    d_windows = d_conv_low.reshape(my_windows, WINDOW_LENGTH, chan_width)
    own_back = shift_stack(d_windows, slot_tap_table, False)
    other_back = shift_stack(d_windows, other_table, False)
    input_grad = (
        d_hidden
        + jnp.einsum("sto,sro->tr", own_back, conv_weight, preferred_element_type=jnp.float32)
        + jnp.einsum("sto,sro->tr", other_back, other_weight, preferred_element_type=jnp.float32)
    )
    own_terms = jnp.einsum("str,to->sro", own_stack, d_conv_low, preferred_element_type=jnp.float32)
    other_terms = jnp.einsum(
        "str,to->sro", other_stack, d_conv_low, preferred_element_type=jnp.float32
    )
    bits = [2] * dp_bits

    def by_tap(own, other):
        return jnp.where(my_index == 0, jnp.stack([own, other]), jnp.stack([other, own]))

    def conv_part(begin, end, order):
        own = own_terms[begin:end]
        other = other_terms[begin:end]
        both = by_tap(own, other)
        rows = chan_width >> dp_bits
        both = both.reshape([2, end - begin] + bits + [rows, chan_width])
        return halve(jnp.moveaxis(both, 1, 1 + dp_bits), order, jnp.bfloat16)

    cut = own_slots * 2 // 5
    conv_weight_grad = jnp.concatenate(
        [
            conv_part(0, cut, first),
            conv_part(cut, 2 * cut, second),
            conv_part(2 * cut, own_slots, third),
        ]
    )

    def spread(total, order, kind):
        rows = total.shape[0] >> (dp_bits + 1)
        split = total.reshape(bits + [2, rows] + list(total.shape[1:]))
        return halve(jnp.moveaxis(split, dp_bits, 0), order, kind)

    d_w_out_mine = spread(d_w_out, first, jnp.bfloat16)
    d_w_in_mine = spread(d_w_in, second, jnp.bfloat16)
    owners = 2 << dp_bits
    small = [d_b_in, d_b_out, d_conv_bias, d_gain_one, d_bias_one, d_gain_two, d_bias_two]
    joined = jnp.concatenate([v.reshape(owners, -1) for v in small], axis=1)
    joined_mine = spread(joined, third, jnp.float32).reshape(-1)
    vectors = []
    start = 0
    for v in small:
        size = v.shape[0] // owners
        vectors.append(joined_mine[start : start + size])
        start += size
    return (
        block_output,
        input_grad,
        conv_weight_grad,
        vectors[2],
        vectors[3],
        vectors[4],
        d_w_in_mine,
        vectors[0],
        d_w_out_mine,
        vectors[1],
        vectors[5],
        vectors[6],
    )


TILE = 256
COLS = 512
PAD = KERNEL_TAPS // 2 * DILATION_STEP
MIB = 2**20
TABLE_ROWS = 16
F32 = jnp.float32
BF16 = jnp.bfloat16
HBM = pl.BlockSpec(memory_space=pltpu.HBM)
VMEM = pl.BlockSpec(memory_space=pltpu.VMEM)
SMEM = pl.BlockSpec(memory_space=pltpu.SMEM)


def dot_plain(left, right):
    return lax.dot_general(left, right, (((1,), (0,)), ((), ())), preferred_element_type=F32)


def gelu_and_slope(value):
    cdf = 0.5 + 0.5 * lax.erf(value * 0.7071067811865476)
    density = 0.3989422804014327 * jnp.exp(value * value * -0.5)
    return value * cdf, cdf + value * density


def norm_parts(value):
    center = value - jnp.mean(value, axis=-1, keepdims=True)
    spread = jnp.mean(center * center, axis=-1, keepdims=True)
    scale = lax.rsqrt(spread + 1e-05)
    return center * scale, scale


def norm_back(grad, unit):
    return grad - jnp.mean(grad, axis=-1, keepdims=True) - unit * jnp.mean(
        grad * unit, axis=-1, keepdims=True
    )


def fold_rows(value):
    return jnp.sum(value.reshape(value.shape[0] // 8, 8, value.shape[1]), axis=0)


def one_row(value):
    return jnp.sum(value, axis=0, keepdims=True)


def my_bits(dp_bits):
    place = lax.axis_index("dp")
    mine = {bit: (place >> bit) & 1 for bit in range(dp_bits)}
    mine["t"] = lax.axis_index("tap")
    return mine


def relative(order, owner, mine):
    spot = 0
    for label in order:
        spot = spot * 2 + (owner[label] ^ mine[label])
    return spot


def rows_at(start, size):
    return pl.ds(pl.multiple_of(start, 16), size)


def split_copy(source, target, sems, first):
    rows = target.shape[0] // 4
    return [
        pltpu.make_async_copy(
            source.at[at * rows : (at + 1) * rows, :],
            target.at[at * rows : (at + 1) * rows, :],
            sems.at[first + at],
        )
        for at in range(4)
    ]


def wait_all(copies):
    for copy in copies:
        copy.wait()


def clear_pads(pad_ref):
    zeros = jnp.zeros((PAD, pad_ref.shape[2]), pad_ref.dtype)
    for win in range(pad_ref.shape[0]):
        pad_ref[win, 0:PAD, :] = zeros
        pad_ref[win, PAD + WINDOW_LENGTH :, :] = zeros


def row_tiles(rows):
    for at in range(0, rows, TILE):
        yield slice(at, at + TILE), at // WINDOW_LENGTH, at % WINDOW_LENGTH


def window_weight(species, counts, win, windows, lanes):
    kind = species[lax.axis_index("tap") * windows + win]
    count = jnp.full((8, lanes), counts[kind], jnp.int32).astype(F32)
    return (4.0 / count)[0:1, :]


def own_conv_kernel(table, x_hbm, weight_hbm, _, x_pad, part, token, weight, sems):
    windows = x_pad.shape[0]
    slots = weight.shape[0]
    base = lax.axis_index("tap") * windows * WINDOW_LENGTH
    copies = []
    for win in range(windows):
        source = x_hbm.at[rows_at(base + win * WINDOW_LENGTH, WINDOW_LENGTH), :]
        copies.append((source, x_pad.at[win, PAD : PAD + WINDOW_LENGTH, :]))
    copies += [(weight_hbm.at[slot], weight.at[slot]) for slot in range(slots)]
    copies = [
        pltpu.make_async_copy(source, target, sems.at[at])
        for at, (source, target) in enumerate(copies)
    ]
    for copy in copies:
        copy.start()
    clear_pads(x_pad)
    token[...] = jnp.zeros(token.shape, token.dtype)
    for copy in copies:
        copy.wait()
    for rows, win, begin in row_tiles(part.shape[0]):
        total = None
        for slot in range(slots):
            shifted = rows_at(table[slot] * DILATION_STEP + begin, TILE)
            term = dot_plain(x_pad[win, shifted, :], weight[slot])
            total = term if total is None else total + term
        part[rows, :] = total


def fetch_plan(rows):
    direct = rows // 8
    return direct, (rows - 2 * direct) // 8


def join_pieces(plan, pieces, weight):
    direct, shared = fetch_plan(weight.shape[1])
    place = lax.axis_index("dp")
    for (turn, first), piece in zip(plan, pieces):
        if first is None:
            at = ((place & 1) ^ turn) * direct
            for slot in range(weight.shape[0]):
                part = piece[slot * direct : (slot + 1) * direct, :]
                weight[slot, rows_at(at, direct), :] = part
            continue
        slots = weight.shape[0]
        for begin, place_turn in ((0, turn), (slots, first)):
            if begin < piece.shape[0]:
                at = 2 * direct + ((place & 7) ^ place_turn) * shared
                weight[:, rows_at(at, shared), :] = piece[begin : begin + slots]


def main_kernel(orders, dp_bits, turns, *refs):
    species, counts = refs[:2]
    x_pad, part, grad_hbm, w_in_hbm, w_out_hbm = refs[2:7]
    conv_bias, gain_one, bias_one, b_in, b_out, gain_two, bias_two = refs[7:14]
    pieces = refs[14 : 14 + len(turns)]
    y_hbm, unit, slope, d_up, weight, keep, send, small, grad_in, w_in, table = refs[
        14 + len(turns) : 25 + len(turns)
    ]
    w_out, hidden, low, act, hid_slope, d_out, y_low, result, sem, sems = refs[25 + len(turns) :]
    told = pieces[turns.index((0, None))]
    told_at = told.shape[0] - TABLE_ROWS
    taps = []
    for slot in range(weight.shape[0]):
        line = told[told_at : told_at + TABLE_ROWS, 0:128].astype(F32)
        chosen = lax.broadcasted_iota(jnp.int32, line.shape, 0) == slot
        taps.append(jnp.max(jnp.where(chosen, line, 0.0)).astype(jnp.int32))
        table[slot] = taps[slot]
    mine = my_bits(dp_bits)
    rows_dev, chan = hidden.shape
    hid_width = w_in.shape[1]
    windows = x_pad.shape[0]
    in_copies = split_copy(w_in_hbm, w_in, sems, 0)
    out_copies = split_copy(w_out_hbm, w_out, sems, 4)
    grad_copies = split_copy(grad_hbm, grad_in, sems, 8)
    for copy in in_copies + out_copies + grad_copies:
        copy.start()
    join_pieces(turns, pieces, weight)
    for rows, win, begin in row_tiles(rows_dev):
        total = part[rows, :] + conv_bias[...]
        for slot in range(weight.shape[0]):
            shifted = rows_at(taps[slot] * DILATION_STEP + begin, TILE)
            total = total + dot_plain(x_pad[win, shifted, :], weight[slot])
        value, steep = gelu_and_slope(total)
        normed, scale = norm_parts(value)
        unit[rows, :] = normed
        slope[rows, :] = scale * steep
        here = x_pad[win, PAD + begin : PAD + begin + TILE, :].astype(F32)
        summed = here + (normed * gain_one[...] + bias_one[...])
        hidden[rows, :] = summed
        low[rows, :] = summed.astype(BF16)
    wait_all(in_copies)
    for rows, win, begin in row_tiles(rows_dev):
        for at in range(0, hid_width, COLS):
            cols = slice(at, at + COLS)
            up = dot_plain(low[rows, :], w_in[:, cols]) + b_in[:, cols]
            value, steep = gelu_and_slope(up)
            act[rows, cols] = value.astype(BF16)
            hid_slope[rows, cols] = steep
    sum_b_out = 0.0
    sum_gain = 0.0
    sum_bias = 0.0
    wait_all(out_copies + grad_copies)
    for rows, win, begin in row_tiles(rows_dev):
        pre_out = dot_plain(act[rows, :], w_out[...]) + b_out[...]
        normed, scale = norm_parts(pre_out)
        result_rows = hidden[rows, :] + (normed * gain_two[...] + bias_two[...])
        y_low[rows, :] = result_rows.astype(BF16)
        grad_y = grad_in[rows, :].astype(F32) * window_weight(species, counts, win, windows, chan)
        sum_bias = sum_bias + fold_rows(grad_y)
        sum_gain = sum_gain + fold_rows(grad_y * normed)
        back = (norm_back(grad_y * gain_two[...], normed) * scale).astype(BF16)
        d_out[rows, :] = back
        sum_b_out = sum_b_out + fold_rows(back.astype(F32))
    y_copy = pltpu.make_async_copy(y_low, y_hbm, sem)
    y_copy.start()
    small[0:1, :] = one_row(sum_b_out)
    small[1:2, :] = one_row(sum_gain)
    small[2:3, :] = one_row(sum_bias)
    small[7:8, :] = jnp.zeros((1, chan), F32)
    sums_in = [0.0] * (hid_width // COLS)
    for rows, win, begin in row_tiles(rows_dev):
        for number, at in enumerate(range(0, hid_width, COLS)):
            cols = slice(at, at + COLS)
            d_act = contract_cols(d_out[rows, :], w_out[cols, :])
            back = (d_act * hid_slope[rows, cols]).astype(BF16)
            d_up[rows, cols] = back
            sums_in[number] = sums_in[number] + fold_rows(back.astype(F32))
    for number, total in enumerate(sums_in):
        small[3 + number : 4 + number, :] = one_row(total)
    core = mine[0]
    out_block = hid_width >> (dp_bits + 1)
    in_block = chan >> (dp_bits + 1)
    chunks = hid_width // COLS
    half = (out_block + chunks * in_block) // 2

    def hand_out(spot, first_row, block, targets):
        for start in range(0, result.shape[1], 4 * block):
            owner_at = (first_row + start) // block
            for tap in range(2):
                owner = {bit: (owner_at >> (bit + 1)) & 1 for bit in range(1, dp_bits)}
                owner["t"] = tap
                inner = start + tap * block
                for part_at, source, size, shift in targets:
                    spread = relative(orders[part_at], owner, mine) + (part_at << dp_bits)
                    place = rows_at(spread * half + shift, size)
                    mine_at = rows_at(inner + source + core * 2 * block, size)
                    other_at = rows_at(inner + source + (1 - core) * 2 * block, size)
                    keep[place, :] = result[spot, mine_at, :]
                    send[place, :] = result[spot, other_at, :].astype(BF16)

    for number, at in enumerate(range(0, hid_width, COLS)):
        result[number % 2] = contract_rows(act[:, at : at + COLS], d_out[...])
        size = out_block // 2
        hand_out(number % 2, at, out_block, [(0, 0, size, 0), (1, size, size, 0)])
    for number, at in enumerate(range(0, hid_width, COLS)):
        result[number % 2] = contract_rows(low[...], d_up[:, at : at + COLS])
        part_at, step = divmod(number, chunks // 2)
        shift = out_block // 2 + step * in_block
        hand_out(number % 2, 0, in_block, [(part_at, 0, in_block, shift)])
    y_copy.wait()


def back_kernel(
    species, counts, grad_in, w_in, d_up, unit, slope, gain_one, small_in, d_pad, d_hidden, small
):
    windows = d_pad.shape[0]
    chan = d_hidden.shape[1]
    sum_gain = 0.0
    sum_bias = 0.0
    sum_conv = 0.0
    clear_pads(d_pad)
    for rows, win, begin in row_tiles(d_hidden.shape[0]):
        grad = grad_in[rows, :].astype(F32) * window_weight(species, counts, win, windows, chan)
        grad = grad + contract_cols(d_up[rows, :], w_in[...])
        d_hidden[rows, :] = grad
        normed = unit[rows, :]
        sum_bias = sum_bias + fold_rows(grad)
        sum_gain = sum_gain + fold_rows(grad * normed)
        back = (norm_back(grad * gain_one[...], normed) * slope[rows, :]).astype(BF16)
        d_pad[win, PAD + begin : PAD + begin + TILE, :] = back
        sum_conv = sum_conv + fold_rows(back.astype(F32))
    small[0:8, :] = small_in[...]
    small[8:9, :] = one_row(sum_conv)
    small[9:10, :] = one_row(sum_gain)
    small[10:11, :] = one_row(sum_bias)
    small[11:16, :] = jnp.zeros((5, chan), F32)


def store_small(total, ref, first):
    count = total.shape[0]
    high = total.astype(BF16)
    ref[first : first + count, :] = high
    ref[first + count : first + 2 * count, :] = (total - high.astype(F32)).astype(BF16)


def load_small(ref, first, count):
    high = ref[first : first + count, :].astype(F32)
    return high + ref[first + count : first + 2 * count, :].astype(F32)


def terms_kernel(slots, orders, dp_bits, with_small, own_table, other_table, x_pad, d_pad, *refs):
    if with_small:
        small, _, keep, send, result = refs
        store_small(small[...], send, keep.shape[0])
    else:
        weight_hbm, _, keep, send, weight, result, sem = refs
        copies = [
            pltpu.make_async_copy(weight_hbm.at[slot], weight.at[slot], sem.at[slot])
            for slot in range(weight.shape[0])
        ]
        for copy in copies:
            copy.start()
    mine = my_bits(dp_bits)
    rows = x_pad.shape[2] >> dp_bits
    core = mine[0]
    turn = 0
    for near_tap, table in enumerate((own_table, other_table)):
        for number, slot in enumerate(slots):
            spot = turn % 2
            turn += 1
            total = None
            for win in range(x_pad.shape[0]):
                shifted = rows_at((KERNEL_TAPS - 1 - table[slot]) * DILATION_STEP, WINDOW_LENGTH)
                term = contract_rows(
                    x_pad[win, PAD : PAD + WINDOW_LENGTH, :], d_pad[win, shifted, :]
                )
                total = term if total is None else total + term
            result[spot] = total
            for start in range(0, x_pad.shape[2], 2 * rows):
                owner_at = start // rows
                owner = {bit: (owner_at >> bit) & 1 for bit in range(1, dp_bits)}
                owner["t"] = mine["t"] ^ near_tap
                size = rows // 2
                for part_at in range(2):
                    spread = relative(orders[part_at], owner, mine) + (part_at << dp_bits)
                    place = rows_at((spread * len(slots) + number) * size, size)
                    mine_at = rows_at(start + core * rows + part_at * size, size)
                    other_at = rows_at(start + (1 - core) * rows + part_at * size, size)
                    keep[place, :] = result[spot, mine_at, :]
                    send[place, :] = result[spot, other_at, :].astype(BF16)
    if not with_small:
        wait_all(copies)


def input_sum(table, d_pad, base, weight, rows, win, begin):
    total = base[rows, :]
    for slot in range(weight.shape[0]):
        shifted = rows_at((KERNEL_TAPS - 1 - table[slot]) * DILATION_STEP + begin, TILE)
        total = total + contract_cols(d_pad[win, shifted, :], weight[slot])
    return total


def input_near_kernel(table, d_pad, base, weight, _, out):
    for rows, win, begin in row_tiles(out.shape[0]):
        out[rows, :] = input_sum(table, d_pad, base, weight, rows, win, begin)


def input_far_kernel(table, d_pad, base, weight, _, out_hbm, token, out, sems):
    copies = []
    token[...] = jnp.zeros(token.shape, token.dtype)
    for rows, win, begin in row_tiles(out.shape[0]):
        out[rows, :] = input_sum(table, d_pad, base, weight, rows, win, begin)
        copies.append(
            pltpu.make_async_copy(out.at[rows, :], out_hbm.at[rows, :], sems.at[len(copies)])
        )
        copies[-1].start()
    for copy in copies:
        copy.wait()


def step_kernel(joined_in, joined_out, with_small, *refs):
    gots = refs[: 2 - joined_in]
    keep = refs[2 - joined_in]
    outs = refs[4 - joined_in + with_small :]
    rows = keep.shape[0] // 2
    half = rows // 2
    for part in range(2):
        got = gots[0 if joined_in else part]
        base = part * rows if joined_in else 0
        start = part * rows
        sent = keep[start + half : start + rows, :] + got[base + half : base + rows, :].astype(F32)
        if joined_out:
            outs[1][part * half : (part + 1) * half, :] = sent.astype(BF16)
        else:
            outs[1 + part][0:half, :] = sent.astype(BF16)
        kept = keep[start : start + half, :] + got[base : base + half, :].astype(F32)
        outs[0][part * half : (part + 1) * half, :] = kept
    if with_small:
        small = refs[3 - joined_in]
        total = small[...] + load_small(gots[0], rows * (1 + joined_in), small.shape[0])
        outs[3 - joined_out][...] = total
        store_small(total, outs[1], half * (1 + joined_out))


def sum_of(gots, keep, rows):
    total = keep[rows, :]
    for got in gots:
        total = total + got[rows, :].astype(F32)
    return total


def last_ffn_kernel(members, *refs):
    gots = refs[:members]
    keep, _, w_in_out, w_out_out = refs[members:]
    out_rows, chan = w_out_out.shape
    in_rows = w_in_out.shape[0]
    half = keep.shape[0] // 2
    steps = w_in_out.shape[1] // chan // 2
    for part in range(2):
        base = part * half
        size = out_rows // 2
        w_out_out[part * size : (part + 1) * size, :] = sum_of(gots, keep, slice(base, base + size))
        for step in range(steps):
            at = base + size + step * in_rows
            cols = slice((part * steps + step) * chan, (part * steps + step + 1) * chan)
            w_in_out[:, cols] = sum_of(gots, keep, slice(at, at + in_rows))


def last_small_kernel(got, keep, small, _, out, next_small):
    rows = out.shape[0]
    out[...] = keep[...] + got[0:rows, :].astype(F32)
    next_small[...] = small[...] + load_small(got, rows, small.shape[0])


def last_conv_kernel(got, keep, done, out):
    size = out.shape[1] // 2
    first = done.shape[0] // out.shape[1]
    rest = out.shape[0] - first
    for slot in range(out.shape[0]):
        for part in range(2):
            place = slice(part * size, (part + 1) * size)
            if slot < first:
                at = (part * first + slot) * size
                out[slot, place, :] = done[at : at + size, :]
            else:
                at = (part * rest + slot - first) * size
                out[slot, place, :] = keep[at : at + size, :] + got[at : at + size, :].astype(F32)


def params(mib):
    return pltpu.CompilerParams(vmem_limit_bytes=mib * MIB)


def claim(micros):
    return pl.CostEstimate(flops=int(micros * 1.1e9), bytes_accessed=1, transcendentals=0)


def after_kernel(_, token, out):
    del token, out


def after(value, token, claimed=0):
    return pl.pallas_call(
        after_kernel,
        out_shape=pltpu.VMEM(value.shape, value.dtype),
        in_specs=[VMEM] * 2,
        out_specs=VMEM,
        input_output_aliases={0: 0},
        compiler_params=params(4),
        cost_estimate=claim(claimed),
        name="after",
    )(near(value), near(token))


def far(value):
    return pltpu.with_memory_space_constraint(value, pltpu.HBM)


def near(value):
    return pltpu.with_memory_space_constraint(value, pltpu.VMEM)


def step(gots, keep, joined_out, token, small=None):
    lanes = keep.shape[1]
    half = keep.shape[0] // 4
    extra = 0 if small is None else 2 * small.shape[0]
    sent = [2 * half + extra] if joined_out else [half + extra, half]
    outs = [pltpu.VMEM((2 * half, lanes), F32)]
    outs += [pltpu.VMEM((rows, lanes), BF16) for rows in sent]
    operands = [near(got) for got in gots] + [near(keep)]
    if small is not None:
        outs.append(pltpu.VMEM(small.shape, F32))
        operands.append(near(small))
    out = pl.pallas_call(
        functools.partial(step_kernel, len(gots) == 1, joined_out, small is not None),
        out_shape=outs,
        in_specs=[VMEM] * (len(operands) + 1),
        out_specs=[VMEM] * len(outs),
        compiler_params=params(4),
        cost_estimate=claim(0),
        name="step",
    )(*operands, near(token))
    if small is None:
        return out[0], out[1:], None
    return out[0], out[1:-1], out[-1]


def swap(value, mask):
    count = lax.axis_size("dp") * lax.axis_size("tap")
    return lax.ppermute(value, ("dp", "tap"), [(i, i ^ mask) for i in range(count)])


def cut_kernel(table, weight_hbm, shared, direct, sems):
    slots = shared.shape[0]
    rows = (direct.shape[0] - TABLE_ROWS) // slots
    place = lax.axis_index("dp")
    start = 2 * rows + (place & 7) * shared.shape[1]
    near_start = (place & 1) * rows
    copies = []
    for slot in range(slots):
        pair = (
            (weight_hbm.at[slot, rows_at(start, shared.shape[1]), :], shared.at[slot]),
            (
                weight_hbm.at[slot, rows_at(near_start, rows), :],
                direct.at[slot * rows : (slot + 1) * rows, :],
            ),
        )
        for source, target in pair:
            copies.append(pltpu.make_async_copy(source, target, sems.at[len(copies)]))
    for copy in copies:
        copy.start()
    at = lax.broadcasted_iota(jnp.int32, (TABLE_ROWS, direct.shape[1]), 0)
    taps = jnp.zeros(at.shape, jnp.int32)
    for slot in range(slots):
        taps = jnp.where(at == slot, table[slot], taps)
    direct[slots * rows :, :] = taps.astype(F32).astype(BF16)
    for copy in copies:
        copy.wait()


def cut_pieces(table, conv_weight):
    slots, chan, width = conv_weight.shape
    direct, shared = fetch_plan(chan)
    return pl.pallas_call(
        cut_kernel,
        out_shape=[
            pltpu.VMEM((slots, shared, width), BF16),
            pltpu.VMEM((slots * direct + TABLE_ROWS, width), BF16),
        ],
        in_specs=[SMEM, HBM],
        out_specs=[VMEM] * 2,
        scratch_shapes=[pltpu.SemaphoreType.DMA((2 * slots,))],
        compiler_params=params(4),
        cost_estimate=claim(0),
        name="cut_pieces",
    )(table, far(conv_weight))


def pick_kernel(over_one, over_two, _, low, high, both):
    slots = over_one.shape[0]
    low[...] = over_two[0 : low.shape[0]]
    high[...] = over_one[low.shape[0] :]
    both[0:slots] = over_one[...]
    both[slots:] = over_two[...]


def pair_up_kernel(low, high, both):
    both[0 : low.shape[0]] = low[...]
    both[low.shape[0] :] = high[...]


def vmem_call(kernel, shapes, operands, name):
    return pl.pallas_call(
        kernel,
        out_shape=[pltpu.VMEM(shape, BF16) for shape in shapes],
        in_specs=[VMEM] * len(operands),
        out_specs=[VMEM] * len(shapes),
        compiler_params=params(4),
        cost_estimate=claim(0),
        name=name,
    )(*[near(operand) for operand in operands])


def fetch_pieces(first, direct, token):
    over_one = swap_dp(first, 1)
    over_two = swap_dp(first, 2)
    straight = swap_tap(after(direct, first))
    slots = first.shape[0]
    cut = (slots + 1) // 2
    rest = first.shape[1:]
    shapes = [(count,) + rest for count in (cut, slots - cut, 2 * slots)]
    low, high, both = vmem_call(pick_kernel, shapes, [over_one, over_two, token], "pick")
    (last,) = vmem_call(
        pair_up_kernel, [first.shape], [swap_dp(low, 1), swap_dp(high, 2)], "pair_up"
    )
    straight = after(straight, low)
    both_mate = swap_dp(both, 0)
    return [
        ((0, 0), first),
        ((2, 4), both),
        ((0, None), straight),
        ((6, 0), last),
        ((1, 0), swap_dp(first, 0)),
        ((3, 5), both_mate),
        ((1, None), swap_dp(straight, 0)),
        ((7, 0), swap_dp(last, 0)),
    ]


def fast_shards(
    block_input,
    conv_weight,
    slot_tap_table,
    conv_bias,
    conv_norm_gain,
    conv_norm_bias,
    w_in,
    b_in,
    w_out,
    b_out,
    ffn_norm_gain,
    ffn_norm_bias,
    species_id,
    species_count,
    out_grad,
):
    tap_count = lax.axis_size("tap")
    dp_bits = (lax.axis_size("dp") - 1).bit_length()
    rows_dev = block_input.shape[0] // tap_count
    chan = block_input.shape[1]
    hid = w_in.shape[1]
    windows = rows_dev // WINDOW_LENGTH
    slots = conv_weight.shape[0]
    vmem = pltpu.VMEM
    line = list(range(2, dp_bits))
    orders = (["t", 1] + line, [1, "t"] + line)
    over_x, over_y = 1, 4
    pad_shape = (windows, WINDOW_LENGTH + 2 * PAD, chan)
    rows_f = (rows_dev, chan)
    small_cost = claim(0)

    def row(vector):
        return vector.reshape(1, -1)

    shared, direct = cut_pieces(slot_tap_table, conv_weight)
    weight_shape = conv_weight.shape
    tiles = rows_dev // TILE
    dma = pltpu.SemaphoreType.DMA
    first = swap_tap(shared)
    x_pad, part, token = pl.pallas_call(
        own_conv_kernel,
        out_shape=[vmem(pad_shape, BF16), vmem(rows_f, F32), vmem((8, 128), F32)],
        in_specs=[SMEM] + [HBM] * 2 + [VMEM],
        out_specs=[VMEM] * 3,
        scratch_shapes=[vmem(weight_shape, BF16), dma((windows + slots,))],
        compiler_params=params(8),
        cost_estimate=claim(0),
        name="own_conv",
    )(slot_tap_table, far(block_input), far(conv_weight), near(first))
    pieces = fetch_pieces(first, direct, token)

    block_f = (hid + chan * hid // COLS) >> (dp_bits + 1)
    half_f = block_f << dp_bits
    main = pl.pallas_call(
        functools.partial(main_kernel, orders, dp_bits, [turn for turn, _ in pieces]),
        out_shape=[
            pltpu.HBM(rows_f, BF16),
            vmem(rows_f, F32),
            vmem(rows_f, F32),
            vmem((rows_dev, hid), BF16),
            vmem(conv_weight.shape, BF16),
            vmem((half_f, chan), F32),
            vmem((half_f, chan), BF16),
            vmem((8, chan), F32),
            vmem(rows_f, BF16),
            vmem(w_in.shape, BF16),
            jax.ShapeDtypeStruct((slots,), jnp.int32),
        ],
        in_specs=[SMEM] * 2 + [VMEM] * 2 + [HBM] * 3 + [VMEM] * (7 + len(pieces)),
        out_specs=[HBM] + [VMEM] * 9 + [SMEM],
        scratch_shapes=[
            vmem(w_out.shape, BF16),
            vmem(rows_f, F32),
            vmem(rows_f, BF16),
            vmem((rows_dev, hid), BF16),
            vmem((rows_dev, hid), F32),
            vmem(rows_f, BF16),
            vmem(rows_f, BF16),
            vmem((2, COLS, chan), F32),
            dma,
            dma((12,)),
        ],
        compiler_params=params(34),
        cost_estimate=small_cost,
        name="main_rows",
    )(
        species_id,
        species_count,
        near(x_pad),
        near(part),
        far(out_grad),
        far(w_in),
        far(w_out),
        row(conv_bias),
        row(conv_norm_gain),
        row(conv_norm_bias),
        row(b_in),
        row(b_out),
        row(ffn_norm_gain),
        row(ffn_norm_bias),
        *[near(piece) for _, piece in pieces],
    )
    block_output, unit, slope, d_up, other_weight, keep_f, send_f, small_ffn = main[:8]
    grad_in, w_in_near, other_table = main[8:]
    got_f = swap_dp(send_f, 0)

    d_pad, d_hidden, small = pl.pallas_call(
        back_kernel,
        out_shape=[vmem(pad_shape, BF16), vmem(rows_f, F32), vmem((16, chan), F32)],
        in_specs=[SMEM] * 2 + [VMEM] * 7,
        out_specs=[VMEM] * 3,
        compiler_params=params(8),
        cost_estimate=small_cost,
        name="back_rows",
    )(
        species_id,
        species_count,
        near(grad_in),
        near(w_in_near),
        near(d_up),
        near(unit),
        near(slope),
        row(conv_norm_gain),
        near(small_ffn),
    )
    keep_f, sends_f, _ = step([got_f], keep_f, False, small)
    gots_f = [swap(sends_f[0], over_x), swap(sends_f[1], over_y)]

    def terms(group, token, small, name):
        count = len(group) * chan
        extra = 0 if small is None else 2 * small.shape[0]
        outs = [vmem((count, chan), F32), vmem((count + extra, chan), BF16)]
        scratch = [vmem((2, chan, chan), F32)]
        if small is None:
            last, last_spec = far(conv_weight), HBM
            outs.append(vmem(weight_shape, BF16))
            scratch.append(dma((slots,)))
        else:
            last, last_spec = near(small), VMEM
        return pl.pallas_call(
            functools.partial(terms_kernel, group, orders, dp_bits, small is not None),
            out_shape=outs,
            in_specs=[SMEM] * 2 + [VMEM] * 2 + [last_spec, VMEM],
            out_specs=[VMEM] * len(outs),
            scratch_shapes=scratch,
            compiler_params=params(8),
            cost_estimate=small_cost,
            name=name,
        )(slot_tap_table, other_table, near(x_pad), near(d_pad), last, near(token))

    cut = (slots * 3 + 4) // 5
    keep_a, send_a = terms(range(0, cut), sends_f[0], small, "terms_a")
    got_a = swap_dp(send_a, 0)
    keep_b, send_b, own_weight = terms(range(cut, slots), keep_a, None, "terms_b")
    got_b = swap_dp(send_b, 0)
    def spaced(token, claimed=1):
        return after(mark, token, claimed)

    def turned(sends):
        return [swap(sends[0], over_y), swap(sends[1], over_x)]

    def along(sends, stage):
        return [swap(sends[0], 2 << line[stage])]

    mark = token
    keep_f, sends_f, _ = step(gots_f, keep_f, False, keep_b)
    gots_f = turned(sends_f)
    keep_a, sends_a, small = step([got_a], keep_a, False, spaced(keep_f, 100), small)
    gots_a = [swap(sends_a[0], over_x), swap(sends_a[1], over_y)]
    partial = pl.pallas_call(
        input_near_kernel,
        out_shape=vmem(rows_f, F32),
        in_specs=[SMEM] + [VMEM] * 4,
        out_specs=VMEM,
        compiler_params=params(8),
        cost_estimate=claim(0),
        name="input_near",
    )(slot_tap_table, near(d_pad), near(d_hidden), near(own_weight), near(keep_a))
    input_grad, mark = pl.pallas_call(
        input_far_kernel,
        out_shape=[pltpu.HBM(rows_f, F32), vmem((8, 128), F32)],
        in_specs=[SMEM] + [VMEM] * 4,
        out_specs=[HBM, VMEM],
        scratch_shapes=[vmem(rows_f, F32), pltpu.SemaphoreType.DMA((rows_dev // TILE,))],
        compiler_params=params(8),
        cost_estimate=small_cost,
        name="input_far",
    )(other_table, near(d_pad), near(partial), near(other_weight), near(keep_a))
    mark = spaced(mark)
    keep_f, sends_f, _ = step(gots_f, keep_f, True, mark)
    got_f = along(sends_f, 0)
    keep_b, sends_b, _ = step([got_b], keep_b, False, keep_f)
    gots_b = [swap(sends_b[0], over_x), swap(sends_b[1], over_y)]
    mark = spaced(keep_b)
    keep_a, sends_a, small = step(gots_a, keep_a, False, mark, small)
    gots_a = turned(sends_a)
    mark = spaced(keep_a)
    for stage in range(1, len(line)):
        keep_f, sends_f, _ = step(got_f, keep_f, True, mark)
        got_f = along(sends_f, stage)
        mark = spaced(keep_f)
    keep_b, sends_b, _ = step(gots_b, keep_b, False, mark)
    gots_b = turned(sends_b)
    mark = spaced(keep_b)
    keep_a, sends_a, small = step(gots_a, keep_a, True, mark, small)
    got_a = along(sends_a, 0)
    mark = spaced(keep_a)
    w_in_mine, w_out_mine = pl.pallas_call(
        functools.partial(last_ffn_kernel, 1),
        out_shape=[
            jax.ShapeDtypeStruct((chan >> (dp_bits + 1), hid), F32),
            jax.ShapeDtypeStruct((hid >> (dp_bits + 1), chan), F32),
        ],
        in_specs=[VMEM] * 3,
        out_specs=[VMEM] * 2,
        compiler_params=params(4),
        cost_estimate=claim(0),
        name="last_ffn",
    )(near(got_f[0]), near(keep_f), near(mark))
    keep_b, sends_b, _ = step(gots_b, keep_b, True, mark)
    got_b = along(sends_b, 0)
    mark = spaced(keep_b)
    for stage in range(1, len(line)):
        keep_a, sends_a, small = step(got_a, keep_a, True, mark, small)
        got_a = along(sends_a, stage)
        mark = spaced(keep_a)
        keep_b, sends_b, _ = step(got_b, keep_b, True, mark)
        got_b = along(sends_b, stage)
        mark = spaced(keep_b)
    part_a, small = pl.pallas_call(
        last_small_kernel,
        out_shape=[vmem(keep_a.shape, F32), vmem(small.shape, F32)],
        in_specs=[VMEM] * 4,
        out_specs=[VMEM] * 2,
        compiler_params=params(4),
        cost_estimate=claim(0),
        name="last_a",
    )(near(got_a[0]), near(keep_a), near(small), near(mark))
    conv_weight_grad = pl.pallas_call(
        last_conv_kernel,
        out_shape=jax.ShapeDtypeStruct((slots, chan >> dp_bits, chan), F32),
        in_specs=[VMEM] * 3,
        out_specs=VMEM,
        compiler_params=params(4),
        cost_estimate=claim(0),
        name="last_conv",
    )(near(got_b[0]), near(keep_b), near(part_a))
    chunks = hid // COLS

    owner = lax.axis_index("dp") * tap_count + lax.axis_index("tap")
    width = chan >> (dp_bits + 1)
    lanes = lax.dynamic_slice(small, (0, owner * width), (small.shape[0], width))
    wide = hid >> (dp_bits + 1)
    d_b_in = lax.dynamic_slice(small[3 : 3 + chunks].reshape(-1), (owner * wide,), (wide,))
    return (
        block_output,
        input_grad,
        conv_weight_grad,
        lanes[8],
        lanes[9],
        lanes[10],
        w_in_mine,
        d_b_in,
        w_out_mine,
        lanes[0],
        lanes[1],
        lanes[2],
    )


def narrow_enough(mesh):
    return mesh.shape["tap"] == 2 and mesh.shape["dp"] == 16


def solution(mesh):
    chosen = fast_shards if narrow_enough(mesh) else plain_shards
    return jax.shard_map(
        chosen,
        mesh=mesh,
        in_specs=(
            P("dp", None),
            P("tap", None, None),
            P("tap"),
            P(),
            P(),
            P(),
            P(),
            P(),
            P(),
            P(),
            P(),
            P(),
            P("dp"),
            P(),
            P(("dp", "tap"), None),
        ),
        out_specs=(
            P(("dp", "tap"), None),
            P(("dp", "tap"), None),
            P("tap", "dp", None),
            P(("dp", "tap")),
            P(("dp", "tap")),
            P(("dp", "tap")),
            P(("dp", "tap"), None),
            P(("dp", "tap")),
            P(("dp", "tap"), None),
            P(("dp", "tap")),
            P(("dp", "tap")),
            P(("dp", "tap")),
        ),
        check_vma=False,
    )
```

```python
import functools

import jax
import jax.numpy as jnp
from jax import lax
from jax.experimental import pallas as pl
from jax.experimental.pallas import tpu as pltpu
from jax.sharding import PartitionSpec as P

KERNEL_TAPS = 9
DILATION_STEP = 16
WINDOW_LENGTH = 512


def layer_norm(values):
    mean_val = jnp.mean(values, axis=-1, keepdims=True)
    center = values - mean_val
    spread = jnp.mean(center * center, axis=-1, keepdims=True)
    return center * lax.rsqrt(spread + 1e-05)


def exact_gelu(values):
    return jax.nn.gelu(values, approximate=False)


def conv_branch(pre_conv, gain_one, bias_one):
    return layer_norm(exact_gelu(pre_conv)) * gain_one + bias_one


def ffn_branch(pre_out, gain_two, bias_two):
    return layer_norm(pre_out) * gain_two + bias_two


def shift_stack(win_rows, tap_table, forward):
    tap_extent = KERNEL_TAPS // 2 * DILATION_STEP
    padded_input = jnp.pad(win_rows, ((0, 0), (tap_extent, tap_extent), (0, 0)))
    pieces = []
    for index_of_slot in range(tap_table.shape[0]):
        if forward:
            tap_offset = tap_table[index_of_slot]
        else:
            tap_offset = KERNEL_TAPS - 1 - tap_table[index_of_slot]
        shifted_input = lax.dynamic_slice_in_dim(
            padded_input, tap_offset * DILATION_STEP, WINDOW_LENGTH, 1
        )
        pieces.append(shifted_input.reshape(-1, win_rows.shape[2]))
    return jnp.stack(pieces)


def contract_rows(left, right):
    return lax.dot_general(
        left, right, (((0,), (0,)), ((), ())), preferred_element_type=jnp.float32
    )


def contract_cols(left, right):
    return lax.dot_general(
        left, right, (((1,), (1,)), ((), ())), preferred_element_type=jnp.float32
    )


def swap_dp(value, bit):
    count = lax.axis_size("dp")
    return lax.ppermute(value, "dp", [(i, i ^ (1 << bit)) for i in range(count)])


def swap_tap(value):
    return lax.ppermute(value, "tap", [(0, 1), (1, 0)])


def halve(part, order, kind):
    dp_bits = (lax.axis_size("dp") - 1).bit_length()
    place = lax.axis_index("dp")
    tap = lax.axis_index("tap")
    labels = ["t"] + list(range(dp_bits - 1, -1, -1))
    for step in order:
        axis = labels.index(step)
        labels.pop(axis)
        mine = tap if step == "t" else (place >> step) & 1
        keep = lax.dynamic_index_in_dim(part, mine, axis, keepdims=False)
        send = lax.dynamic_index_in_dim(part, 1 - mine, axis, keepdims=False).astype(kind)
        got = swap_tap(send) if step == "t" else swap_dp(send, step)
        part = keep + got.astype(jnp.float32)
    return part


def orders(dp_bits):
    rest = list(range(2, dp_bits))
    first = [0, "t", 1] + rest
    second = [0, 1] + rest[:1] + ["t"] + rest[1:]
    third = [0] + rest[:1] + ["t", 1] + rest[1:]
    return first, second, third


def plain_shards(
    block_input,
    conv_weight,
    slot_tap_table,
    conv_bias,
    conv_norm_gain,
    conv_norm_bias,
    w_in,
    b_in,
    w_out,
    b_out,
    ffn_norm_gain,
    ffn_norm_bias,
    species_id,
    species_count,
    out_grad,
):
    tap_count = lax.axis_size("tap")
    my_index = lax.axis_index("tap")
    core = lax.axis_index("dp") & 1
    dp_bits = (lax.axis_size("dp") - 1).bit_length()
    tok_dev, chan_width = block_input.shape
    hid_width = w_in.shape[1]
    half_rows = tok_dev // tap_count
    windows = tok_dev // WINDOW_LENGTH
    my_windows = windows // tap_count
    own_slots = conv_weight.shape[0]
    half_chan = chan_width // 2
    first, second, third = orders(dp_bits)

    other_table = swap_tap(slot_tap_table)
    part_send = lax.dynamic_slice_in_dim(conv_weight, core * half_chan, half_chan, 1)
    part_here = swap_tap(part_send)
    part_mate = swap_dp(part_here, 0)
    low_part = jnp.where(core == 0, part_here, part_mate)
    high_part = jnp.where(core == 0, part_mate, part_here)
    other_weight = jnp.concatenate([low_part, high_part], axis=1)

    my_x = lax.dynamic_slice_in_dim(block_input, my_index * half_rows, half_rows, 0)
    x_windows = my_x.reshape(my_windows, WINDOW_LENGTH, chan_width)
    mine_x = my_x.astype(jnp.float32)
    own_stack = shift_stack(x_windows, slot_tap_table, True)
    other_stack = shift_stack(x_windows, other_table, True)
    conv_out = jnp.einsum("str,sro->to", own_stack, conv_weight, preferred_element_type=jnp.float32)
    conv_out = conv_out + jnp.einsum(
        "str,sro->to", other_stack, other_weight, preferred_element_type=jnp.float32
    )
    pre_conv = conv_out + conv_bias
    norm_one, conv_back = jax.vjp(conv_branch, pre_conv, conv_norm_gain, conv_norm_bias)
    hidden = mine_x + norm_one
    hidden_low = hidden.astype(jnp.bfloat16)
    pre_up = jnp.dot(hidden_low, w_in, preferred_element_type=jnp.float32) + b_in
    activ, activ_back = jax.vjp(exact_gelu, pre_up)
    act_low = activ.astype(jnp.bfloat16)
    pre_out = jnp.dot(act_low, w_out, preferred_element_type=jnp.float32) + b_out
    norm_two, ffn_back = jax.vjp(ffn_branch, pre_out, ffn_norm_gain, ffn_norm_bias)
    block_output = (hidden + norm_two).astype(jnp.bfloat16)
    my_species = lax.dynamic_slice_in_dim(species_id, my_index * my_windows, my_windows, 0)
    species_range = jnp.arange(species_count.shape[0], dtype=jnp.int32)
    matches = my_species[:, None] == species_range[None, :]
    window_count = jnp.sum(jnp.where(matches, species_count[None, :], 0), axis=1)
    window_scale = 4.0 / window_count.astype(jnp.float32)
    grad_y = (
        out_grad.astype(jnp.float32).reshape(my_windows, WINDOW_LENGTH, chan_width)
        * window_scale[:, None, None]
    ).reshape(half_rows, chan_width)
    d_pre_out, d_gain_two, d_bias_two = ffn_back(grad_y)
    d_out_low = d_pre_out.astype(jnp.bfloat16)
    d_w_out = contract_rows(act_low, d_out_low)
    d_b_out = jnp.sum(d_out_low.astype(jnp.float32), axis=0)
    d_activ = contract_cols(d_out_low, w_out)
    (d_pre_up,) = activ_back(d_activ)
    d_up_low = d_pre_up.astype(jnp.bfloat16)
    d_w_in = contract_rows(hidden_low, d_up_low)
    d_b_in = jnp.sum(d_up_low.astype(jnp.float32), axis=0)
    d_hidden = grad_y + contract_cols(d_up_low, w_in)
    d_pre_conv, d_gain_one, d_bias_one = conv_back(d_hidden)
    d_conv_low = d_pre_conv.astype(jnp.bfloat16)
    d_conv_bias = jnp.sum(d_conv_low.astype(jnp.float32), axis=0)
    d_windows = d_conv_low.reshape(my_windows, WINDOW_LENGTH, chan_width)
    own_back = shift_stack(d_windows, slot_tap_table, False)
    other_back = shift_stack(d_windows, other_table, False)
    input_grad = (
        d_hidden
        + jnp.einsum("sto,sro->tr", own_back, conv_weight, preferred_element_type=jnp.float32)
        + jnp.einsum("sto,sro->tr", other_back, other_weight, preferred_element_type=jnp.float32)
    )
    own_terms = jnp.einsum("str,to->sro", own_stack, d_conv_low, preferred_element_type=jnp.float32)
    other_terms = jnp.einsum(
        "str,to->sro", other_stack, d_conv_low, preferred_element_type=jnp.float32
    )
    bits = [2] * dp_bits

    def by_tap(own, other):
        return jnp.where(my_index == 0, jnp.stack([own, other]), jnp.stack([other, own]))

    def conv_part(begin, end, order):
        own = own_terms[begin:end]
        other = other_terms[begin:end]
        both = by_tap(own, other)
        rows = chan_width >> dp_bits
        both = both.reshape([2, end - begin] + bits + [rows, chan_width])
        return halve(jnp.moveaxis(both, 1, 1 + dp_bits), order, jnp.bfloat16)

    cut = own_slots * 2 // 5
    conv_weight_grad = jnp.concatenate(
        [
            conv_part(0, cut, first),
            conv_part(cut, 2 * cut, second),
            conv_part(2 * cut, own_slots, third),
        ]
    )

    def spread(total, order, kind):
        rows = total.shape[0] >> (dp_bits + 1)
        split = total.reshape(bits + [2, rows] + list(total.shape[1:]))
        return halve(jnp.moveaxis(split, dp_bits, 0), order, kind)

    d_w_out_mine = spread(d_w_out, first, jnp.bfloat16)
    d_w_in_mine = spread(d_w_in, second, jnp.bfloat16)
    owners = 2 << dp_bits
    small = [d_b_in, d_b_out, d_conv_bias, d_gain_one, d_bias_one, d_gain_two, d_bias_two]
    joined = jnp.concatenate([v.reshape(owners, -1) for v in small], axis=1)
    joined_mine = spread(joined, third, jnp.float32).reshape(-1)
    vectors = []
    start = 0
    for v in small:
        size = v.shape[0] // owners
        vectors.append(joined_mine[start : start + size])
        start += size
    return (
        block_output,
        input_grad,
        conv_weight_grad,
        vectors[2],
        vectors[3],
        vectors[4],
        d_w_in_mine,
        vectors[0],
        d_w_out_mine,
        vectors[1],
        vectors[5],
        vectors[6],
    )


TILE = 256
COLS = 512
PAD = KERNEL_TAPS // 2 * DILATION_STEP
MIB = 2**20
TABLE_ROWS = 16
F32 = jnp.float32
BF16 = jnp.bfloat16
HBM = pl.BlockSpec(memory_space=pltpu.HBM)
VMEM = pl.BlockSpec(memory_space=pltpu.VMEM)
SMEM = pl.BlockSpec(memory_space=pltpu.SMEM)


def dot_plain(left, right):
    return lax.dot_general(left, right, (((1,), (0,)), ((), ())), preferred_element_type=F32)


def gelu_and_slope(value):
    cdf = 0.5 + 0.5 * lax.erf(value * 0.7071067811865476)
    density = 0.3989422804014327 * jnp.exp(value * value * -0.5)
    return value * cdf, cdf + value * density


def norm_parts(value):
    center = value - jnp.mean(value, axis=-1, keepdims=True)
    spread = jnp.mean(center * center, axis=-1, keepdims=True)
    scale = lax.rsqrt(spread + 1e-05)
    return center * scale, scale


def norm_back(grad, unit):
    return grad - jnp.mean(grad, axis=-1, keepdims=True) - unit * jnp.mean(
        grad * unit, axis=-1, keepdims=True
    )


def fold_rows(value):
    return jnp.sum(value.reshape(value.shape[0] // 8, 8, value.shape[1]), axis=0)


def one_row(value):
    return jnp.sum(value, axis=0, keepdims=True)


def my_bits(dp_bits):
    place = lax.axis_index("dp")
    mine = {bit: (place >> bit) & 1 for bit in range(dp_bits)}
    mine["t"] = lax.axis_index("tap")
    return mine


def relative(order, owner, mine):
    spot = 0
    for label in order:
        spot = spot * 2 + (owner[label] ^ mine[label])
    return spot


def rows_at(start, size):
    return pl.ds(pl.multiple_of(start, 16), size)


def split_copy(source, target, sems, first):
    rows = target.shape[0] // 4
    return [
        pltpu.make_async_copy(
            source.at[at * rows : (at + 1) * rows, :],
            target.at[at * rows : (at + 1) * rows, :],
            sems.at[first + at],
        )
        for at in range(4)
    ]


def wait_all(copies):
    for copy in copies:
        copy.wait()


def clear_pads(pad_ref):
    zeros = jnp.zeros((PAD, pad_ref.shape[2]), pad_ref.dtype)
    for win in range(pad_ref.shape[0]):
        pad_ref[win, 0:PAD, :] = zeros
        pad_ref[win, PAD + WINDOW_LENGTH :, :] = zeros


def each_tile(rows, body, together=1):
    per = WINDOW_LENGTH // TILE

    @pl.loop(0, rows // TILE // together)
    def _(step):
        for member in range(together):
            number = step * together + member
            body(rows_at(number * TILE, TILE), number // per, (number % per) * TILE)


def window_weight(species, counts, win, windows, lanes):
    kind = species[lax.axis_index("tap") * windows + win]
    count = jnp.full((8, lanes), counts[kind], jnp.int32).astype(F32)
    return (4.0 / count)[0:1, :]


def own_conv_kernel(table, x_hbm, weight_hbm, _, x_pad, part, token, weight, sems):
    windows = x_pad.shape[0]
    slots = weight.shape[0]
    base = lax.axis_index("tap") * windows * WINDOW_LENGTH
    copies = []
    for win in range(windows):
        source = x_hbm.at[rows_at(base + win * WINDOW_LENGTH, WINDOW_LENGTH), :]
        copies.append((source, x_pad.at[win, PAD : PAD + WINDOW_LENGTH, :]))
    copies += [(weight_hbm.at[slot], weight.at[slot]) for slot in range(slots)]
    copies = [
        pltpu.make_async_copy(source, target, sems.at[at])
        for at, (source, target) in enumerate(copies)
    ]
    for copy in copies:
        copy.start()
    clear_pads(x_pad)
    token[...] = jnp.zeros(token.shape, token.dtype)
    for copy in copies:
        copy.wait()

    def convolve(rows, win, begin):
        total = None
        for slot in range(slots):
            shifted = rows_at(table[slot] * DILATION_STEP + begin, TILE)
            term = dot_plain(x_pad[win, shifted, :], weight[slot])
            total = term if total is None else total + term
        part[rows, :] = total

    each_tile(part.shape[0], convolve, 2)


def fetch_plan(rows):
    direct = rows // 8
    return direct, (rows - 2 * direct) // 8


def join_pieces(plan, pieces, weight):
    direct, shared = fetch_plan(weight.shape[1])
    place = lax.axis_index("dp")
    for (turn, first), piece in zip(plan, pieces):
        if first is None:
            at = ((place & 1) ^ turn) * direct
            for slot in range(weight.shape[0]):
                part = piece[slot * direct : (slot + 1) * direct, :]
                weight[slot, rows_at(at, direct), :] = part
            continue
        slots = weight.shape[0]
        for begin, place_turn in ((0, turn), (slots, first)):
            if begin < piece.shape[0]:
                at = 2 * direct + ((place & 7) ^ place_turn) * shared
                weight[:, rows_at(at, shared), :] = piece[begin : begin + slots]


def main_kernel(orders, dp_bits, turns, *refs):
    species, counts = refs[:2]
    x_pad, part, grad_hbm, w_in_hbm, w_out_hbm = refs[2:7]
    conv_bias, gain_one, bias_one, b_in, b_out, gain_two, bias_two = refs[7:14]
    pieces = refs[14 : 14 + len(turns)]
    y_hbm, unit, slope, d_up, weight, keep, send, small, grad_in, w_in, table = refs[
        14 + len(turns) : 25 + len(turns)
    ]
    w_out, hidden, low, act, hid_slope, d_out, y_low, result, sums, sem, sems = refs[25 + len(turns) :]
    told = pieces[turns.index((0, None))]
    told_at = told.shape[0] - TABLE_ROWS
    taps = []
    for slot in range(weight.shape[0]):
        line = told[told_at : told_at + TABLE_ROWS, 0:128].astype(F32)
        chosen = lax.broadcasted_iota(jnp.int32, line.shape, 0) == slot
        taps.append(jnp.max(jnp.where(chosen, line, 0.0)).astype(jnp.int32))
        table[slot] = taps[slot]
    mine = my_bits(dp_bits)
    rows_dev, chan = hidden.shape
    hid_width = w_in.shape[1]
    windows = x_pad.shape[0]
    in_copies = split_copy(w_in_hbm, w_in, sems, 0)
    out_copies = split_copy(w_out_hbm, w_out, sems, 4)
    grad_copies = split_copy(grad_hbm, grad_in, sems, 8)
    for copy in in_copies + out_copies + grad_copies:
        copy.start()
    join_pieces(turns, pieces, weight)
    sums[...] = jnp.zeros(sums.shape, F32)

    def first_norm(rows, win, begin):
        total = part[rows, :] + conv_bias[...]
        for slot in range(weight.shape[0]):
            shifted = rows_at(taps[slot] * DILATION_STEP + begin, TILE)
            total = total + dot_plain(x_pad[win, shifted, :], weight[slot])
        value, steep = gelu_and_slope(total)
        normed, scale = norm_parts(value)
        unit[rows, :] = normed
        slope[rows, :] = scale * steep
        here = x_pad[win, rows_at(PAD + begin, TILE), :].astype(F32)
        summed = here + (normed * gain_one[...] + bias_one[...])
        hidden[rows, :] = summed
        low[rows, :] = summed.astype(BF16)

    each_tile(rows_dev, first_norm, 2)
    wait_all(in_copies)

    def go_up(rows, win, begin):
        for at in range(0, hid_width, COLS):
            cols = slice(at, at + COLS)
            up = dot_plain(low[rows, :], w_in[:, cols]) + b_in[:, cols]
            value, steep = gelu_and_slope(up)
            act[rows, cols] = value.astype(BF16)
            hid_slope[rows, cols] = steep

    each_tile(rows_dev, go_up, 2)
    wait_all(out_copies + grad_copies)

    def second_norm(rows, win, begin):
        pre_out = dot_plain(act[rows, :], w_out[...]) + b_out[...]
        normed, scale = norm_parts(pre_out)
        result_rows = hidden[rows, :] + (normed * gain_two[...] + bias_two[...])
        y_low[rows, :] = result_rows.astype(BF16)
        grad_y = grad_in[rows, :].astype(F32) * window_weight(species, counts, win, windows, chan)
        back = (norm_back(grad_y * gain_two[...], normed) * scale).astype(BF16)
        d_out[rows, :] = back
        sums[0] += fold_rows(back.astype(F32))
        sums[1] += fold_rows(grad_y * normed)
        sums[2] += fold_rows(grad_y)

    each_tile(rows_dev, second_norm, 2)
    y_copy = pltpu.make_async_copy(y_low, y_hbm, sem)
    y_copy.start()

    def go_down(rows, win, begin):
        for number, at in enumerate(range(0, hid_width, COLS)):
            cols = slice(at, at + COLS)
            d_act = contract_cols(d_out[rows, :], w_out[cols, :])
            back = (d_act * hid_slope[rows, cols]).astype(BF16)
            d_up[rows, cols] = back
            sums[3 + number] += fold_rows(back.astype(F32))

    each_tile(rows_dev, go_down, 2)
    for number in range(8):
        small[number : number + 1, :] = one_row(sums[number])
    core = mine[0]
    out_block = hid_width >> (dp_bits + 1)
    in_block = chan >> (dp_bits + 1)
    chunks = hid_width // COLS
    half = (out_block + chunks * in_block) // 2

    def hand_out(spot, first_row, block, targets):
        for start in range(0, result.shape[1], 4 * block):
            owner_at = first_row // block + start // block
            for tap in range(2):
                owner = {bit: (owner_at >> (bit + 1)) & 1 for bit in range(1, dp_bits)}
                owner["t"] = tap
                inner = start + tap * block
                for part_at, source, size, shift in targets:
                    spread = relative(orders[part_at], owner, mine) + (part_at << dp_bits)
                    place = rows_at(spread * half + shift, size)
                    mine_at = rows_at(inner + source + core * 2 * block, size)
                    other_at = rows_at(inner + source + (1 - core) * 2 * block, size)
                    keep[place, :] = result[spot, mine_at, :]
                    send[place, :] = result[spot, other_at, :].astype(BF16)

    size = out_block // 2

    @pl.loop(0, chunks // 2)
    def _(pair):
        for spot in range(2):
            at = pl.multiple_of((pair * 2 + spot) * COLS, COLS)
            result[spot] = contract_rows(act[:, pl.ds(at, COLS)], d_out[...])
            hand_out(spot, at, out_block, [(0, 0, size, 0), (1, size, size, 0)])

    @pl.loop(0, chunks // 2)
    def _(step):
        shift = size + step * in_block
        for spot in range(2):
            at = pl.multiple_of((spot * (chunks // 2) + step) * COLS, COLS)
            result[spot] = contract_rows(low[...], d_up[:, pl.ds(at, COLS)])
            hand_out(spot, 0, in_block, [(spot, 0, in_block, shift)])

    y_copy.wait()


def back_kernel(
    species,
    counts,
    grad_in,
    w_in,
    d_up,
    unit,
    slope,
    gain_one,
    small_in,
    d_pad,
    d_hidden,
    small,
    sums,
):
    windows = d_pad.shape[0]
    chan = d_hidden.shape[1]
    clear_pads(d_pad)
    sums[...] = jnp.zeros(sums.shape, F32)

    def through_norm(rows, win, begin):
        grad = grad_in[rows, :].astype(F32) * window_weight(species, counts, win, windows, chan)
        grad = grad + contract_cols(d_up[rows, :], w_in[...])
        d_hidden[rows, :] = grad
        normed = unit[rows, :]
        back = (norm_back(grad * gain_one[...], normed) * slope[rows, :]).astype(BF16)
        d_pad[win, rows_at(PAD + begin, TILE), :] = back
        sums[0] += fold_rows(back.astype(F32))
        sums[1] += fold_rows(grad * normed)
        sums[2] += fold_rows(grad)

    each_tile(d_hidden.shape[0], through_norm, 2)
    small[0:8, :] = small_in[...]
    for number in range(8):
        small[8 + number : 9 + number, :] = one_row(sums[number])


def store_small(total, ref, first):
    count = total.shape[0]
    high = total.astype(BF16)
    ref[first : first + count, :] = high
    ref[first + count : first + 2 * count, :] = (total - high.astype(F32)).astype(BF16)


def load_small(ref, first, count):
    high = ref[first : first + count, :].astype(F32)
    return high + ref[first + count : first + 2 * count, :].astype(F32)


def terms_kernel(slots, orders, dp_bits, with_small, own_table, other_table, x_pad, d_pad, *refs):
    if with_small:
        small, _, keep, send, result = refs
        store_small(small[...], send, keep.shape[0])
    else:
        weight_hbm, _, keep, send, weight, result, sem = refs
        copies = [
            pltpu.make_async_copy(weight_hbm.at[slot], weight.at[slot], sem.at[slot])
            for slot in range(weight.shape[0])
        ]
        for copy in copies:
            copy.start()
    mine = my_bits(dp_bits)
    rows = x_pad.shape[2] >> dp_bits
    core = mine[0]
    tables = (own_table, other_table)
    size = rows // 2

    @pl.loop(0, len(slots))
    def _(number):
        for near_tap in range(2):
            tap = tables[near_tap][slots[0] + number]
            shifted = rows_at((KERNEL_TAPS - 1 - tap) * DILATION_STEP, WINDOW_LENGTH)
            total = None
            for win in range(x_pad.shape[0]):
                term = contract_rows(
                    x_pad[win, PAD : PAD + WINDOW_LENGTH, :], d_pad[win, shifted, :]
                )
                total = term if total is None else total + term
            result[near_tap] = total
            for start in range(0, x_pad.shape[2], 2 * rows):
                owner_at = start // rows
                owner = {bit: (owner_at >> bit) & 1 for bit in range(1, dp_bits)}
                owner["t"] = mine["t"] ^ near_tap
                for part_at in range(2):
                    spread = relative(orders[part_at], owner, mine) + (part_at << dp_bits)
                    place = rows_at((spread * len(slots) + number) * size, size)
                    mine_at = rows_at(start + core * rows + part_at * size, size)
                    other_at = rows_at(start + (1 - core) * rows + part_at * size, size)
                    keep[place, :] = result[near_tap, mine_at, :]
                    send[place, :] = result[near_tap, other_at, :].astype(BF16)

    if not with_small:
        wait_all(copies)


def input_sum(table, d_pad, base, weight, rows, win, begin):
    total = base[rows, :]
    for slot in range(weight.shape[0]):
        shifted = rows_at((KERNEL_TAPS - 1 - table[slot]) * DILATION_STEP + begin, TILE)
        total = total + contract_cols(d_pad[win, shifted, :], weight[slot])
    return total


def input_near_kernel(table, d_pad, base, weight, _, out):
    def gather(rows, win, begin):
        out[rows, :] = input_sum(table, d_pad, base, weight, rows, win, begin)

    each_tile(out.shape[0], gather, 2)


def input_far_kernel(table, d_pad, base, weight, _, out_hbm, token, out, sems):
    token[...] = jnp.zeros(token.shape, token.dtype)

    def copy_of(rows):
        return pltpu.make_async_copy(out.at[rows, :], out_hbm.at[rows, :], sems.at[0])

    def gather(rows, win, begin):
        out[rows, :] = input_sum(table, d_pad, base, weight, rows, win, begin)
        copy_of(rows).start()

    each_tile(out.shape[0], gather, 2)
    pltpu.make_async_copy(out, out_hbm, sems.at[0]).wait()


def step_kernel(joined_in, joined_out, with_small, *refs):
    gots = refs[: 2 - joined_in]
    keep = refs[2 - joined_in]
    outs = refs[4 - joined_in + with_small :]
    rows = keep.shape[0] // 2
    half = rows // 2
    for part in range(2):
        got = gots[0 if joined_in else part]
        base = part * rows if joined_in else 0
        start = part * rows
        sent = keep[start + half : start + rows, :] + got[base + half : base + rows, :].astype(F32)
        if joined_out:
            outs[1][part * half : (part + 1) * half, :] = sent.astype(BF16)
        else:
            outs[1 + part][0:half, :] = sent.astype(BF16)
        kept = keep[start : start + half, :] + got[base : base + half, :].astype(F32)
        outs[0][part * half : (part + 1) * half, :] = kept
    if with_small:
        small = refs[3 - joined_in]
        total = small[...] + load_small(gots[0], rows * (1 + joined_in), small.shape[0])
        outs[3 - joined_out][...] = total
        store_small(total, outs[1], half * (1 + joined_out))


def sum_of(gots, keep, rows):
    total = keep[rows, :]
    for got in gots:
        total = total + got[rows, :].astype(F32)
    return total


def last_ffn_kernel(members, *refs):
    gots = refs[:members]
    keep, _, w_in_out, w_out_out = refs[members:]
    out_rows, chan = w_out_out.shape
    in_rows = w_in_out.shape[0]
    half = keep.shape[0] // 2
    steps = w_in_out.shape[1] // chan // 2
    for part in range(2):
        base = part * half
        size = out_rows // 2
        w_out_out[part * size : (part + 1) * size, :] = sum_of(gots, keep, slice(base, base + size))
        for step in range(steps):
            at = base + size + step * in_rows
            cols = slice((part * steps + step) * chan, (part * steps + step + 1) * chan)
            w_in_out[:, cols] = sum_of(gots, keep, slice(at, at + in_rows))


def last_small_kernel(got, keep, small, _, out, next_small):
    rows = out.shape[0]
    out[...] = keep[...] + got[0:rows, :].astype(F32)
    next_small[...] = small[...] + load_small(got, rows, small.shape[0])


def last_conv_kernel(got, keep, done, out):
    size = out.shape[1] // 2
    first = done.shape[0] // out.shape[1]
    rest = out.shape[0] - first
    for slot in range(out.shape[0]):
        for part in range(2):
            place = slice(part * size, (part + 1) * size)
            if slot < first:
                at = (part * first + slot) * size
                out[slot, place, :] = done[at : at + size, :]
            else:
                at = (part * rest + slot - first) * size
                out[slot, place, :] = keep[at : at + size, :] + got[at : at + size, :].astype(F32)


def params(mib):
    return pltpu.CompilerParams(vmem_limit_bytes=mib * MIB)


def claim(micros):
    return pl.CostEstimate(flops=int(micros * 1.1e9), bytes_accessed=1, transcendentals=0)


def after_kernel(_, token, out):
    del token, out


def after(value, token, claimed=0):
    return pl.pallas_call(
        after_kernel,
        out_shape=pltpu.VMEM(value.shape, value.dtype),
        in_specs=[VMEM] * 2,
        out_specs=VMEM,
        input_output_aliases={0: 0},
        compiler_params=params(4),
        cost_estimate=claim(claimed),
        name="after",
    )(near(value), near(token))


def far(value):
    return pltpu.with_memory_space_constraint(value, pltpu.HBM)


def near(value):
    return pltpu.with_memory_space_constraint(value, pltpu.VMEM)


def step(gots, keep, joined_out, token, small=None):
    lanes = keep.shape[1]
    half = keep.shape[0] // 4
    extra = 0 if small is None else 2 * small.shape[0]
    sent = [2 * half + extra] if joined_out else [half + extra, half]
    outs = [pltpu.VMEM((2 * half, lanes), F32)]
    outs += [pltpu.VMEM((rows, lanes), BF16) for rows in sent]
    operands = [near(got) for got in gots] + [near(keep)]
    if small is not None:
        outs.append(pltpu.VMEM(small.shape, F32))
        operands.append(near(small))
    out = pl.pallas_call(
        functools.partial(step_kernel, len(gots) == 1, joined_out, small is not None),
        out_shape=outs,
        in_specs=[VMEM] * (len(operands) + 1),
        out_specs=[VMEM] * len(outs),
        compiler_params=params(4),
        cost_estimate=claim(0),
        name="step",
    )(*operands, near(token))
    if small is None:
        return out[0], out[1:], None
    return out[0], out[1:-1], out[-1]


def swap(value, mask):
    count = lax.axis_size("dp") * lax.axis_size("tap")
    return lax.ppermute(value, ("dp", "tap"), [(i, i ^ mask) for i in range(count)])


def cut_kernel(table, weight_hbm, shared, direct, sems):
    slots = shared.shape[0]
    rows = (direct.shape[0] - TABLE_ROWS) // slots
    place = lax.axis_index("dp")
    start = 2 * rows + (place & 7) * shared.shape[1]
    near_start = (place & 1) * rows
    copies = []
    for slot in range(slots):
        pair = (
            (weight_hbm.at[slot, rows_at(start, shared.shape[1]), :], shared.at[slot]),
            (
                weight_hbm.at[slot, rows_at(near_start, rows), :],
                direct.at[slot * rows : (slot + 1) * rows, :],
            ),
        )
        for source, target in pair:
            copies.append(pltpu.make_async_copy(source, target, sems.at[len(copies)]))
    for copy in copies:
        copy.start()
    at = lax.broadcasted_iota(jnp.int32, (TABLE_ROWS, direct.shape[1]), 0)
    taps = jnp.zeros(at.shape, jnp.int32)
    for slot in range(slots):
        taps = jnp.where(at == slot, table[slot], taps)
    direct[slots * rows :, :] = taps.astype(F32).astype(BF16)
    for copy in copies:
        copy.wait()


def cut_pieces(table, conv_weight):
    slots, chan, width = conv_weight.shape
    direct, shared = fetch_plan(chan)
    return pl.pallas_call(
        cut_kernel,
        out_shape=[
            pltpu.VMEM((slots, shared, width), BF16),
            pltpu.VMEM((slots * direct + TABLE_ROWS, width), BF16),
        ],
        in_specs=[SMEM, HBM],
        out_specs=[VMEM] * 2,
        scratch_shapes=[pltpu.SemaphoreType.DMA((2 * slots,))],
        compiler_params=params(4),
        cost_estimate=claim(0),
        name="cut_pieces",
    )(table, far(conv_weight))


def pick_kernel(over_one, over_two, _, low, high, both):
    slots = over_one.shape[0]
    low[...] = over_two[0 : low.shape[0]]
    high[...] = over_one[low.shape[0] :]
    both[0:slots] = over_one[...]
    both[slots:] = over_two[...]


def pair_up_kernel(low, high, both):
    both[0 : low.shape[0]] = low[...]
    both[low.shape[0] :] = high[...]


def vmem_call(kernel, shapes, operands, name):
    return pl.pallas_call(
        kernel,
        out_shape=[pltpu.VMEM(shape, BF16) for shape in shapes],
        in_specs=[VMEM] * len(operands),
        out_specs=[VMEM] * len(shapes),
        compiler_params=params(4),
        cost_estimate=claim(0),
        name=name,
    )(*[near(operand) for operand in operands])


def fetch_pieces(first, direct, token):
    over_one = swap_dp(first, 1)
    over_two = swap_dp(first, 2)
    straight = swap_tap(after(direct, first))
    slots = first.shape[0]
    cut = (slots + 1) // 2
    rest = first.shape[1:]
    shapes = [(count,) + rest for count in (cut, slots - cut, 2 * slots)]
    low, high, both = vmem_call(pick_kernel, shapes, [over_one, over_two, token], "pick")
    (last,) = vmem_call(
        pair_up_kernel, [first.shape], [swap_dp(low, 1), swap_dp(high, 2)], "pair_up"
    )
    straight = after(straight, low)
    both_mate = swap_dp(both, 0)
    return [
        ((0, 0), first),
        ((2, 4), both),
        ((0, None), straight),
        ((6, 0), last),
        ((1, 0), swap_dp(first, 0)),
        ((3, 5), both_mate),
        ((1, None), swap_dp(straight, 0)),
        ((7, 0), swap_dp(last, 0)),
    ]


def fast_shards(
    block_input,
    conv_weight,
    slot_tap_table,
    conv_bias,
    conv_norm_gain,
    conv_norm_bias,
    w_in,
    b_in,
    w_out,
    b_out,
    ffn_norm_gain,
    ffn_norm_bias,
    species_id,
    species_count,
    out_grad,
):
    tap_count = lax.axis_size("tap")
    dp_bits = (lax.axis_size("dp") - 1).bit_length()
    rows_dev = block_input.shape[0] // tap_count
    chan = block_input.shape[1]
    hid = w_in.shape[1]
    windows = rows_dev // WINDOW_LENGTH
    slots = conv_weight.shape[0]
    vmem = pltpu.VMEM
    line = list(range(2, dp_bits))
    orders = (["t", 1] + line, [1, "t"] + line)
    over_x, over_y = 1, 4
    pad_shape = (windows, WINDOW_LENGTH + 2 * PAD, chan)
    rows_f = (rows_dev, chan)
    small_cost = claim(0)

    def row(vector):
        return vector.reshape(1, -1)

    shared, direct = cut_pieces(slot_tap_table, conv_weight)
    weight_shape = conv_weight.shape
    tiles = rows_dev // TILE
    dma = pltpu.SemaphoreType.DMA
    first = swap_tap(shared)
    x_pad, part, token = pl.pallas_call(
        own_conv_kernel,
        out_shape=[vmem(pad_shape, BF16), vmem(rows_f, F32), vmem((8, 128), F32)],
        in_specs=[SMEM] + [HBM] * 2 + [VMEM],
        out_specs=[VMEM] * 3,
        scratch_shapes=[vmem(weight_shape, BF16), dma((windows + slots,))],
        compiler_params=params(8),
        cost_estimate=claim(0),
        name="own_conv",
    )(slot_tap_table, far(block_input), far(conv_weight), near(first))
    pieces = fetch_pieces(first, direct, token)

    block_f = (hid + chan * hid // COLS) >> (dp_bits + 1)
    half_f = block_f << dp_bits
    main = pl.pallas_call(
        functools.partial(main_kernel, orders, dp_bits, [turn for turn, _ in pieces]),
        out_shape=[
            pltpu.HBM(rows_f, BF16),
            vmem(rows_f, F32),
            vmem(rows_f, F32),
            vmem((rows_dev, hid), BF16),
            vmem(conv_weight.shape, BF16),
            vmem((half_f, chan), F32),
            vmem((half_f, chan), BF16),
            vmem((8, chan), F32),
            vmem(rows_f, BF16),
            vmem(w_in.shape, BF16),
            jax.ShapeDtypeStruct((slots,), jnp.int32),
        ],
        in_specs=[SMEM] * 2 + [VMEM] * 2 + [HBM] * 3 + [VMEM] * (7 + len(pieces)),
        out_specs=[HBM] + [VMEM] * 9 + [SMEM],
        scratch_shapes=[
            vmem(w_out.shape, BF16),
            vmem(rows_f, F32),
            vmem(rows_f, BF16),
            vmem((rows_dev, hid), BF16),
            vmem((rows_dev, hid), F32),
            vmem(rows_f, BF16),
            vmem(rows_f, BF16),
            vmem((2, COLS, chan), F32),
            vmem((8, 8, chan), F32),
            dma,
            dma((12,)),
        ],
        compiler_params=params(34),
        cost_estimate=small_cost,
        name="main_rows",
    )(
        species_id,
        species_count,
        near(x_pad),
        near(part),
        far(out_grad),
        far(w_in),
        far(w_out),
        row(conv_bias),
        row(conv_norm_gain),
        row(conv_norm_bias),
        row(b_in),
        row(b_out),
        row(ffn_norm_gain),
        row(ffn_norm_bias),
        *[near(piece) for _, piece in pieces],
    )
    block_output, unit, slope, d_up, other_weight, keep_f, send_f, small_ffn = main[:8]
    grad_in, w_in_near, other_table = main[8:]
    got_f = swap_dp(send_f, 0)

    d_pad, d_hidden, small = pl.pallas_call(
        back_kernel,
        out_shape=[vmem(pad_shape, BF16), vmem(rows_f, F32), vmem((16, chan), F32)],
        in_specs=[SMEM] * 2 + [VMEM] * 7,
        out_specs=[VMEM] * 3,
        scratch_shapes=[vmem((8, 8, chan), F32)],
        compiler_params=params(8),
        cost_estimate=small_cost,
        name="back_rows",
    )(
        species_id,
        species_count,
        near(grad_in),
        near(w_in_near),
        near(d_up),
        near(unit),
        near(slope),
        row(conv_norm_gain),
        near(small_ffn),
    )
    keep_f, sends_f, _ = step([got_f], keep_f, False, small)
    gots_f = [swap(sends_f[0], over_x), swap(sends_f[1], over_y)]

    def terms(group, token, small, name):
        count = len(group) * chan
        extra = 0 if small is None else 2 * small.shape[0]
        outs = [vmem((count, chan), F32), vmem((count + extra, chan), BF16)]
        scratch = [vmem((2, chan, chan), F32)]
        if small is None:
            last, last_spec = far(conv_weight), HBM
            outs.append(vmem(weight_shape, BF16))
            scratch.append(dma((slots,)))
        else:
            last, last_spec = near(small), VMEM
        return pl.pallas_call(
            functools.partial(terms_kernel, group, orders, dp_bits, small is not None),
            out_shape=outs,
            in_specs=[SMEM] * 2 + [VMEM] * 2 + [last_spec, VMEM],
            out_specs=[VMEM] * len(outs),
            scratch_shapes=scratch,
            compiler_params=params(8),
            cost_estimate=small_cost,
            name=name,
        )(slot_tap_table, other_table, near(x_pad), near(d_pad), last, near(token))

    cut = (slots * 3 + 4) // 5
    keep_a, send_a = terms(range(0, cut), sends_f[0], small, "terms_a")
    got_a = swap_dp(send_a, 0)
    keep_b, send_b, own_weight = terms(range(cut, slots), keep_a, None, "terms_b")
    got_b = swap_dp(send_b, 0)
    def spaced(token, claimed=1):
        return after(mark, token, claimed)

    def turned(sends):
        return [swap(sends[0], over_y), swap(sends[1], over_x)]

    def along(sends, stage):
        return [swap(sends[0], 2 << line[stage])]

    mark = token
    keep_f, sends_f, _ = step(gots_f, keep_f, False, keep_b)
    gots_f = turned(sends_f)
    keep_a, sends_a, small = step([got_a], keep_a, False, spaced(keep_f, 100), small)
    gots_a = [swap(sends_a[0], over_x), swap(sends_a[1], over_y)]
    partial = pl.pallas_call(
        input_near_kernel,
        out_shape=vmem(rows_f, F32),
        in_specs=[SMEM] + [VMEM] * 4,
        out_specs=VMEM,
        compiler_params=params(8),
        cost_estimate=claim(0),
        name="input_near",
    )(slot_tap_table, near(d_pad), near(d_hidden), near(own_weight), near(keep_a))
    input_grad, mark = pl.pallas_call(
        input_far_kernel,
        out_shape=[pltpu.HBM(rows_f, F32), vmem((8, 128), F32)],
        in_specs=[SMEM] + [VMEM] * 4,
        out_specs=[HBM, VMEM],
        scratch_shapes=[vmem(rows_f, F32), pltpu.SemaphoreType.DMA((rows_dev // TILE,))],
        compiler_params=params(8),
        cost_estimate=small_cost,
        name="input_far",
    )(other_table, near(d_pad), near(partial), near(other_weight), near(keep_a))
    mark = spaced(mark)
    keep_f, sends_f, _ = step(gots_f, keep_f, True, mark)
    got_f = along(sends_f, 0)
    keep_b, sends_b, _ = step([got_b], keep_b, False, keep_f)
    gots_b = [swap(sends_b[0], over_x), swap(sends_b[1], over_y)]
    mark = spaced(keep_b)
    keep_a, sends_a, small = step(gots_a, keep_a, False, mark, small)
    gots_a = turned(sends_a)
    mark = spaced(keep_a)
    for stage in range(1, len(line)):
        keep_f, sends_f, _ = step(got_f, keep_f, True, mark)
        got_f = along(sends_f, stage)
        mark = spaced(keep_f)
    keep_b, sends_b, _ = step(gots_b, keep_b, False, mark)
    gots_b = turned(sends_b)
    mark = spaced(keep_b)
    keep_a, sends_a, small = step(gots_a, keep_a, True, mark, small)
    got_a = along(sends_a, 0)
    mark = spaced(keep_a)
    w_in_mine, w_out_mine = pl.pallas_call(
        functools.partial(last_ffn_kernel, 1),
        out_shape=[
            jax.ShapeDtypeStruct((chan >> (dp_bits + 1), hid), F32),
            jax.ShapeDtypeStruct((hid >> (dp_bits + 1), chan), F32),
        ],
        in_specs=[VMEM] * 3,
        out_specs=[VMEM] * 2,
        compiler_params=params(4),
        cost_estimate=claim(0),
        name="last_ffn",
    )(near(got_f[0]), near(keep_f), near(mark))
    keep_b, sends_b, _ = step(gots_b, keep_b, True, mark)
    got_b = along(sends_b, 0)
    mark = spaced(keep_b)
    for stage in range(1, len(line)):
        keep_a, sends_a, small = step(got_a, keep_a, True, mark, small)
        got_a = along(sends_a, stage)
        mark = spaced(keep_a)
        keep_b, sends_b, _ = step(got_b, keep_b, True, mark)
        got_b = along(sends_b, stage)
        mark = spaced(keep_b)
    part_a, small = pl.pallas_call(
        last_small_kernel,
        out_shape=[vmem(keep_a.shape, F32), vmem(small.shape, F32)],
        in_specs=[VMEM] * 4,
        out_specs=[VMEM] * 2,
        compiler_params=params(4),
        cost_estimate=claim(0),
        name="last_a",
    )(near(got_a[0]), near(keep_a), near(small), near(mark))
    conv_weight_grad = pl.pallas_call(
        last_conv_kernel,
        out_shape=jax.ShapeDtypeStruct((slots, chan >> dp_bits, chan), F32),
        in_specs=[VMEM] * 3,
        out_specs=VMEM,
        compiler_params=params(4),
        cost_estimate=claim(0),
        name="last_conv",
    )(near(got_b[0]), near(keep_b), near(part_a))
    chunks = hid // COLS

    owner = lax.axis_index("dp") * tap_count + lax.axis_index("tap")
    width = chan >> (dp_bits + 1)
    lanes = lax.dynamic_slice(small, (0, owner * width), (small.shape[0], width))
    wide = hid >> (dp_bits + 1)
    d_b_in = lax.dynamic_slice(small[3 : 3 + chunks].reshape(-1), (owner * wide,), (wide,))
    return (
        block_output,
        input_grad,
        conv_weight_grad,
        lanes[8],
        lanes[9],
        lanes[10],
        w_in_mine,
        d_b_in,
        w_out_mine,
        lanes[0],
        lanes[1],
        lanes[2],
    )


def narrow_enough(mesh):
    return mesh.shape["tap"] == 2 and mesh.shape["dp"] == 16


def solution(mesh):
    chosen = fast_shards if narrow_enough(mesh) else plain_shards
    return jax.shard_map(
        chosen,
        mesh=mesh,
        in_specs=(
            P("dp", None),
            P("tap", None, None),
            P("tap"),
            P(),
            P(),
            P(),
            P(),
            P(),
            P(),
            P(),
            P(),
            P(),
            P("dp"),
            P(),
            P(("dp", "tap"), None),
        ),
        out_specs=(
            P(("dp", "tap"), None),
            P(("dp", "tap"), None),
            P("tap", "dp", None),
            P(("dp", "tap")),
            P(("dp", "tap")),
            P(("dp", "tap")),
            P(("dp", "tap"), None),
            P(("dp", "tap")),
            P(("dp", "tap"), None),
            P(("dp", "tap")),
            P(("dp", "tap")),
            P(("dp", "tap")),
        ),
        check_vma=False,
    )
```

```python
import functools

import jax
import jax.numpy as jnp
from jax import lax
from jax.experimental import pallas as pl
from jax.experimental.pallas import tpu as pltpu
from jax.sharding import PartitionSpec as P

KERNEL_TAPS = 9
DILATION_STEP = 16
WINDOW_LENGTH = 512


def layer_norm(values):
    mean_val = jnp.mean(values, axis=-1, keepdims=True)
    center = values - mean_val
    spread = jnp.mean(center * center, axis=-1, keepdims=True)
    return center * lax.rsqrt(spread + 1e-05)


def exact_gelu(values):
    return jax.nn.gelu(values, approximate=False)


def conv_branch(pre_conv, gain_one, bias_one):
    return layer_norm(exact_gelu(pre_conv)) * gain_one + bias_one


def ffn_branch(pre_out, gain_two, bias_two):
    return layer_norm(pre_out) * gain_two + bias_two


def shift_stack(win_rows, tap_table, forward):
    tap_extent = KERNEL_TAPS // 2 * DILATION_STEP
    padded_input = jnp.pad(win_rows, ((0, 0), (tap_extent, tap_extent), (0, 0)))
    pieces = []
    for index_of_slot in range(tap_table.shape[0]):
        if forward:
            tap_offset = tap_table[index_of_slot]
        else:
            tap_offset = KERNEL_TAPS - 1 - tap_table[index_of_slot]
        shifted_input = lax.dynamic_slice_in_dim(
            padded_input, tap_offset * DILATION_STEP, WINDOW_LENGTH, 1
        )
        pieces.append(shifted_input.reshape(-1, win_rows.shape[2]))
    return jnp.stack(pieces)


def contract_rows(left, right):
    return lax.dot_general(
        left, right, (((0,), (0,)), ((), ())), preferred_element_type=jnp.float32
    )


def contract_cols(left, right):
    return lax.dot_general(
        left, right, (((1,), (1,)), ((), ())), preferred_element_type=jnp.float32
    )


def swap_dp(value, bit):
    count = lax.axis_size("dp")
    return lax.ppermute(value, "dp", [(i, i ^ (1 << bit)) for i in range(count)])


def swap_tap(value):
    return lax.ppermute(value, "tap", [(0, 1), (1, 0)])


def halve(part, order, kind):
    dp_bits = (lax.axis_size("dp") - 1).bit_length()
    place = lax.axis_index("dp")
    tap = lax.axis_index("tap")
    labels = ["t"] + list(range(dp_bits - 1, -1, -1))
    for step in order:
        axis = labels.index(step)
        labels.pop(axis)
        mine = tap if step == "t" else (place >> step) & 1
        keep = lax.dynamic_index_in_dim(part, mine, axis, keepdims=False)
        send = lax.dynamic_index_in_dim(part, 1 - mine, axis, keepdims=False).astype(kind)
        got = swap_tap(send) if step == "t" else swap_dp(send, step)
        part = keep + got.astype(jnp.float32)
    return part


def orders(dp_bits):
    rest = list(range(2, dp_bits))
    first = [0, "t", 1] + rest
    second = [0, 1] + rest[:1] + ["t"] + rest[1:]
    third = [0] + rest[:1] + ["t", 1] + rest[1:]
    return first, second, third


def plain_shards(
    block_input,
    conv_weight,
    slot_tap_table,
    conv_bias,
    conv_norm_gain,
    conv_norm_bias,
    w_in,
    b_in,
    w_out,
    b_out,
    ffn_norm_gain,
    ffn_norm_bias,
    species_id,
    species_count,
    out_grad,
):
    tap_count = lax.axis_size("tap")
    my_index = lax.axis_index("tap")
    core = lax.axis_index("dp") & 1
    dp_bits = (lax.axis_size("dp") - 1).bit_length()
    tok_dev, chan_width = block_input.shape
    hid_width = w_in.shape[1]
    half_rows = tok_dev // tap_count
    windows = tok_dev // WINDOW_LENGTH
    my_windows = windows // tap_count
    own_slots = conv_weight.shape[0]
    half_chan = chan_width // 2
    first, second, third = orders(dp_bits)

    other_table = swap_tap(slot_tap_table)
    part_send = lax.dynamic_slice_in_dim(conv_weight, core * half_chan, half_chan, 1)
    part_here = swap_tap(part_send)
    part_mate = swap_dp(part_here, 0)
    low_part = jnp.where(core == 0, part_here, part_mate)
    high_part = jnp.where(core == 0, part_mate, part_here)
    other_weight = jnp.concatenate([low_part, high_part], axis=1)

    my_x = lax.dynamic_slice_in_dim(block_input, my_index * half_rows, half_rows, 0)
    x_windows = my_x.reshape(my_windows, WINDOW_LENGTH, chan_width)
    mine_x = my_x.astype(jnp.float32)
    own_stack = shift_stack(x_windows, slot_tap_table, True)
    other_stack = shift_stack(x_windows, other_table, True)
    conv_out = jnp.einsum("str,sro->to", own_stack, conv_weight, preferred_element_type=jnp.float32)
    conv_out = conv_out + jnp.einsum(
        "str,sro->to", other_stack, other_weight, preferred_element_type=jnp.float32
    )
    pre_conv = conv_out + conv_bias
    norm_one, conv_back = jax.vjp(conv_branch, pre_conv, conv_norm_gain, conv_norm_bias)
    hidden = mine_x + norm_one
    hidden_low = hidden.astype(jnp.bfloat16)
    pre_up = jnp.dot(hidden_low, w_in, preferred_element_type=jnp.float32) + b_in
    activ, activ_back = jax.vjp(exact_gelu, pre_up)
    act_low = activ.astype(jnp.bfloat16)
    pre_out = jnp.dot(act_low, w_out, preferred_element_type=jnp.float32) + b_out
    norm_two, ffn_back = jax.vjp(ffn_branch, pre_out, ffn_norm_gain, ffn_norm_bias)
    block_output = (hidden + norm_two).astype(jnp.bfloat16)
    my_species = lax.dynamic_slice_in_dim(species_id, my_index * my_windows, my_windows, 0)
    species_range = jnp.arange(species_count.shape[0], dtype=jnp.int32)
    matches = my_species[:, None] == species_range[None, :]
    window_count = jnp.sum(jnp.where(matches, species_count[None, :], 0), axis=1)
    window_scale = 4.0 / window_count.astype(jnp.float32)
    grad_y = (
        out_grad.astype(jnp.float32).reshape(my_windows, WINDOW_LENGTH, chan_width)
        * window_scale[:, None, None]
    ).reshape(half_rows, chan_width)
    d_pre_out, d_gain_two, d_bias_two = ffn_back(grad_y)
    d_out_low = d_pre_out.astype(jnp.bfloat16)
    d_w_out = contract_rows(act_low, d_out_low)
    d_b_out = jnp.sum(d_out_low.astype(jnp.float32), axis=0)
    d_activ = contract_cols(d_out_low, w_out)
    (d_pre_up,) = activ_back(d_activ)
    d_up_low = d_pre_up.astype(jnp.bfloat16)
    d_w_in = contract_rows(hidden_low, d_up_low)
    d_b_in = jnp.sum(d_up_low.astype(jnp.float32), axis=0)
    d_hidden = grad_y + contract_cols(d_up_low, w_in)
    d_pre_conv, d_gain_one, d_bias_one = conv_back(d_hidden)
    d_conv_low = d_pre_conv.astype(jnp.bfloat16)
    d_conv_bias = jnp.sum(d_conv_low.astype(jnp.float32), axis=0)
    d_windows = d_conv_low.reshape(my_windows, WINDOW_LENGTH, chan_width)
    own_back = shift_stack(d_windows, slot_tap_table, False)
    other_back = shift_stack(d_windows, other_table, False)
    input_grad = (
        d_hidden
        + jnp.einsum("sto,sro->tr", own_back, conv_weight, preferred_element_type=jnp.float32)
        + jnp.einsum("sto,sro->tr", other_back, other_weight, preferred_element_type=jnp.float32)
    )
    own_terms = jnp.einsum("str,to->sro", own_stack, d_conv_low, preferred_element_type=jnp.float32)
    other_terms = jnp.einsum(
        "str,to->sro", other_stack, d_conv_low, preferred_element_type=jnp.float32
    )
    bits = [2] * dp_bits

    def by_tap(own, other):
        return jnp.where(my_index == 0, jnp.stack([own, other]), jnp.stack([other, own]))

    def conv_part(begin, end, order):
        own = own_terms[begin:end]
        other = other_terms[begin:end]
        both = by_tap(own, other)
        rows = chan_width >> dp_bits
        both = both.reshape([2, end - begin] + bits + [rows, chan_width])
        return halve(jnp.moveaxis(both, 1, 1 + dp_bits), order, jnp.bfloat16)

    cut = own_slots * 2 // 5
    conv_weight_grad = jnp.concatenate(
        [
            conv_part(0, cut, first),
            conv_part(cut, 2 * cut, second),
            conv_part(2 * cut, own_slots, third),
        ]
    )

    def spread(total, order, kind):
        rows = total.shape[0] >> (dp_bits + 1)
        split = total.reshape(bits + [2, rows] + list(total.shape[1:]))
        return halve(jnp.moveaxis(split, dp_bits, 0), order, kind)

    d_w_out_mine = spread(d_w_out, first, jnp.bfloat16)
    d_w_in_mine = spread(d_w_in, second, jnp.bfloat16)
    owners = 2 << dp_bits
    small = [d_b_in, d_b_out, d_conv_bias, d_gain_one, d_bias_one, d_gain_two, d_bias_two]
    joined = jnp.concatenate([v.reshape(owners, -1) for v in small], axis=1)
    joined_mine = spread(joined, third, jnp.float32).reshape(-1)
    vectors = []
    start = 0
    for v in small:
        size = v.shape[0] // owners
        vectors.append(joined_mine[start : start + size])
        start += size
    return (
        block_output,
        input_grad,
        conv_weight_grad,
        vectors[2],
        vectors[3],
        vectors[4],
        d_w_in_mine,
        vectors[0],
        d_w_out_mine,
        vectors[1],
        vectors[5],
        vectors[6],
    )


TILE = 512
COLS = 512
PAD = KERNEL_TAPS // 2 * DILATION_STEP
MIB = 2**20
TABLE_ROWS = 16
F32 = jnp.float32
BF16 = jnp.bfloat16
HBM = pl.BlockSpec(memory_space=pltpu.HBM)
VMEM = pl.BlockSpec(memory_space=pltpu.VMEM)
SMEM = pl.BlockSpec(memory_space=pltpu.SMEM)


def dot_plain(left, right):
    return lax.dot_general(left, right, (((1,), (0,)), ((), ())), preferred_element_type=F32)


def gelu_and_slope(value):
    cdf = 0.5 + 0.5 * lax.erf(value * 0.7071067811865476)
    density = jnp.exp2(value * value * -0.7213475204444817)
    return value * cdf, cdf + (value * 0.3989422804014327) * density


def norm_parts(value):
    center = value - jnp.mean(value, axis=-1, keepdims=True)
    spread = jnp.mean(center * center, axis=-1, keepdims=True)
    scale = lax.rsqrt(spread + 1e-05)
    return center * scale, scale


def norm_back(grad, unit):
    return grad - jnp.mean(grad, axis=-1, keepdims=True) - unit * jnp.mean(
        grad * unit, axis=-1, keepdims=True
    )


def fold_rows(value):
    return jnp.sum(value.reshape(value.shape[0] // 8, 8, value.shape[1]), axis=0)


def one_row(value):
    return jnp.sum(value, axis=0, keepdims=True)


def my_bits(dp_bits):
    place = lax.axis_index("dp")
    mine = {bit: (place >> bit) & 1 for bit in range(dp_bits)}
    mine["t"] = lax.axis_index("tap")
    return mine


def relative(order, owner, mine):
    spot = 0
    for label in order:
        spot = spot * 2 + (owner[label] ^ mine[label])
    return spot


def rows_at(start, size):
    return pl.ds(pl.multiple_of(start, 16), size)


def split_copy(source, target, sems, first):
    rows = target.shape[0] // 4
    return [
        pltpu.make_async_copy(
            source.at[at * rows : (at + 1) * rows, :],
            target.at[at * rows : (at + 1) * rows, :],
            sems.at[first + at],
        )
        for at in range(4)
    ]


def wait_all(copies):
    for copy in copies:
        copy.wait()


def clear_pads(pad_ref):
    zeros = jnp.zeros((PAD, pad_ref.shape[2]), pad_ref.dtype)
    for win in range(pad_ref.shape[0]):
        pad_ref[win, 0:PAD, :] = zeros
        pad_ref[win, PAD + WINDOW_LENGTH :, :] = zeros


def each_tile(rows, body, together=1):
    per = WINDOW_LENGTH // TILE

    @pl.loop(0, rows // TILE // together)
    def _(step):
        for member in range(together):
            number = step * together + member
            body(rows_at(number * TILE, TILE), number // per, (number % per) * TILE)


def window_weight(species, counts, win, windows, lanes):
    kind = species[lax.axis_index("tap") * windows + win]
    count = jnp.full((8, lanes), counts[kind], jnp.int32).astype(F32)
    return (4.0 / count)[0:1, :]


def load_kernel(
    table, x_hbm, weight_hbm, w_in_hbm, x_pad, weight, w_in, straight, sems
):
    windows = x_pad.shape[0]
    slots = weight.shape[0]
    rows = weight.shape[1] // 8
    base = lax.axis_index("tap") * windows * WINDOW_LENGTH
    start = ((lax.axis_index("dp") & 7) ^ 6) * rows
    copies = []
    for slot in range(slots):
        source = weight_hbm.at[slot, rows_at(start, rows), :]
        copies.append((source, straight.at[slot * rows : (slot + 1) * rows, :]))
    for win in range(windows):
        source = x_hbm.at[rows_at(base + win * WINDOW_LENGTH, WINDOW_LENGTH), :]
        copies.append((source, x_pad.at[win, PAD : PAD + WINDOW_LENGTH, :]))
    copies += [(weight_hbm.at[slot], weight.at[slot]) for slot in range(slots)]
    copies = [
        pltpu.make_async_copy(source, target, sems.at[at])
        for at, (source, target) in enumerate(copies)
    ]
    copies += split_copy(w_in_hbm, w_in, sems, len(copies))
    for copy in copies:
        copy.start()
    at = lax.broadcasted_iota(jnp.int32, (TABLE_ROWS, straight.shape[1]), 0)
    taps = jnp.zeros(at.shape, jnp.int32)
    for slot in range(slots):
        taps = jnp.where(at == slot, table[slot], taps)
    straight[slots * rows :, :] = taps.astype(F32).astype(BF16)
    clear_pads(x_pad)
    wait_all(copies)


def own_conv_kernel(table, x_pad, weight, _, part, token):
    token[...] = jnp.zeros(token.shape, token.dtype)

    def convolve(rows, win, begin):
        total = None
        for slot in range(weight.shape[0]):
            shifted = rows_at(table[slot] * DILATION_STEP + begin, TILE)
            term = dot_plain(x_pad[win, shifted, :], weight[slot])
            total = term if total is None else total + term
        part[rows, :] = total

    each_tile(part.shape[0], convolve, 2)


def join_pieces(plan, pieces, weight):
    slots = weight.shape[0]
    rows = weight.shape[1] // 8
    place = lax.axis_index("dp") & 7
    for turns, piece in zip(plan, pieces):
        flat = len(piece.shape) == 2
        for number, turn in enumerate(turns):
            there = rows_at((place ^ turn) * rows, rows)
            if flat:
                for slot in range(slots):
                    weight[slot, there, :] = piece[slot * rows : (slot + 1) * rows, :]
            else:
                weight[:, there, :] = piece[number * slots : (number + 1) * slots]


def main_kernel(orders, dp_bits, turns, *refs):
    species, counts = refs[:2]
    x_pad, part, grad_hbm, w_in, w_out_hbm = refs[2:7]
    conv_bias, gain_one, bias_one, b_in, b_out, gain_two, bias_two = refs[7:14]
    pieces = refs[14 : 14 + len(turns)]
    y_hbm, unit, slope, d_up, weight, keep, send, small, grad_in, table = refs[
        14 + len(turns) : 24 + len(turns)
    ]
    w_out, hidden, low, act, hid_slope, d_out, y_low, result, sums, sem, sems = refs[24 + len(turns) :]
    told = pieces[turns.index((6,))]
    told_at = told.shape[0] - TABLE_ROWS
    taps = []
    for slot in range(weight.shape[0]):
        line = told[told_at : told_at + TABLE_ROWS, 0:128].astype(F32)
        chosen = lax.broadcasted_iota(jnp.int32, line.shape, 0) == slot
        taps.append(jnp.max(jnp.where(chosen, line, 0.0)).astype(jnp.int32))
        table[slot] = taps[slot]
    mine = my_bits(dp_bits)
    rows_dev, chan = hidden.shape
    hid_width = w_in.shape[1]
    windows = x_pad.shape[0]
    out_copies = split_copy(w_out_hbm, w_out, sems, 4)
    grad_copies = split_copy(grad_hbm, grad_in, sems, 8)
    for copy in out_copies + grad_copies:
        copy.start()
    join_pieces(turns, pieces, weight)
    sums[...] = jnp.zeros(sums.shape, F32)

    def first_norm(rows, win, begin):
        total = part[rows, :] + conv_bias[...]
        for slot in range(weight.shape[0]):
            shifted = rows_at(taps[slot] * DILATION_STEP + begin, TILE)
            total = total + dot_plain(x_pad[win, shifted, :], weight[slot])
        value, steep = gelu_and_slope(total)
        normed, scale = norm_parts(value)
        unit[rows, :] = normed
        slope[rows, :] = scale * steep
        here = x_pad[win, rows_at(PAD + begin, TILE), :].astype(F32)
        summed = here + (normed * gain_one[...] + bias_one[...])
        hidden[rows, :] = summed
        low[rows, :] = summed.astype(BF16)

    each_tile(rows_dev, first_norm, 2)

    def go_up(rows, win, begin):
        for at in range(0, hid_width, COLS):
            cols = slice(at, at + COLS)
            up = dot_plain(low[rows, :], w_in[:, cols]) + b_in[:, cols]
            value, steep = gelu_and_slope(up)
            act[rows, cols] = value.astype(BF16)
            hid_slope[rows, cols] = steep

    each_tile(rows_dev, go_up, 2)
    wait_all(out_copies + grad_copies)

    def second_norm(rows, win, begin):
        pre_out = dot_plain(act[rows, :], w_out[...]) + b_out[...]
        normed, scale = norm_parts(pre_out)
        result_rows = hidden[rows, :] + (normed * gain_two[...] + bias_two[...])
        y_low[rows, :] = result_rows.astype(BF16)
        grad_y = grad_in[rows, :].astype(F32) * window_weight(species, counts, win, windows, chan)
        back = (norm_back(grad_y * gain_two[...], normed) * scale).astype(BF16)
        d_out[rows, :] = back
        sums[0] += fold_rows(back.astype(F32))
        sums[1] += fold_rows(grad_y * normed)
        sums[2] += fold_rows(grad_y)

    each_tile(rows_dev, second_norm, 2)
    y_copy = pltpu.make_async_copy(y_low, y_hbm, sem)
    y_copy.start()

    def go_down(rows, win, begin):
        for number, at in enumerate(range(0, hid_width, COLS)):
            cols = slice(at, at + COLS)
            d_act = contract_cols(d_out[rows, :], w_out[cols, :])
            back = (d_act * hid_slope[rows, cols]).astype(BF16)
            d_up[rows, cols] = back
            sums[3 + number] += fold_rows(back.astype(F32))

    each_tile(rows_dev, go_down, 2)
    for number in range(8):
        small[number : number + 1, :] = one_row(sums[number])
    core = mine[0]
    out_block = hid_width >> (dp_bits + 1)
    in_block = chan >> (dp_bits + 1)
    chunks = hid_width // COLS
    half = (out_block + chunks * in_block) // 2

    def hand_out(spot, first_row, block, targets):
        for start in range(0, result.shape[1], 4 * block):
            owner_at = first_row // block + start // block
            for tap in range(2):
                owner = {bit: (owner_at >> (bit + 1)) & 1 for bit in range(1, dp_bits)}
                owner["t"] = tap
                inner = start + tap * block
                for part_at, source, size, shift in targets:
                    spread = relative(orders[part_at], owner, mine) + (part_at << dp_bits)
                    place = rows_at(spread * half + shift, size)
                    mine_at = rows_at(inner + source + core * 2 * block, size)
                    other_at = rows_at(inner + source + (1 - core) * 2 * block, size)
                    keep[place, :] = result[spot, mine_at, :]
                    send[place, :] = result[spot, other_at, :].astype(BF16)

    size = out_block // 2

    @pl.loop(0, chunks // 2)
    def _(pair):
        for spot in range(2):
            at = pl.multiple_of((pair * 2 + spot) * COLS, COLS)
            result[spot] = contract_rows(act[:, pl.ds(at, COLS)], d_out[...])
            hand_out(spot, at, out_block, [(0, 0, size, 0), (1, size, size, 0)])

    @pl.loop(0, chunks // 2)
    def _(step):
        shift = size + step * in_block
        for spot in range(2):
            at = pl.multiple_of((spot * (chunks // 2) + step) * COLS, COLS)
            result[spot] = contract_rows(low[...], d_up[:, pl.ds(at, COLS)])
            hand_out(spot, 0, in_block, [(spot, 0, in_block, shift)])

    y_copy.wait()


def back_kernel(
    species,
    counts,
    grad_in,
    w_in,
    d_up,
    unit,
    slope,
    gain_one,
    small_in,
    d_pad,
    d_hidden,
    small,
    sums,
):
    windows = d_pad.shape[0]
    chan = d_hidden.shape[1]
    clear_pads(d_pad)
    sums[...] = jnp.zeros(sums.shape, F32)

    def through_norm(rows, win, begin):
        grad = grad_in[rows, :].astype(F32) * window_weight(species, counts, win, windows, chan)
        grad = grad + contract_cols(d_up[rows, :], w_in[...])
        d_hidden[rows, :] = grad
        normed = unit[rows, :]
        back = (norm_back(grad * gain_one[...], normed) * slope[rows, :]).astype(BF16)
        d_pad[win, rows_at(PAD + begin, TILE), :] = back
        sums[0] += fold_rows(back.astype(F32))
        sums[1] += fold_rows(grad * normed)
        sums[2] += fold_rows(grad)

    each_tile(d_hidden.shape[0], through_norm, 2)
    small[0:8, :] = small_in[...]
    for number in range(8):
        small[8 + number : 9 + number, :] = one_row(sums[number])


def store_small(total, ref, first):
    count = total.shape[0]
    high = total.astype(BF16)
    ref[first : first + count, :] = high
    ref[first + count : first + 2 * count, :] = (total - high.astype(F32)).astype(BF16)


def load_small(ref, first, count):
    high = ref[first : first + count, :].astype(F32)
    return high + ref[first + count : first + 2 * count, :].astype(F32)


def terms_kernel(slots, orders, dp_bits, with_small, own_table, other_table, x_pad, d_pad, *refs):
    if with_small:
        small, _, keep, send, result = refs
        store_small(small[...], send, keep.shape[0])
    else:
        _, keep, send, result = refs
    mine = my_bits(dp_bits)
    rows = x_pad.shape[2] >> dp_bits
    core = mine[0]
    tables = (own_table, other_table)
    size = rows // 2

    @pl.loop(0, len(slots))
    def _(number):
        for near_tap in range(2):
            tap = tables[near_tap][slots[0] + number]
            shifted = rows_at((KERNEL_TAPS - 1 - tap) * DILATION_STEP, WINDOW_LENGTH)
            total = None
            for win in range(x_pad.shape[0]):
                term = contract_rows(
                    x_pad[win, PAD : PAD + WINDOW_LENGTH, :], d_pad[win, shifted, :]
                )
                total = term if total is None else total + term
            result[near_tap] = total
            for start in range(0, x_pad.shape[2], 2 * rows):
                owner_at = start // rows
                owner = {bit: (owner_at >> bit) & 1 for bit in range(1, dp_bits)}
                owner["t"] = mine["t"] ^ near_tap
                for part_at in range(2):
                    spread = relative(orders[part_at], owner, mine) + (part_at << dp_bits)
                    place = rows_at((spread * len(slots) + number) * size, size)
                    mine_at = rows_at(start + core * rows + part_at * size, size)
                    other_at = rows_at(start + (1 - core) * rows + part_at * size, size)
                    keep[place, :] = result[near_tap, mine_at, :]
                    send[place, :] = result[near_tap, other_at, :].astype(BF16)


def input_sum(table, d_pad, base, weight, rows, win, begin):
    total = base[rows, :]
    for slot in range(weight.shape[0]):
        shifted = rows_at((KERNEL_TAPS - 1 - table[slot]) * DILATION_STEP + begin, TILE)
        total = total + contract_cols(d_pad[win, shifted, :], weight[slot])
    return total


def input_near_kernel(table, d_pad, base, weight, _, out):
    def gather(rows, win, begin):
        out[rows, :] = input_sum(table, d_pad, base, weight, rows, win, begin)

    each_tile(out.shape[0], gather, 2)


def input_far_kernel(table, d_pad, base, weight, _, out_hbm, token, out, sems):
    token[...] = jnp.zeros(token.shape, token.dtype)

    def copy_of(rows):
        return pltpu.make_async_copy(out.at[rows, :], out_hbm.at[rows, :], sems.at[0])

    def gather(rows, win, begin):
        out[rows, :] = input_sum(table, d_pad, base, weight, rows, win, begin)
        copy_of(rows).start()

    each_tile(out.shape[0], gather, 2)
    pltpu.make_async_copy(out, out_hbm, sems.at[0]).wait()


def fused_kernel(got_count, plans, *refs):
    gots = refs[:got_count]
    at = got_count
    inputs = []
    for plan in plans:
        inputs.append(refs[at : at + 1 + plan["with_small"]])
        at += 1 + plan["with_small"]
    at += 1
    kept = []
    for plan in plans:
        kept.append(refs[at : at + 1 + plan["with_small"]])
        at += 1 + plan["with_small"]
    sent = refs[at:]
    for plan, source, target in zip(plans, inputs, kept):
        keep = source[0]
        rows = keep.shape[0] // 2
        half = rows // 2
        for part in range(2):
            which, base = plan["ins"][part]
            out, spot = plan["outs"][part]
            start = part * rows
            theirs = gots[which][base + half : base + rows, :].astype(F32)
            total = keep[start + half : start + rows, :] + theirs
            sent[out][spot : spot + half, :] = total.astype(BF16)
            ours = gots[which][base : base + half, :].astype(F32)
            target[0][part * half : (part + 1) * half, :] = keep[start : start + half, :] + ours
        if plan["with_small"]:
            which, base = plan["small_in"]
            count = source[1].shape[0]
            total = source[1][...] + load_small(gots[which], base, count)
            target[1][...] = total
            out, spot = plan["small_out"]
            store_small(total, sent[out], spot)


def sum_of(gots, keep, rows):
    total = keep[rows, :]
    for got in gots:
        total = total + got[rows, :].astype(F32)
    return total


def last_ffn_kernel(members, *refs):
    gots = refs[:members]
    keep, _, w_in_out, w_out_out, token = refs[members:]
    token[...] = jnp.zeros(token.shape, token.dtype)
    out_rows, chan = w_out_out.shape
    in_rows = w_in_out.shape[0]
    half = keep.shape[0] // 2
    steps = w_in_out.shape[1] // chan // 2
    for part in range(2):
        base = part * half
        size = out_rows // 2
        w_out_out[part * size : (part + 1) * size, :] = sum_of(gots, keep, slice(base, base + size))
        for step in range(steps):
            at = base + size + step * in_rows
            cols = slice((part * steps + step) * chan, (part * steps + step + 1) * chan)
            w_in_out[:, cols] = sum_of(gots, keep, slice(at, at + in_rows))


def last_conv_kernel(
    got,
    keep_a,
    small,
    keep_b,
    out,
    total,
    conv_bias,
    gain_one,
    bias_one,
    b_out,
    gain_two,
    bias_two,
    b_in,
):
    size = out.shape[1] // 2
    first = keep_a.shape[0] // out.shape[1]
    rest = out.shape[0] - first
    shift = keep_a.shape[0]
    for slot in range(out.shape[0]):
        for part in range(2):
            if slot < first:
                at = (part * first + slot) * size
                kept, base = keep_a, 0
            else:
                at = (part * rest + slot - first) * size
                kept, base = keep_b, shift
            theirs = got[base + at : base + at + size, :].astype(F32)
            out[slot, part * size : (part + 1) * size, :] = kept[at : at + size, :] + theirs
    total[...] = small[...] + load_small(got, shift + keep_b.shape[0], small.shape[0])
    lanes = small.shape[1]
    owner = lax.axis_index("dp") * lax.axis_size("tap") + lax.axis_index("tap")
    width = b_out.shape[1]
    turned = pltpu.roll(total[...], (lanes - owner * width) % lanes, 1)
    for at, target in (
        (0, b_out),
        (1, gain_two),
        (2, bias_two),
        (8, conv_bias),
        (9, gain_one),
        (10, bias_one),
    ):
        target[...] = turned[at : at + 1, 0:width]
    width = b_in.shape[1]
    start = owner * width
    line = total[pl.ds(3 + start // lanes, 1), :]
    line = pltpu.roll(jnp.broadcast_to(line, (8, lanes)), (lanes - start % lanes) % lanes, 1)
    b_in[...] = line[0:1, 0:width]


def params(mib):
    return pltpu.CompilerParams(vmem_limit_bytes=mib * MIB)


def claim(micros):
    return pl.CostEstimate(flops=int(micros * 1.1e9), bytes_accessed=1, transcendentals=0)


def after_kernel(_, token, out):
    del token, out


def after(value, token, claimed=0):
    return pl.pallas_call(
        after_kernel,
        out_shape=pltpu.VMEM(value.shape, value.dtype),
        in_specs=[VMEM] * 2,
        out_specs=VMEM,
        input_output_aliases={0: 0},
        compiler_params=params(4),
        cost_estimate=claim(claimed),
        name="after",
    )(near(value), near(token))


def far(value):
    return pltpu.with_memory_space_constraint(value, pltpu.HBM)


def near(value):
    return pltpu.with_memory_space_constraint(value, pltpu.VMEM)


def fused_step(gots, flows, plans, sizes, token):
    lanes = flows[0]["keep"].shape[1]
    operands = [near(got) for got in gots]
    outs = []
    for flow, plan in zip(flows, plans):
        plan["with_small"] = "small_in" in plan
        operands.append(near(flow["keep"]))
        outs.append(pltpu.VMEM((flow["keep"].shape[0] // 2, lanes), F32))
        if plan["with_small"]:
            operands.append(near(flow["small"]))
            outs.append(pltpu.VMEM(flow["small"].shape, F32))
    operands.append(near(token))
    kept = len(outs)
    outs += [pltpu.VMEM((rows, lanes), BF16) for rows in sizes]
    out = pl.pallas_call(
        functools.partial(fused_kernel, len(gots), plans),
        out_shape=outs,
        in_specs=[VMEM] * len(operands),
        out_specs=[VMEM] * len(outs),
        compiler_params=params(4),
        cost_estimate=claim(0),
        name="step",
    )(*operands)
    at = 0
    for flow, plan in zip(flows, plans):
        flow["keep"] = out[at]
        at += 1
        if plan["with_small"]:
            flow["small"] = out[at]
            at += 1
    return out[kept:]


def swap(value, mask):
    count = lax.axis_size("dp") * lax.axis_size("tap")
    return lax.ppermute(value, ("dp", "tap"), [(i, i ^ mask) for i in range(count)])


def cut_kernel(weight_hbm, piece, sems):
    rows = piece.shape[1]
    start = (lax.axis_index("dp") & 7) * rows
    copies = [
        pltpu.make_async_copy(
            weight_hbm.at[slot, rows_at(start, rows), :], piece.at[slot], sems.at[slot]
        )
        for slot in range(piece.shape[0])
    ]
    for copy in copies:
        copy.start()
    wait_all(copies)


def cut_piece(conv_weight):
    slots, chan, width = conv_weight.shape
    return pl.pallas_call(
        cut_kernel,
        out_shape=pltpu.VMEM((slots, chan // 8, width), BF16),
        in_specs=[HBM],
        out_specs=VMEM,
        scratch_shapes=[pltpu.SemaphoreType.DMA((slots,))],
        compiler_params=params(4),
        cost_estimate=claim(0),
        name="cut_piece",
    )(far(conv_weight))


def both_kernel(over_one, over_two, _, both):
    slots = over_one.shape[0]
    both[0:slots] = over_one[...]
    both[slots:] = over_two[...]


def fetch_pieces(first, straight, token):
    over_one = swap_dp(first, 1)
    over_two = swap_dp(first, 2)
    straight = swap_tap(after(straight, first))
    slots = first.shape[0]
    both = pl.pallas_call(
        both_kernel,
        out_shape=pltpu.VMEM((2 * slots,) + first.shape[1:], BF16),
        in_specs=[VMEM] * 3,
        out_specs=VMEM,
        compiler_params=params(4),
        cost_estimate=claim(0),
        name="both",
    )(near(over_one), near(over_two), near(token))
    return [
        ((0,), first),
        ((2, 4), both),
        ((6,), straight),
        ((1,), swap_dp(first, 0)),
        ((3, 5), swap_dp(both, 0)),
        ((7,), swap_dp(straight, 0)),
    ]


def fast_shards(
    block_input,
    conv_weight,
    slot_tap_table,
    conv_bias,
    conv_norm_gain,
    conv_norm_bias,
    w_in,
    b_in,
    w_out,
    b_out,
    ffn_norm_gain,
    ffn_norm_bias,
    species_id,
    species_count,
    out_grad,
):
    tap_count = lax.axis_size("tap")
    dp_bits = (lax.axis_size("dp") - 1).bit_length()
    rows_dev = block_input.shape[0] // tap_count
    chan = block_input.shape[1]
    hid = w_in.shape[1]
    windows = rows_dev // WINDOW_LENGTH
    slots = conv_weight.shape[0]
    vmem = pltpu.VMEM
    line = list(range(2, dp_bits))
    orders = (["t", 1] + line, [1, "t"] + line)
    orders_b = ([2, "t", 1] + line[1:], [2, 1, "t"] + line[1:])
    over_x, over_y = 1, 4
    pad_shape = (windows, WINDOW_LENGTH + 2 * PAD, chan)
    rows_f = (rows_dev, chan)
    small_cost = claim(0)

    def row(vector):
        return vector.reshape(1, -1)

    piece = cut_piece(conv_weight)
    weight_shape = conv_weight.shape
    tiles = rows_dev // TILE
    dma = pltpu.SemaphoreType.DMA
    first = swap_tap(piece)
    x_pad, own_weight, w_in_near, straight = pl.pallas_call(
        load_kernel,
        out_shape=[
            vmem(pad_shape, BF16),
            vmem(weight_shape, BF16),
            vmem(w_in.shape, BF16),
            vmem((slots * chan // 8 + TABLE_ROWS, chan), BF16),
        ],
        in_specs=[SMEM] + [HBM] * 3,
        out_specs=[VMEM] * 4,
        scratch_shapes=[dma((windows + 2 * slots + 4,))],
        compiler_params=params(8),
        cost_estimate=claim(0),
        name="load",
    )(slot_tap_table, far(block_input), far(conv_weight), far(w_in))
    first = after(first, x_pad)
    part, token = pl.pallas_call(
        own_conv_kernel,
        out_shape=[vmem(rows_f, F32), vmem((8, 128), F32)],
        in_specs=[SMEM] + [VMEM] * 3,
        out_specs=[VMEM] * 2,
        compiler_params=params(8),
        cost_estimate=claim(0),
        name="own_conv",
    )(slot_tap_table, near(x_pad), near(own_weight), near(first))
    pieces = fetch_pieces(first, straight, token)

    block_f = (hid + chan * hid // COLS) >> (dp_bits + 1)
    half_f = block_f << dp_bits
    main = pl.pallas_call(
        functools.partial(main_kernel, orders, dp_bits, [turn for turn, _ in pieces]),
        out_shape=[
            pltpu.HBM(rows_f, BF16),
            vmem(rows_f, F32),
            vmem(rows_f, F32),
            vmem((rows_dev, hid), BF16),
            vmem(conv_weight.shape, BF16),
            vmem((half_f, chan), F32),
            vmem((half_f, chan), BF16),
            vmem((8, chan), F32),
            vmem(rows_f, BF16),
            jax.ShapeDtypeStruct((slots,), jnp.int32),
        ],
        in_specs=[SMEM] * 2 + [VMEM] * 2 + [HBM, VMEM, HBM] + [VMEM] * (7 + len(pieces)),
        out_specs=[HBM] + [VMEM] * 8 + [SMEM],
        scratch_shapes=[
            vmem(w_out.shape, BF16),
            vmem(rows_f, F32),
            vmem(rows_f, BF16),
            vmem((rows_dev, hid), BF16),
            vmem((rows_dev, hid), F32),
            vmem(rows_f, BF16),
            vmem(rows_f, BF16),
            vmem((2, COLS, chan), F32),
            vmem((8, 8, chan), F32),
            dma,
            dma((12,)),
        ],
        compiler_params=params(34),
        cost_estimate=small_cost,
        name="main_rows",
    )(
        species_id,
        species_count,
        near(x_pad),
        near(part),
        far(out_grad),
        near(w_in_near),
        far(w_out),
        row(conv_bias),
        row(conv_norm_gain),
        row(conv_norm_bias),
        row(b_in),
        row(b_out),
        row(ffn_norm_gain),
        row(ffn_norm_bias),
        *[near(piece) for _, piece in pieces],
    )
    block_output, unit, slope, d_up, other_weight, keep_f, send_f, small_ffn = main[:8]
    grad_in, other_table = main[8:]
    got_f = swap_dp(send_f, 0)

    d_pad, d_hidden, small = pl.pallas_call(
        back_kernel,
        out_shape=[vmem(pad_shape, BF16), vmem(rows_f, F32), vmem((16, chan), F32)],
        in_specs=[SMEM] * 2 + [VMEM] * 7,
        out_specs=[VMEM] * 3,
        scratch_shapes=[vmem((8, 8, chan), F32)],
        compiler_params=params(8),
        cost_estimate=small_cost,
        name="back_rows",
    )(
        species_id,
        species_count,
        near(grad_in),
        near(w_in_near),
        near(d_up),
        near(unit),
        near(slope),
        row(conv_norm_gain),
        near(small_ffn),
    )
    flow_f = dict(keep=keep_f)
    rows = keep_f.shape[0] // 2
    plan = dict(ins=[(0, 0), (0, rows)], outs=[(0, 0), (1, 0)])
    sends_f = fused_step([got_f], [flow_f], [plan], [rows // 2] * 2, small)
    gots_f = [swap(sends_f[0], over_x), swap(sends_f[1], over_y)]

    def terms(group, orders, token, small, name):
        count = len(group) * chan
        extra = 0 if small is None else 2 * small.shape[0]
        outs = [vmem((count, chan), F32), vmem((count + extra, chan), BF16)]
        scratch = [vmem((2, chan, chan), F32)]
        more = [] if small is None else [near(small)]
        return pl.pallas_call(
            functools.partial(terms_kernel, group, orders, dp_bits, small is not None),
            out_shape=outs,
            in_specs=[SMEM] * 2 + [VMEM] * (3 + len(more)),
            out_specs=[VMEM] * len(outs),
            scratch_shapes=scratch,
            compiler_params=params(8),
            cost_estimate=small_cost,
            name=name,
        )(slot_tap_table, other_table, near(x_pad), near(d_pad), *more, near(token))

    cut = (slots * 3 + 4) // 5
    keep_a, send_a = terms(range(0, cut), orders, sends_f[0], None, "terms_a")
    got_a = swap_dp(send_a, 0)
    keep_b, send_b = terms(range(cut, slots), orders_b, keep_a, small, "terms_b")
    got_b = swap_dp(send_b, 0)
    def spaced(token, claimed=1):
        return after(mark, token, claimed)

    mark = token
    flow_a = dict(keep=keep_a)
    flow_b = dict(keep=keep_b, small=small)
    extra = 2 * small.shape[0]
    over_z, over_zz = 2 << line[0], 2 << line[1]

    def half_of(flow):
        return flow["keep"].shape[0] // 4

    def joined(base, flow):
        return [(0, base), (0, base + 2 * half_of(flow))]

    size = half_of(flow_f)
    plan = dict(ins=[(0, 0), (1, 0)], outs=[(0, 0), (1, 0)])
    sends = fused_step(gots_f, [flow_f], [plan], [size] * 2, keep_b)
    gots_f = [swap(sends[0], over_y), swap(sends[1], over_x)]
    mark = spaced(flow_f["keep"], 100)
    size = half_of(flow_b)
    plan = dict(
        ins=joined(0, flow_b),
        small_in=(0, 4 * size),
        outs=[(0, 0), (0, size)],
        small_out=(0, 2 * size),
    )
    sends = fused_step([got_b], [flow_b], [plan], [2 * size + extra], mark)
    got_b = swap(sends[0], over_z)
    partial = pl.pallas_call(
        input_near_kernel,
        out_shape=vmem(rows_f, F32),
        in_specs=[SMEM] + [VMEM] * 4,
        out_specs=VMEM,
        compiler_params=params(8),
        cost_estimate=claim(0),
        name="input_near",
    )(slot_tap_table, near(d_pad), near(d_hidden), near(own_weight), near(flow_b["keep"]))
    size = half_of(flow_f)
    plan = dict(ins=[(0, 0), (1, 0)], outs=[(0, 0), (0, size)])
    sends = fused_step(gots_f, [flow_f], [plan], [2 * size], partial)
    got_f = swap(sends[0], over_z)
    mark = spaced(flow_f["keep"])
    size = half_of(flow_a)
    plan = dict(ins=joined(0, flow_a), outs=[(0, 0), (1, 0)])
    sends = fused_step([got_a], [flow_a], [plan], [size] * 2, mark)
    gots_a = [swap(sends[0], over_x), swap(sends[1], over_y)]
    input_grad, mark = pl.pallas_call(
        input_far_kernel,
        out_shape=[pltpu.HBM(rows_f, F32), vmem((8, 128), F32)],
        in_specs=[SMEM] + [VMEM] * 4,
        out_specs=[HBM, VMEM],
        scratch_shapes=[vmem(rows_f, F32), pltpu.SemaphoreType.DMA((rows_dev // TILE,))],
        compiler_params=params(8),
        cost_estimate=small_cost,
        name="input_far",
    )(other_table, near(d_pad), near(partial), near(other_weight), near(flow_a["keep"]))
    mark = spaced(mark)
    size = half_of(flow_f)
    plan = dict(ins=joined(0, flow_f), outs=[(0, 0), (0, size)])
    sends = fused_step([got_f], [flow_f], [plan], [2 * size], mark)
    got_f = swap(sends[0], over_zz)
    mark = spaced(flow_f["keep"])
    size, size_b = half_of(flow_a), half_of(flow_b)
    plan = dict(ins=[(0, 0), (1, 0)], outs=[(0, 0), (1, 0)])
    plan_b = dict(
        ins=[(2, 0), (2, 2 * size_b)],
        small_in=(2, 4 * size_b),
        outs=[(1, size), (0, size)],
        small_out=(1, size + size_b),
    )
    sends = fused_step(
        gots_a + [got_b],
        [flow_a, flow_b],
        [plan, plan_b],
        [size + size_b, size + size_b + extra],
        mark,
    )
    gots = [swap(sends[0], over_y), swap(sends[1], over_x)]
    mark = spaced(flow_a["keep"])
    shift = size
    size = half_of(flow_a)
    plan = dict(ins=[(0, 0), (1, 0)], outs=[(0, 0), (0, size)])
    sends = fused_step(gots, [flow_a], [plan], [2 * size], mark)
    got_a = swap(sends[0], over_z)
    size = half_of(flow_b)
    plan = dict(
        ins=[(1, shift), (0, shift)],
        small_in=(1, shift + 2 * size),
        outs=[(0, 0), (1, 0)],
        small_out=(0, size),
    )
    sends = fused_step(gots, [flow_b], [plan], [size + extra, size], flow_a["keep"])
    gots_b = [swap(sends[0], over_y), swap(sends[1], over_x)]
    mark = spaced(flow_b["keep"])
    w_in_mine, w_out_mine, mark = pl.pallas_call(
        functools.partial(last_ffn_kernel, 1),
        out_shape=[
            jax.ShapeDtypeStruct((chan >> (dp_bits + 1), hid), F32),
            jax.ShapeDtypeStruct((hid >> (dp_bits + 1), chan), F32),
            vmem((8, 128), F32),
        ],
        in_specs=[VMEM] * 3,
        out_specs=[VMEM] * 3,
        compiler_params=params(4),
        cost_estimate=claim(0),
        name="last_ffn",
    )(near(got_f), near(flow_f["keep"]), near(mark))
    mark = spaced(mark)
    size, size_b = half_of(flow_a), half_of(flow_b)
    plan = dict(ins=joined(0, flow_a), outs=[(0, 0), (0, size)])
    shift = 2 * size
    plan_b = dict(
        ins=[(1, 0), (2, 0)],
        small_in=(1, 2 * size_b),
        outs=[(0, shift), (0, shift + size_b)],
        small_out=(0, shift + 2 * size_b),
    )
    sends = fused_step(
        [got_a] + gots_b, [flow_a, flow_b], [plan, plan_b], [shift + 2 * size_b + extra], mark
    )
    got = swap(sends[0], over_zz)
    width = chan >> (dp_bits + 1)
    wide = hid >> (dp_bits + 1)
    small = flow_b["small"]
    conv_weight_grad, _, *vectors = pl.pallas_call(
        last_conv_kernel,
        out_shape=[
            jax.ShapeDtypeStruct((slots, chan >> dp_bits, chan), F32),
            vmem(small.shape, F32),
        ]
        + [jax.ShapeDtypeStruct((1, width), F32)] * 6
        + [jax.ShapeDtypeStruct((1, wide), F32)],
        in_specs=[VMEM] * 4,
        out_specs=[VMEM] * 9,
        compiler_params=params(4),
        cost_estimate=claim(0),
        name="last_conv",
    )(near(got), near(flow_a["keep"]), near(small), near(flow_b["keep"]))
    conv_bias_grad, gain_one_grad, bias_one_grad, b_out_grad, gain_two_grad, bias_two_grad, b_in_grad = [
        vector.reshape(-1) for vector in vectors
    ]
    return (
        block_output,
        input_grad,
        conv_weight_grad,
        conv_bias_grad,
        gain_one_grad,
        bias_one_grad,
        w_in_mine,
        b_in_grad,
        w_out_mine,
        b_out_grad,
        gain_two_grad,
        bias_two_grad,
    )


def narrow_enough(mesh):
    return mesh.shape["tap"] == 2 and mesh.shape["dp"] == 16


def solution(mesh):
    chosen = fast_shards if narrow_enough(mesh) else plain_shards
    return jax.shard_map(
        chosen,
        mesh=mesh,
        in_specs=(
            P("dp", None),
            P("tap", None, None),
            P("tap"),
            P(),
            P(),
            P(),
            P(),
            P(),
            P(),
            P(),
            P(),
            P(),
            P("dp"),
            P(),
            P(("dp", "tap"), None),
        ),
        out_specs=(
            P(("dp", "tap"), None),
            P(("dp", "tap"), None),
            P("tap", "dp", None),
            P(("dp", "tap")),
            P(("dp", "tap")),
            P(("dp", "tap")),
            P(("dp", "tap"), None),
            P(("dp", "tap")),
            P(("dp", "tap"), None),
            P(("dp", "tap")),
            P(("dp", "tap")),
            P(("dp", "tap")),
        ),
        check_vma=False,
    )
```

```python
import functools

import jax
import jax.numpy as jnp
from jax import lax
from jax.experimental import pallas as pl
from jax.experimental.pallas import tpu as pltpu
from jax.sharding import PartitionSpec as P

KERNEL_TAPS = 9
DILATION_STEP = 16
WINDOW_LENGTH = 512


def layer_norm(values):
    mean_val = jnp.mean(values, axis=-1, keepdims=True)
    center = values - mean_val
    spread = jnp.mean(center * center, axis=-1, keepdims=True)
    return center * lax.rsqrt(spread + 1e-05)


def exact_gelu(values):
    return jax.nn.gelu(values, approximate=False)


def conv_branch(pre_conv, gain_one, bias_one):
    return layer_norm(exact_gelu(pre_conv)) * gain_one + bias_one


def ffn_branch(pre_out, gain_two, bias_two):
    return layer_norm(pre_out) * gain_two + bias_two


def shift_stack(win_rows, tap_table, forward):
    tap_extent = KERNEL_TAPS // 2 * DILATION_STEP
    padded_input = jnp.pad(win_rows, ((0, 0), (tap_extent, tap_extent), (0, 0)))
    pieces = []
    for index_of_slot in range(tap_table.shape[0]):
        if forward:
            tap_offset = tap_table[index_of_slot]
        else:
            tap_offset = KERNEL_TAPS - 1 - tap_table[index_of_slot]
        shifted_input = lax.dynamic_slice_in_dim(
            padded_input, tap_offset * DILATION_STEP, WINDOW_LENGTH, 1
        )
        pieces.append(shifted_input.reshape(-1, win_rows.shape[2]))
    return jnp.stack(pieces)


def contract_rows(left, right):
    return lax.dot_general(
        left, right, (((0,), (0,)), ((), ())), preferred_element_type=jnp.float32
    )


def contract_cols(left, right):
    return lax.dot_general(
        left, right, (((1,), (1,)), ((), ())), preferred_element_type=jnp.float32
    )


def swap_dp(value, bit):
    count = lax.axis_size("dp")
    return lax.ppermute(value, "dp", [(i, i ^ (1 << bit)) for i in range(count)])


def swap_tap(value):
    return lax.ppermute(value, "tap", [(0, 1), (1, 0)])


def halve(part, order, kind):
    dp_bits = (lax.axis_size("dp") - 1).bit_length()
    place = lax.axis_index("dp")
    tap = lax.axis_index("tap")
    labels = ["t"] + list(range(dp_bits - 1, -1, -1))
    for step in order:
        axis = labels.index(step)
        labels.pop(axis)
        mine = tap if step == "t" else (place >> step) & 1
        keep = lax.dynamic_index_in_dim(part, mine, axis, keepdims=False)
        send = lax.dynamic_index_in_dim(part, 1 - mine, axis, keepdims=False).astype(kind)
        got = swap_tap(send) if step == "t" else swap_dp(send, step)
        part = keep + got.astype(jnp.float32)
    return part


def orders(dp_bits):
    rest = list(range(2, dp_bits))
    first = [0, "t", 1] + rest
    second = [0, 1] + rest[:1] + ["t"] + rest[1:]
    third = [0] + rest[:1] + ["t", 1] + rest[1:]
    return first, second, third


def plain_shards(
    block_input,
    conv_weight,
    slot_tap_table,
    conv_bias,
    conv_norm_gain,
    conv_norm_bias,
    w_in,
    b_in,
    w_out,
    b_out,
    ffn_norm_gain,
    ffn_norm_bias,
    species_id,
    species_count,
    out_grad,
):
    tap_count = lax.axis_size("tap")
    my_index = lax.axis_index("tap")
    core = lax.axis_index("dp") & 1
    dp_bits = (lax.axis_size("dp") - 1).bit_length()
    tok_dev, chan_width = block_input.shape
    hid_width = w_in.shape[1]
    half_rows = tok_dev // tap_count
    windows = tok_dev // WINDOW_LENGTH
    my_windows = windows // tap_count
    own_slots = conv_weight.shape[0]
    half_chan = chan_width // 2
    first, second, third = orders(dp_bits)

    other_table = swap_tap(slot_tap_table)
    part_send = lax.dynamic_slice_in_dim(conv_weight, core * half_chan, half_chan, 1)
    part_here = swap_tap(part_send)
    part_mate = swap_dp(part_here, 0)
    low_part = jnp.where(core == 0, part_here, part_mate)
    high_part = jnp.where(core == 0, part_mate, part_here)
    other_weight = jnp.concatenate([low_part, high_part], axis=1)

    my_x = lax.dynamic_slice_in_dim(block_input, my_index * half_rows, half_rows, 0)
    x_windows = my_x.reshape(my_windows, WINDOW_LENGTH, chan_width)
    mine_x = my_x.astype(jnp.float32)
    own_stack = shift_stack(x_windows, slot_tap_table, True)
    other_stack = shift_stack(x_windows, other_table, True)
    conv_out = jnp.einsum("str,sro->to", own_stack, conv_weight, preferred_element_type=jnp.float32)
    conv_out = conv_out + jnp.einsum(
        "str,sro->to", other_stack, other_weight, preferred_element_type=jnp.float32
    )
    pre_conv = conv_out + conv_bias
    norm_one, conv_back = jax.vjp(conv_branch, pre_conv, conv_norm_gain, conv_norm_bias)
    hidden = mine_x + norm_one
    hidden_low = hidden.astype(jnp.bfloat16)
    pre_up = jnp.dot(hidden_low, w_in, preferred_element_type=jnp.float32) + b_in
    activ, activ_back = jax.vjp(exact_gelu, pre_up)
    act_low = activ.astype(jnp.bfloat16)
    pre_out = jnp.dot(act_low, w_out, preferred_element_type=jnp.float32) + b_out
    norm_two, ffn_back = jax.vjp(ffn_branch, pre_out, ffn_norm_gain, ffn_norm_bias)
    block_output = (hidden + norm_two).astype(jnp.bfloat16)
    my_species = lax.dynamic_slice_in_dim(species_id, my_index * my_windows, my_windows, 0)
    species_range = jnp.arange(species_count.shape[0], dtype=jnp.int32)
    matches = my_species[:, None] == species_range[None, :]
    window_count = jnp.sum(jnp.where(matches, species_count[None, :], 0), axis=1)
    window_scale = 4.0 / window_count.astype(jnp.float32)
    grad_y = (
        out_grad.astype(jnp.float32).reshape(my_windows, WINDOW_LENGTH, chan_width)
        * window_scale[:, None, None]
    ).reshape(half_rows, chan_width)
    d_pre_out, d_gain_two, d_bias_two = ffn_back(grad_y)
    d_out_low = d_pre_out.astype(jnp.bfloat16)
    d_w_out = contract_rows(act_low, d_out_low)
    d_b_out = jnp.sum(d_out_low.astype(jnp.float32), axis=0)
    d_activ = contract_cols(d_out_low, w_out)
    (d_pre_up,) = activ_back(d_activ)
    d_up_low = d_pre_up.astype(jnp.bfloat16)
    d_w_in = contract_rows(hidden_low, d_up_low)
    d_b_in = jnp.sum(d_up_low.astype(jnp.float32), axis=0)
    d_hidden = grad_y + contract_cols(d_up_low, w_in)
    d_pre_conv, d_gain_one, d_bias_one = conv_back(d_hidden)
    d_conv_low = d_pre_conv.astype(jnp.bfloat16)
    d_conv_bias = jnp.sum(d_conv_low.astype(jnp.float32), axis=0)
    d_windows = d_conv_low.reshape(my_windows, WINDOW_LENGTH, chan_width)
    own_back = shift_stack(d_windows, slot_tap_table, False)
    other_back = shift_stack(d_windows, other_table, False)
    input_grad = (
        d_hidden
        + jnp.einsum("sto,sro->tr", own_back, conv_weight, preferred_element_type=jnp.float32)
        + jnp.einsum("sto,sro->tr", other_back, other_weight, preferred_element_type=jnp.float32)
    )
    own_terms = jnp.einsum("str,to->sro", own_stack, d_conv_low, preferred_element_type=jnp.float32)
    other_terms = jnp.einsum(
        "str,to->sro", other_stack, d_conv_low, preferred_element_type=jnp.float32
    )
    bits = [2] * dp_bits

    def by_tap(own, other):
        return jnp.where(my_index == 0, jnp.stack([own, other]), jnp.stack([other, own]))

    def conv_part(begin, end, order):
        own = own_terms[begin:end]
        other = other_terms[begin:end]
        both = by_tap(own, other)
        rows = chan_width >> dp_bits
        both = both.reshape([2, end - begin] + bits + [rows, chan_width])
        return halve(jnp.moveaxis(both, 1, 1 + dp_bits), order, jnp.bfloat16)

    cut = own_slots * 2 // 5
    conv_weight_grad = jnp.concatenate(
        [
            conv_part(0, cut, first),
            conv_part(cut, 2 * cut, second),
            conv_part(2 * cut, own_slots, third),
        ]
    )

    def spread(total, order, kind):
        rows = total.shape[0] >> (dp_bits + 1)
        split = total.reshape(bits + [2, rows] + list(total.shape[1:]))
        return halve(jnp.moveaxis(split, dp_bits, 0), order, kind)

    d_w_out_mine = spread(d_w_out, first, jnp.bfloat16)
    d_w_in_mine = spread(d_w_in, second, jnp.bfloat16)
    owners = 2 << dp_bits
    small = [d_b_in, d_b_out, d_conv_bias, d_gain_one, d_bias_one, d_gain_two, d_bias_two]
    joined = jnp.concatenate([v.reshape(owners, -1) for v in small], axis=1)
    joined_mine = spread(joined, third, jnp.float32).reshape(-1)
    vectors = []
    start = 0
    for v in small:
        size = v.shape[0] // owners
        vectors.append(joined_mine[start : start + size])
        start += size
    return (
        block_output,
        input_grad,
        conv_weight_grad,
        vectors[2],
        vectors[3],
        vectors[4],
        d_w_in_mine,
        vectors[0],
        d_w_out_mine,
        vectors[1],
        vectors[5],
        vectors[6],
    )


TILE = 512
COLS = 512
PAD = KERNEL_TAPS // 2 * DILATION_STEP
MIB = 2**20
TABLE_ROWS = 16
F32 = jnp.float32
BF16 = jnp.bfloat16
HBM = pl.BlockSpec(memory_space=pltpu.HBM)
VMEM = pl.BlockSpec(memory_space=pltpu.VMEM)
SMEM = pl.BlockSpec(memory_space=pltpu.SMEM)


def dot_plain(left, right):
    return lax.dot_general(left, right, (((1,), (0,)), ((), ())), preferred_element_type=F32)


def gelu_and_slope(value):
    cdf = 0.5 + 0.5 * lax.erf(value * 0.7071067811865476)
    density = jnp.exp2(value * value * -0.7213475204444817)
    return value * cdf, cdf + (value * 0.3989422804014327) * density


def norm_parts(value):
    center = value - jnp.mean(value, axis=-1, keepdims=True)
    spread = jnp.mean(center * center, axis=-1, keepdims=True)
    scale = lax.rsqrt(spread + 1e-05)
    return center * scale, scale


def norm_back(grad, unit):
    return grad - jnp.mean(grad, axis=-1, keepdims=True) - unit * jnp.mean(
        grad * unit, axis=-1, keepdims=True
    )


def fold_rows(value):
    return jnp.sum(value.reshape(value.shape[0] // 8, 8, value.shape[1]), axis=0)


def one_row(value):
    return jnp.sum(value, axis=0, keepdims=True)


def my_bits(dp_bits):
    place = lax.axis_index("dp")
    mine = {bit: (place >> bit) & 1 for bit in range(dp_bits)}
    mine["t"] = lax.axis_index("tap")
    return mine


def relative(order, owner, mine):
    spot = 0
    for label in order:
        spot = spot * 2 + (owner[label] ^ mine[label])
    return spot


def rows_at(start, size):
    return pl.ds(pl.multiple_of(start, 16), size)


def split_copy(source, target, sems, first):
    rows = target.shape[0] // 4
    return [
        pltpu.make_async_copy(
            source.at[at * rows : (at + 1) * rows, :],
            target.at[at * rows : (at + 1) * rows, :],
            sems.at[first + at],
        )
        for at in range(4)
    ]


def wait_all(copies):
    for copy in copies:
        copy.wait()


def clear_pads(pad_ref):
    zeros = jnp.zeros((PAD, pad_ref.shape[2]), pad_ref.dtype)
    for win in range(pad_ref.shape[0]):
        pad_ref[win, 0:PAD, :] = zeros
        pad_ref[win, PAD + WINDOW_LENGTH :, :] = zeros


def each_tile(rows, body, together=1):
    per = WINDOW_LENGTH // TILE

    @pl.loop(0, rows // TILE // together)
    def _(step):
        for member in range(together):
            number = step * together + member
            body(rows_at(number * TILE, TILE), number // per, (number % per) * TILE)


def window_weight(species, counts, win, windows, lanes):
    kind = species[lax.axis_index("tap") * windows + win]
    count = jnp.full((8, lanes), counts[kind], jnp.int32).astype(F32)
    return (4.0 / count)[0:1, :]


def load_kernel(
    table, x_hbm, weight_hbm, w_in_hbm, x_pad, weight, w_in, straight, sems
):
    windows = x_pad.shape[0]
    slots = weight.shape[0]
    rows = weight.shape[1] // 8
    base = lax.axis_index("tap") * windows * WINDOW_LENGTH
    start = ((lax.axis_index("dp") & 7) ^ 6) * rows
    copies = []
    for slot in range(slots):
        source = weight_hbm.at[slot, rows_at(start, rows), :]
        copies.append((source, straight.at[slot * rows : (slot + 1) * rows, :]))
    for win in range(windows):
        source = x_hbm.at[rows_at(base + win * WINDOW_LENGTH, WINDOW_LENGTH), :]
        copies.append((source, x_pad.at[win, PAD : PAD + WINDOW_LENGTH, :]))
    copies += [(weight_hbm.at[slot], weight.at[slot]) for slot in range(slots)]
    copies = [
        pltpu.make_async_copy(source, target, sems.at[at])
        for at, (source, target) in enumerate(copies)
    ]
    copies += split_copy(w_in_hbm, w_in, sems, len(copies))
    for copy in copies:
        copy.start()
    at = lax.broadcasted_iota(jnp.int32, (TABLE_ROWS, straight.shape[1]), 0)
    taps = jnp.zeros(at.shape, jnp.int32)
    for slot in range(slots):
        taps = jnp.where(at == slot, table[slot], taps)
    straight[slots * rows :, :] = taps.astype(F32).astype(BF16)
    clear_pads(x_pad)
    wait_all(copies)


def own_conv_kernel(table, x_pad, weight, _, part, token):
    token[...] = jnp.zeros(token.shape, token.dtype)

    def convolve(rows, win, begin):
        total = None
        for slot in range(weight.shape[0]):
            shifted = rows_at(table[slot] * DILATION_STEP + begin, TILE)
            term = dot_plain(x_pad[win, shifted, :], weight[slot])
            total = term if total is None else total + term
        part[rows, :] = total

    each_tile(part.shape[0], convolve, 2)


def join_pieces(plan, pieces, weight):
    slots = weight.shape[0]
    rows = weight.shape[1] // 8
    place = lax.axis_index("dp") & 7
    for turns, piece in zip(plan, pieces):
        flat = len(piece.shape) == 2
        for number, turn in enumerate(turns):
            there = rows_at((place ^ turn) * rows, rows)
            if flat:
                for slot in range(slots):
                    weight[slot, there, :] = piece[slot * rows : (slot + 1) * rows, :]
            else:
                weight[:, there, :] = piece[number * slots : (number + 1) * slots]


def main_kernel(orders, dp_bits, turns, *refs):
    species, counts = refs[:2]
    x_pad, part, grad_hbm, w_in, w_out_hbm = refs[2:7]
    conv_bias, gain_one, bias_one, b_in, b_out, gain_two, bias_two = refs[7:14]
    pieces = refs[14 : 14 + len(turns)]
    y_hbm, unit, slope, d_up, weight, keep, send, small, grad_in, table = refs[
        14 + len(turns) : 24 + len(turns)
    ]
    w_out, hidden, low, act, hid_slope, d_out, y_low, result, sums, sem, sems = refs[24 + len(turns) :]
    told = pieces[turns.index((6,))]
    told_at = told.shape[0] - TABLE_ROWS
    taps = []
    for slot in range(weight.shape[0]):
        line = told[told_at : told_at + TABLE_ROWS, 0:128].astype(F32)
        chosen = lax.broadcasted_iota(jnp.int32, line.shape, 0) == slot
        taps.append(jnp.max(jnp.where(chosen, line, 0.0)).astype(jnp.int32))
        table[slot] = taps[slot]
    mine = my_bits(dp_bits)
    rows_dev, chan = hidden.shape
    hid_width = w_in.shape[1]
    windows = x_pad.shape[0]
    out_copies = split_copy(w_out_hbm, w_out, sems, 4)
    grad_copies = split_copy(grad_hbm, grad_in, sems, 8)
    for copy in out_copies + grad_copies:
        copy.start()
    join_pieces(turns, pieces, weight)
    sums[...] = jnp.zeros(sums.shape, F32)

    def first_norm(rows, win, begin):
        total = part[rows, :] + conv_bias[...]
        for slot in range(weight.shape[0]):
            shifted = rows_at(taps[slot] * DILATION_STEP + begin, TILE)
            total = total + dot_plain(x_pad[win, shifted, :], weight[slot])
        value, steep = gelu_and_slope(total)
        normed, scale = norm_parts(value)
        unit[rows, :] = normed
        slope[rows, :] = scale * steep
        here = x_pad[win, rows_at(PAD + begin, TILE), :].astype(F32)
        summed = here + (normed * gain_one[...] + bias_one[...])
        hidden[rows, :] = summed
        low[rows, :] = summed.astype(BF16)

    each_tile(rows_dev, first_norm, 2)

    def go_up(rows, win, begin):
        for at in range(0, hid_width, COLS):
            cols = slice(at, at + COLS)
            up = dot_plain(low[rows, :], w_in[:, cols]) + b_in[:, cols]
            value, steep = gelu_and_slope(up)
            act[rows, cols] = value.astype(BF16)
            hid_slope[rows, cols] = steep

    each_tile(rows_dev, go_up, 2)
    wait_all(out_copies + grad_copies)

    def second_norm(rows, win, begin):
        pre_out = dot_plain(act[rows, :], w_out[...]) + b_out[...]
        normed, scale = norm_parts(pre_out)
        result_rows = hidden[rows, :] + (normed * gain_two[...] + bias_two[...])
        y_low[rows, :] = result_rows.astype(BF16)
        grad_y = grad_in[rows, :].astype(F32) * window_weight(species, counts, win, windows, chan)
        back = (norm_back(grad_y * gain_two[...], normed) * scale).astype(BF16)
        d_out[rows, :] = back
        sums[0] += fold_rows(back.astype(F32))
        sums[1] += fold_rows(grad_y * normed)
        sums[2] += fold_rows(grad_y)

    each_tile(rows_dev, second_norm, 2)
    y_copy = pltpu.make_async_copy(y_low, y_hbm, sem)
    y_copy.start()

    def go_down(rows, win, begin):
        for number, at in enumerate(range(0, hid_width, COLS)):
            cols = slice(at, at + COLS)
            d_act = contract_cols(d_out[rows, :], w_out[cols, :])
            back = (d_act * hid_slope[rows, cols]).astype(BF16)
            d_up[rows, cols] = back
            sums[3 + number] += fold_rows(back.astype(F32))

    each_tile(rows_dev, go_down, 2)
    for number in range(8):
        small[number : number + 1, :] = one_row(sums[number])
    core = mine[0]
    out_block = hid_width >> (dp_bits + 1)
    in_block = chan >> (dp_bits + 1)
    chunks = hid_width // COLS
    half = (out_block + chunks * in_block) // 2

    def hand_out(spot, first_row, block, targets):
        for start in range(0, result.shape[1], 4 * block):
            owner_at = first_row // block + start // block
            for tap in range(2):
                owner = {bit: (owner_at >> (bit + 1)) & 1 for bit in range(1, dp_bits)}
                owner["t"] = tap
                inner = start + tap * block
                for part_at, source, size, shift in targets:
                    spread = relative(orders[part_at], owner, mine) + (part_at << dp_bits)
                    place = rows_at(spread * half + shift, size)
                    mine_at = rows_at(inner + source + core * 2 * block, size)
                    other_at = rows_at(inner + source + (1 - core) * 2 * block, size)
                    keep[place, :] = result[spot, mine_at, :]
                    send[place, :] = result[spot, other_at, :].astype(BF16)

    size = out_block // 2

    @pl.loop(0, chunks // 2)
    def _(pair):
        for spot in range(2):
            at = pl.multiple_of((pair * 2 + spot) * COLS, COLS)
            result[spot] = contract_rows(act[:, pl.ds(at, COLS)], d_out[...])
            hand_out(spot, at, out_block, [(0, 0, size, 0), (1, size, size, 0)])

    @pl.loop(0, chunks // 2)
    def _(step):
        shift = size + step * in_block
        for spot in range(2):
            at = pl.multiple_of((spot * (chunks // 2) + step) * COLS, COLS)
            result[spot] = contract_rows(low[...], d_up[:, pl.ds(at, COLS)])
            hand_out(spot, 0, in_block, [(spot, 0, in_block, shift)])

    y_copy.wait()


def back_kernel(
    species,
    counts,
    grad_in,
    w_in,
    d_up,
    unit,
    slope,
    gain_one,
    small_in,
    d_pad,
    d_hidden,
    small,
    sums,
):
    windows = d_pad.shape[0]
    chan = d_hidden.shape[1]
    clear_pads(d_pad)
    sums[...] = jnp.zeros(sums.shape, F32)

    def through_norm(rows, win, begin):
        grad = grad_in[rows, :].astype(F32) * window_weight(species, counts, win, windows, chan)
        grad = grad + contract_cols(d_up[rows, :], w_in[...])
        d_hidden[rows, :] = grad
        normed = unit[rows, :]
        back = (norm_back(grad * gain_one[...], normed) * slope[rows, :]).astype(BF16)
        d_pad[win, rows_at(PAD + begin, TILE), :] = back
        sums[0] += fold_rows(back.astype(F32))
        sums[1] += fold_rows(grad * normed)
        sums[2] += fold_rows(grad)

    each_tile(d_hidden.shape[0], through_norm, 2)
    small[0:8, :] = small_in[...]
    for number in range(8):
        small[8 + number : 9 + number, :] = one_row(sums[number])


def store_small(total, ref, first):
    count = total.shape[0]
    high = total.astype(BF16)
    ref[first : first + count, :] = high
    ref[first + count : first + 2 * count, :] = (total - high.astype(F32)).astype(BF16)


def load_small(ref, first, count):
    high = ref[first : first + count, :].astype(F32)
    return high + ref[first + count : first + 2 * count, :].astype(F32)


def terms_kernel(slots, orders, dp_bits, with_small, own_table, other_table, x_pad, d_pad, *refs):
    if with_small:
        small, _, keep, send, result = refs
        store_small(small[...], send, keep.shape[0])
    else:
        _, keep, send, result = refs
    mine = my_bits(dp_bits)
    rows = x_pad.shape[2] >> dp_bits
    core = mine[0]
    tables = (own_table, other_table)
    size = rows // 2

    @pl.loop(0, len(slots))
    def _(number):
        for near_tap in range(2):
            tap = tables[near_tap][slots[0] + number]
            shifted = rows_at((KERNEL_TAPS - 1 - tap) * DILATION_STEP, WINDOW_LENGTH)
            total = None
            for win in range(x_pad.shape[0]):
                term = contract_rows(
                    x_pad[win, PAD : PAD + WINDOW_LENGTH, :], d_pad[win, shifted, :]
                )
                total = term if total is None else total + term
            result[near_tap] = total
            for start in range(0, x_pad.shape[2], 2 * rows):
                owner_at = start // rows
                owner = {bit: (owner_at >> bit) & 1 for bit in range(1, dp_bits)}
                owner["t"] = mine["t"] ^ near_tap
                for part_at in range(2):
                    spread = relative(orders[part_at], owner, mine) + (part_at << dp_bits)
                    place = rows_at((spread * len(slots) + number) * size, size)
                    mine_at = rows_at(start + core * rows + part_at * size, size)
                    other_at = rows_at(start + (1 - core) * rows + part_at * size, size)
                    keep[place, :] = result[near_tap, mine_at, :]
                    send[place, :] = result[near_tap, other_at, :].astype(BF16)


def input_sum(table, d_pad, base, weight, rows, win, begin):
    total = base[rows, :]
    for slot in range(weight.shape[0]):
        shifted = rows_at((KERNEL_TAPS - 1 - table[slot]) * DILATION_STEP + begin, TILE)
        total = total + contract_cols(d_pad[win, shifted, :], weight[slot])
    return total


def input_near_kernel(table, d_pad, base, weight, _, out):
    def gather(rows, win, begin):
        out[rows, :] = input_sum(table, d_pad, base, weight, rows, win, begin)

    each_tile(out.shape[0], gather, 2)


def input_far_kernel(table, d_pad, base, weight, _, out_hbm, token, out, sems):
    token[...] = jnp.zeros(token.shape, token.dtype)

    def copy_of(rows):
        return pltpu.make_async_copy(out.at[rows, :], out_hbm.at[rows, :], sems.at[0])

    def gather(rows, win, begin):
        out[rows, :] = input_sum(table, d_pad, base, weight, rows, win, begin)
        copy_of(rows).start()

    each_tile(out.shape[0], gather, 2)
    pltpu.make_async_copy(out, out_hbm, sems.at[0]).wait()


def fused_kernel(got_count, plans, *refs):
    gots = refs[:got_count]
    at = got_count
    inputs = []
    for plan in plans:
        inputs.append(refs[at : at + 1 + plan["with_small"]])
        at += 1 + plan["with_small"]
    at += 1
    kept = []
    for plan in plans:
        kept.append(refs[at : at + 1 + plan["with_small"]])
        at += 1 + plan["with_small"]
    sent = refs[at:]
    for plan, source, target in zip(plans, inputs, kept):
        keep = source[0]
        rows = keep.shape[0] // 2
        half = rows // 2
        for part in range(2):
            which, base = plan["ins"][part]
            out, spot = plan["outs"][part]
            start = part * rows
            theirs = gots[which][base + half : base + rows, :].astype(F32)
            total = keep[start + half : start + rows, :] + theirs
            sent[out][spot : spot + half, :] = total.astype(BF16)
            ours = gots[which][base : base + half, :].astype(F32)
            target[0][part * half : (part + 1) * half, :] = keep[start : start + half, :] + ours
        if plan["with_small"]:
            which, base = plan["small_in"]
            count = source[1].shape[0]
            total = source[1][...] + load_small(gots[which], base, count)
            target[1][...] = total
            out, spot = plan["small_out"]
            store_small(total, sent[out], spot)


def sum_of(gots, keep, rows):
    total = keep[rows, :]
    for got in gots:
        total = total + got[rows, :].astype(F32)
    return total


def last_ffn_kernel(members, *refs):
    gots = refs[:members]
    keep, _, w_in_out, w_out_out, token = refs[members:]
    token[...] = jnp.zeros(token.shape, token.dtype)
    out_rows, chan = w_out_out.shape
    in_rows = w_in_out.shape[0]
    half = keep.shape[0] // 2
    steps = w_in_out.shape[1] // chan // 2
    for part in range(2):
        base = part * half
        size = out_rows // 2
        w_out_out[part * size : (part + 1) * size, :] = sum_of(gots, keep, slice(base, base + size))
        for step in range(steps):
            at = base + size + step * in_rows
            cols = slice((part * steps + step) * chan, (part * steps + step + 1) * chan)
            w_in_out[:, cols] = sum_of(gots, keep, slice(at, at + in_rows))


def last_conv_kernel(
    got,
    keep_a,
    small,
    keep_b,
    out,
    total,
    conv_bias,
    gain_one,
    bias_one,
    b_out,
    gain_two,
    bias_two,
    b_in,
):
    size = out.shape[1] // 2
    first = keep_a.shape[0] // out.shape[1]
    rest = out.shape[0] - first
    shift = keep_a.shape[0]
    for slot in range(out.shape[0]):
        for part in range(2):
            if slot < first:
                at = (part * first + slot) * size
                kept, base = keep_a, 0
            else:
                at = (part * rest + slot - first) * size
                kept, base = keep_b, shift
            theirs = got[base + at : base + at + size, :].astype(F32)
            out[slot, part * size : (part + 1) * size, :] = kept[at : at + size, :] + theirs
    total[...] = small[...] + load_small(got, shift + keep_b.shape[0], small.shape[0])
    lanes = small.shape[1]
    owner = lax.axis_index("dp") * lax.axis_size("tap") + lax.axis_index("tap")
    width = b_out.shape[1]
    turned = pltpu.roll(total[...], (lanes - owner * width) % lanes, 1)
    for at, target in (
        (0, b_out),
        (1, gain_two),
        (2, bias_two),
        (8, conv_bias),
        (9, gain_one),
        (10, bias_one),
    ):
        target[...] = turned[at : at + 1, 0:width]
    width = b_in.shape[1]
    start = owner * width
    line = total[pl.ds(3 + start // lanes, 1), :]
    line = pltpu.roll(jnp.broadcast_to(line, (8, lanes)), (lanes - start % lanes) % lanes, 1)
    b_in[...] = line[0:1, 0:width]


def params(mib):
    return pltpu.CompilerParams(vmem_limit_bytes=mib * MIB)


def claim(micros):
    return pl.CostEstimate(flops=int(micros * 1.1e9), bytes_accessed=1, transcendentals=0)


def after_kernel(_, token, out):
    del token, out


def after(value, token, claimed=0):
    return pl.pallas_call(
        after_kernel,
        out_shape=pltpu.VMEM(value.shape, value.dtype),
        in_specs=[VMEM] * 2,
        out_specs=VMEM,
        input_output_aliases={0: 0},
        compiler_params=params(4),
        cost_estimate=claim(claimed),
        name="after",
    )(near(value), near(token))


def far(value):
    return pltpu.with_memory_space_constraint(value, pltpu.HBM)


def near(value):
    return pltpu.with_memory_space_constraint(value, pltpu.VMEM)


def fused_step(gots, flows, plans, sizes, token):
    lanes = flows[0]["keep"].shape[1]
    operands = [near(got) for got in gots]
    outs = []
    for flow, plan in zip(flows, plans):
        plan["with_small"] = "small_in" in plan
        operands.append(near(flow["keep"]))
        outs.append(pltpu.VMEM((flow["keep"].shape[0] // 2, lanes), F32))
        if plan["with_small"]:
            operands.append(near(flow["small"]))
            outs.append(pltpu.VMEM(flow["small"].shape, F32))
    operands.append(near(token))
    kept = len(outs)
    outs += [pltpu.VMEM((rows, lanes), BF16) for rows in sizes]
    out = pl.pallas_call(
        functools.partial(fused_kernel, len(gots), plans),
        out_shape=outs,
        in_specs=[VMEM] * len(operands),
        out_specs=[VMEM] * len(outs),
        compiler_params=params(4),
        cost_estimate=claim(0),
        name="step",
    )(*operands)
    at = 0
    for flow, plan in zip(flows, plans):
        flow["keep"] = out[at]
        at += 1
        if plan["with_small"]:
            flow["small"] = out[at]
            at += 1
    return out[kept:]


def swap(value, mask):
    count = lax.axis_size("dp") * lax.axis_size("tap")
    return lax.ppermute(value, ("dp", "tap"), [(i, i ^ mask) for i in range(count)])


def cut_kernel(weight_hbm, piece, sems):
    rows = piece.shape[1]
    start = (lax.axis_index("dp") & 7) * rows
    copies = [
        pltpu.make_async_copy(
            weight_hbm.at[slot, rows_at(start, rows), :], piece.at[slot], sems.at[slot]
        )
        for slot in range(piece.shape[0])
    ]
    for copy in copies:
        copy.start()
    wait_all(copies)


def cut_piece(conv_weight):
    slots, chan, width = conv_weight.shape
    return pl.pallas_call(
        cut_kernel,
        out_shape=pltpu.VMEM((slots, chan // 8, width), BF16),
        in_specs=[HBM],
        out_specs=VMEM,
        scratch_shapes=[pltpu.SemaphoreType.DMA((slots,))],
        compiler_params=params(4),
        cost_estimate=claim(0),
        name="cut_piece",
    )(far(conv_weight))


def both_kernel(over_one, over_two, _, both):
    slots = over_one.shape[0]
    both[0:slots] = over_one[...]
    both[slots:] = over_two[...]


def fetch_pieces(first, straight, token):
    over_one = swap_dp(first, 1)
    over_two = swap_dp(first, 2)
    straight = swap_tap(after(straight, first))
    slots = first.shape[0]
    both = pl.pallas_call(
        both_kernel,
        out_shape=pltpu.VMEM((2 * slots,) + first.shape[1:], BF16),
        in_specs=[VMEM] * 3,
        out_specs=VMEM,
        compiler_params=params(4),
        cost_estimate=claim(0),
        name="both",
    )(near(over_one), near(over_two), near(token))
    return [
        ((0,), first),
        ((2, 4), both),
        ((6,), straight),
        ((1,), swap_dp(first, 0)),
        ((3, 5), swap_dp(both, 0)),
        ((7,), swap_dp(straight, 0)),
    ]


def fast_shards(
    block_input,
    conv_weight,
    slot_tap_table,
    conv_bias,
    conv_norm_gain,
    conv_norm_bias,
    w_in,
    b_in,
    w_out,
    b_out,
    ffn_norm_gain,
    ffn_norm_bias,
    species_id,
    species_count,
    out_grad,
):
    tap_count = lax.axis_size("tap")
    dp_bits = (lax.axis_size("dp") - 1).bit_length()
    rows_dev = block_input.shape[0] // tap_count
    chan = block_input.shape[1]
    hid = w_in.shape[1]
    windows = rows_dev // WINDOW_LENGTH
    slots = conv_weight.shape[0]
    vmem = pltpu.VMEM
    line = list(range(2, dp_bits))
    orders = (["t", 1] + line, [1, "t"] + line)
    orders_b = ([2, "t", 1] + line[1:], [2, 1, "t"] + line[1:])
    over_x, over_y = 1, 4
    pad_shape = (windows, WINDOW_LENGTH + 2 * PAD, chan)
    rows_f = (rows_dev, chan)
    small_cost = claim(0)

    def row(vector):
        return vector.reshape(1, -1)

    piece = cut_piece(conv_weight)
    weight_shape = conv_weight.shape
    tiles = rows_dev // TILE
    dma = pltpu.SemaphoreType.DMA
    first = swap_tap(piece)
    x_pad, own_weight, w_in_near, straight = pl.pallas_call(
        load_kernel,
        out_shape=[
            vmem(pad_shape, BF16),
            vmem(weight_shape, BF16),
            vmem(w_in.shape, BF16),
            vmem((slots * chan // 8 + TABLE_ROWS, chan), BF16),
        ],
        in_specs=[SMEM] + [HBM] * 3,
        out_specs=[VMEM] * 4,
        scratch_shapes=[dma((windows + 2 * slots + 4,))],
        compiler_params=params(8),
        cost_estimate=claim(0),
        name="load",
    )(slot_tap_table, far(block_input), far(conv_weight), far(w_in))
    first = after(first, x_pad)
    part, token = pl.pallas_call(
        own_conv_kernel,
        out_shape=[vmem(rows_f, F32), vmem((8, 128), F32)],
        in_specs=[SMEM] + [VMEM] * 3,
        out_specs=[VMEM] * 2,
        compiler_params=params(8),
        cost_estimate=claim(0),
        name="own_conv",
    )(slot_tap_table, near(x_pad), near(own_weight), near(first))
    pieces = fetch_pieces(first, straight, token)

    block_f = (hid + chan * hid // COLS) >> (dp_bits + 1)
    half_f = block_f << dp_bits
    main = pl.pallas_call(
        functools.partial(main_kernel, orders, dp_bits, [turn for turn, _ in pieces]),
        out_shape=[
            pltpu.HBM(rows_f, BF16),
            vmem(rows_f, F32),
            vmem(rows_f, F32),
            vmem((rows_dev, hid), BF16),
            vmem(conv_weight.shape, BF16),
            vmem((half_f, chan), F32),
            vmem((half_f, chan), BF16),
            vmem((8, chan), F32),
            vmem(rows_f, BF16),
            jax.ShapeDtypeStruct((slots,), jnp.int32),
        ],
        in_specs=[SMEM] * 2 + [VMEM] * 2 + [HBM, VMEM, HBM] + [VMEM] * (7 + len(pieces)),
        out_specs=[HBM] + [VMEM] * 8 + [SMEM],
        scratch_shapes=[
            vmem(w_out.shape, BF16),
            vmem(rows_f, F32),
            vmem(rows_f, BF16),
            vmem((rows_dev, hid), BF16),
            vmem((rows_dev, hid), F32),
            vmem(rows_f, BF16),
            vmem(rows_f, BF16),
            vmem((2, COLS, chan), F32),
            vmem((8, 8, chan), F32),
            dma,
            dma((12,)),
        ],
        compiler_params=params(34),
        cost_estimate=small_cost,
        name="main_rows",
    )(
        species_id,
        species_count,
        near(x_pad),
        near(part),
        far(out_grad),
        near(w_in_near),
        far(w_out),
        row(conv_bias),
        row(conv_norm_gain),
        row(conv_norm_bias),
        row(b_in),
        row(b_out),
        row(ffn_norm_gain),
        row(ffn_norm_bias),
        *[near(piece) for _, piece in pieces],
    )
    block_output, unit, slope, d_up, other_weight, keep_f, send_f, small_ffn = main[:8]
    grad_in, other_table = main[8:]
    got_f = swap_dp(send_f, 0)

    d_pad, d_hidden, small = pl.pallas_call(
        back_kernel,
        out_shape=[vmem(pad_shape, BF16), vmem(rows_f, F32), vmem((16, chan), F32)],
        in_specs=[SMEM] * 2 + [VMEM] * 7,
        out_specs=[VMEM] * 3,
        scratch_shapes=[vmem((8, 8, chan), F32)],
        compiler_params=params(8),
        cost_estimate=small_cost,
        name="back_rows",
    )(
        species_id,
        species_count,
        near(grad_in),
        near(w_in_near),
        near(d_up),
        near(unit),
        near(slope),
        row(conv_norm_gain),
        near(small_ffn),
    )
    flow_f = dict(keep=keep_f)
    rows = keep_f.shape[0] // 2
    plan = dict(ins=[(0, 0), (0, rows)], outs=[(0, 0), (1, 0)])
    sends_f = fused_step([got_f], [flow_f], [plan], [rows // 2] * 2, small)
    gots_f = [swap(sends_f[0], over_x), swap(sends_f[1], over_y)]

    def terms(group, orders, token, small, name):
        count = len(group) * chan
        extra = 0 if small is None else 2 * small.shape[0]
        outs = [vmem((count, chan), F32), vmem((count + extra, chan), BF16)]
        scratch = [vmem((2, chan, chan), F32)]
        more = [] if small is None else [near(small)]
        return pl.pallas_call(
            functools.partial(terms_kernel, group, orders, dp_bits, small is not None),
            out_shape=outs,
            in_specs=[SMEM] * 2 + [VMEM] * (3 + len(more)),
            out_specs=[VMEM] * len(outs),
            scratch_shapes=scratch,
            compiler_params=params(8),
            cost_estimate=small_cost,
            name=name,
        )(slot_tap_table, other_table, near(x_pad), near(d_pad), *more, near(token))

    cut = (slots * 3 + 4) // 5
    keep_a, send_a = terms(range(0, cut), orders, sends_f[0], None, "terms_a")
    got_a = swap_dp(send_a, 0)
    keep_b, send_b = terms(range(cut, slots), orders_b, keep_a, small, "terms_b")
    got_b = swap_dp(send_b, 0)
    def spaced(token, claimed=1):
        return after(mark, token, claimed)

    mark = token
    flow_a = dict(keep=keep_a)
    flow_b = dict(keep=keep_b, small=small)
    extra = 2 * small.shape[0]
    over_z, over_zz = 2 << line[0], 2 << line[1]

    def half_of(flow):
        return flow["keep"].shape[0] // 4

    def joined(base, flow):
        return [(0, base), (0, base + 2 * half_of(flow))]

    size = half_of(flow_f)
    plan = dict(ins=[(0, 0), (1, 0)], outs=[(0, 0), (1, 0)])
    sends = fused_step(gots_f, [flow_f], [plan], [size] * 2, keep_b)
    gots_f = [swap(sends[0], over_y), swap(sends[1], over_x)]
    mark = spaced(flow_f["keep"], 100)
    size = half_of(flow_b)
    plan = dict(
        ins=joined(0, flow_b),
        small_in=(0, 4 * size),
        outs=[(0, 0), (0, size)],
        small_out=(0, 2 * size),
    )
    sends = fused_step([got_b], [flow_b], [plan], [2 * size + extra], mark)
    got_b = swap(sends[0], over_z)
    partial = pl.pallas_call(
        input_near_kernel,
        out_shape=vmem(rows_f, F32),
        in_specs=[SMEM] + [VMEM] * 4,
        out_specs=VMEM,
        compiler_params=params(8),
        cost_estimate=claim(0),
        name="input_near",
    )(slot_tap_table, near(d_pad), near(d_hidden), near(own_weight), near(flow_b["keep"]))
    size = half_of(flow_f)
    plan = dict(ins=[(0, 0), (1, 0)], outs=[(0, 0), (0, size)])
    sends = fused_step(gots_f, [flow_f], [plan], [2 * size], partial)
    got_f = swap(sends[0], over_z)
    mark = spaced(flow_f["keep"])
    size = half_of(flow_a)
    plan = dict(ins=joined(0, flow_a), outs=[(0, 0), (1, 0)])
    sends = fused_step([got_a], [flow_a], [plan], [size] * 2, mark)
    gots_a = [swap(sends[0], over_x), swap(sends[1], over_y)]
    input_grad, mark = pl.pallas_call(
        input_far_kernel,
        out_shape=[pltpu.HBM(rows_f, F32), vmem((8, 128), F32)],
        in_specs=[SMEM] + [VMEM] * 4,
        out_specs=[HBM, VMEM],
        scratch_shapes=[vmem(rows_f, F32), pltpu.SemaphoreType.DMA((rows_dev // TILE,))],
        compiler_params=params(8),
        cost_estimate=small_cost,
        name="input_far",
    )(other_table, near(d_pad), near(partial), near(other_weight), near(flow_a["keep"]))
    mark = spaced(mark)
    size, size_b = half_of(flow_a), half_of(flow_b)
    plan = dict(ins=[(0, 0), (1, 0)], outs=[(0, 0), (1, 0)])
    plan_b = dict(
        ins=[(2, 0), (2, 2 * size_b)],
        small_in=(2, 4 * size_b),
        outs=[(1, size), (0, size)],
        small_out=(1, size + size_b),
    )
    sends = fused_step(
        gots_a + [got_b],
        [flow_a, flow_b],
        [plan, plan_b],
        [size + size_b, size + size_b + extra],
        mark,
    )
    gots = [swap(sends[0], over_y), swap(sends[1], over_x)]
    shift = size
    mark = spaced(flow_a["keep"])
    size = half_of(flow_f)
    plan = dict(ins=joined(0, flow_f), outs=[(0, 0), (0, size)])
    sends = fused_step([got_f], [flow_f], [plan], [2 * size], mark)
    got_f = swap(sends[0], over_zz)
    mark = spaced(flow_f["keep"])
    size = half_of(flow_a)
    plan = dict(ins=[(0, 0), (1, 0)], outs=[(0, 0), (0, size)])
    sends = fused_step(gots, [flow_a], [plan], [2 * size], mark)
    got_a = swap(sends[0], over_z)
    size = half_of(flow_b)
    plan = dict(
        ins=[(1, shift), (0, shift)],
        small_in=(1, shift + 2 * size),
        outs=[(0, 0), (1, 0)],
        small_out=(0, size),
    )
    sends = fused_step(gots, [flow_b], [plan], [size + extra, size], flow_a["keep"])
    gots_b = [swap(sends[0], over_y), swap(sends[1], over_x)]
    mark = flow_b["keep"]
    w_in_mine, w_out_mine, mark = pl.pallas_call(
        functools.partial(last_ffn_kernel, 1),
        out_shape=[
            jax.ShapeDtypeStruct((chan >> (dp_bits + 1), hid), F32),
            jax.ShapeDtypeStruct((hid >> (dp_bits + 1), chan), F32),
            vmem((8, 128), F32),
        ],
        in_specs=[VMEM] * 3,
        out_specs=[VMEM] * 3,
        compiler_params=params(4),
        cost_estimate=claim(0),
        name="last_ffn",
    )(near(got_f), near(flow_f["keep"]), near(mark))
    mark = spaced(mark)
    size, size_b = half_of(flow_a), half_of(flow_b)
    plan = dict(ins=joined(0, flow_a), outs=[(0, 0), (0, size)])
    shift = 2 * size
    plan_b = dict(
        ins=[(1, 0), (2, 0)],
        small_in=(1, 2 * size_b),
        outs=[(0, shift), (0, shift + size_b)],
        small_out=(0, shift + 2 * size_b),
    )
    sends = fused_step(
        [got_a] + gots_b, [flow_a, flow_b], [plan, plan_b], [shift + 2 * size_b + extra], mark
    )
    got = swap(sends[0], over_zz)
    width = chan >> (dp_bits + 1)
    wide = hid >> (dp_bits + 1)
    small = flow_b["small"]
    conv_weight_grad, _, *vectors = pl.pallas_call(
        last_conv_kernel,
        out_shape=[
            jax.ShapeDtypeStruct((slots, chan >> dp_bits, chan), F32),
            vmem(small.shape, F32),
        ]
        + [jax.ShapeDtypeStruct((1, width), F32)] * 6
        + [jax.ShapeDtypeStruct((1, wide), F32)],
        in_specs=[VMEM] * 4,
        out_specs=[VMEM] * 9,
        compiler_params=params(4),
        cost_estimate=claim(0),
        name="last_conv",
    )(near(got), near(flow_a["keep"]), near(small), near(flow_b["keep"]))
    conv_bias_grad, gain_one_grad, bias_one_grad, b_out_grad, gain_two_grad, bias_two_grad, b_in_grad = [
        vector.reshape(-1) for vector in vectors
    ]
    return (
        block_output,
        input_grad,
        conv_weight_grad,
        conv_bias_grad,
        gain_one_grad,
        bias_one_grad,
        w_in_mine,
        b_in_grad,
        w_out_mine,
        b_out_grad,
        gain_two_grad,
        bias_two_grad,
    )


def narrow_enough(mesh):
    return mesh.shape["tap"] == 2 and mesh.shape["dp"] == 16


def solution(mesh):
    chosen = fast_shards if narrow_enough(mesh) else plain_shards
    return jax.shard_map(
        chosen,
        mesh=mesh,
        in_specs=(
            P("dp", None),
            P("tap", None, None),
            P("tap"),
            P(),
            P(),
            P(),
            P(),
            P(),
            P(),
            P(),
            P(),
            P(),
            P("dp"),
            P(),
            P(("dp", "tap"), None),
        ),
        out_specs=(
            P(("dp", "tap"), None),
            P(("dp", "tap"), None),
            P("tap", "dp", None),
            P(("dp", "tap")),
            P(("dp", "tap")),
            P(("dp", "tap")),
            P(("dp", "tap"), None),
            P(("dp", "tap")),
            P(("dp", "tap"), None),
            P(("dp", "tap")),
            P(("dp", "tap")),
            P(("dp", "tap")),
        ),
        check_vma=False,
    )
```

```python
import functools

import jax
import jax.numpy as jnp
from jax import lax
from jax.experimental import pallas as pl
from jax.experimental.pallas import tpu as pltpu
from jax.sharding import PartitionSpec as P

KERNEL_TAPS = 9
DILATION_STEP = 16
WINDOW_LENGTH = 512


def layer_norm(values):
    mean_val = jnp.mean(values, axis=-1, keepdims=True)
    center = values - mean_val
    spread = jnp.mean(center * center, axis=-1, keepdims=True)
    return center * lax.rsqrt(spread + 1e-05)


def exact_gelu(values):
    return jax.nn.gelu(values, approximate=False)


def conv_branch(pre_conv, gain_one, bias_one):
    return layer_norm(exact_gelu(pre_conv)) * gain_one + bias_one


def ffn_branch(pre_out, gain_two, bias_two):
    return layer_norm(pre_out) * gain_two + bias_two


def shift_stack(win_rows, tap_table, forward):
    tap_extent = KERNEL_TAPS // 2 * DILATION_STEP
    padded_input = jnp.pad(win_rows, ((0, 0), (tap_extent, tap_extent), (0, 0)))
    pieces = []
    for index_of_slot in range(tap_table.shape[0]):
        if forward:
            tap_offset = tap_table[index_of_slot]
        else:
            tap_offset = KERNEL_TAPS - 1 - tap_table[index_of_slot]
        shifted_input = lax.dynamic_slice_in_dim(
            padded_input, tap_offset * DILATION_STEP, WINDOW_LENGTH, 1
        )
        pieces.append(shifted_input.reshape(-1, win_rows.shape[2]))
    return jnp.stack(pieces)


def contract_rows(left, right):
    return lax.dot_general(
        left, right, (((0,), (0,)), ((), ())), preferred_element_type=jnp.float32
    )


def contract_cols(left, right):
    return lax.dot_general(
        left, right, (((1,), (1,)), ((), ())), preferred_element_type=jnp.float32
    )


def swap_dp(value, bit):
    count = lax.axis_size("dp")
    return lax.ppermute(value, "dp", [(i, i ^ (1 << bit)) for i in range(count)])


def swap_tap(value):
    return lax.ppermute(value, "tap", [(0, 1), (1, 0)])


def halve(part, order, kind):
    dp_bits = (lax.axis_size("dp") - 1).bit_length()
    place = lax.axis_index("dp")
    tap = lax.axis_index("tap")
    labels = ["t"] + list(range(dp_bits - 1, -1, -1))
    for step in order:
        axis = labels.index(step)
        labels.pop(axis)
        mine = tap if step == "t" else (place >> step) & 1
        keep = lax.dynamic_index_in_dim(part, mine, axis, keepdims=False)
        send = lax.dynamic_index_in_dim(part, 1 - mine, axis, keepdims=False).astype(kind)
        got = swap_tap(send) if step == "t" else swap_dp(send, step)
        part = keep + got.astype(jnp.float32)
    return part


def orders(dp_bits):
    rest = list(range(2, dp_bits))
    first = [0, "t", 1] + rest
    second = [0, 1] + rest[:1] + ["t"] + rest[1:]
    third = [0] + rest[:1] + ["t", 1] + rest[1:]
    return first, second, third


def plain_shards(
    block_input,
    conv_weight,
    slot_tap_table,
    conv_bias,
    conv_norm_gain,
    conv_norm_bias,
    w_in,
    b_in,
    w_out,
    b_out,
    ffn_norm_gain,
    ffn_norm_bias,
    species_id,
    species_count,
    out_grad,
):
    tap_count = lax.axis_size("tap")
    my_index = lax.axis_index("tap")
    core = lax.axis_index("dp") & 1
    dp_bits = (lax.axis_size("dp") - 1).bit_length()
    tok_dev, chan_width = block_input.shape
    hid_width = w_in.shape[1]
    half_rows = tok_dev // tap_count
    windows = tok_dev // WINDOW_LENGTH
    my_windows = windows // tap_count
    own_slots = conv_weight.shape[0]
    half_chan = chan_width // 2
    first, second, third = orders(dp_bits)

    other_table = swap_tap(slot_tap_table)
    part_send = lax.dynamic_slice_in_dim(conv_weight, core * half_chan, half_chan, 1)
    part_here = swap_tap(part_send)
    part_mate = swap_dp(part_here, 0)
    low_part = jnp.where(core == 0, part_here, part_mate)
    high_part = jnp.where(core == 0, part_mate, part_here)
    other_weight = jnp.concatenate([low_part, high_part], axis=1)

    my_x = lax.dynamic_slice_in_dim(block_input, my_index * half_rows, half_rows, 0)
    x_windows = my_x.reshape(my_windows, WINDOW_LENGTH, chan_width)
    mine_x = my_x.astype(jnp.float32)
    own_stack = shift_stack(x_windows, slot_tap_table, True)
    other_stack = shift_stack(x_windows, other_table, True)
    conv_out = jnp.einsum("str,sro->to", own_stack, conv_weight, preferred_element_type=jnp.float32)
    conv_out = conv_out + jnp.einsum(
        "str,sro->to", other_stack, other_weight, preferred_element_type=jnp.float32
    )
    pre_conv = conv_out + conv_bias
    norm_one, conv_back = jax.vjp(conv_branch, pre_conv, conv_norm_gain, conv_norm_bias)
    hidden = mine_x + norm_one
    hidden_low = hidden.astype(jnp.bfloat16)
    pre_up = jnp.dot(hidden_low, w_in, preferred_element_type=jnp.float32) + b_in
    activ, activ_back = jax.vjp(exact_gelu, pre_up)
    act_low = activ.astype(jnp.bfloat16)
    pre_out = jnp.dot(act_low, w_out, preferred_element_type=jnp.float32) + b_out
    norm_two, ffn_back = jax.vjp(ffn_branch, pre_out, ffn_norm_gain, ffn_norm_bias)
    block_output = (hidden + norm_two).astype(jnp.bfloat16)
    my_species = lax.dynamic_slice_in_dim(species_id, my_index * my_windows, my_windows, 0)
    species_range = jnp.arange(species_count.shape[0], dtype=jnp.int32)
    matches = my_species[:, None] == species_range[None, :]
    window_count = jnp.sum(jnp.where(matches, species_count[None, :], 0), axis=1)
    window_scale = 4.0 / window_count.astype(jnp.float32)
    grad_y = (
        out_grad.astype(jnp.float32).reshape(my_windows, WINDOW_LENGTH, chan_width)
        * window_scale[:, None, None]
    ).reshape(half_rows, chan_width)
    d_pre_out, d_gain_two, d_bias_two = ffn_back(grad_y)
    d_out_low = d_pre_out.astype(jnp.bfloat16)
    d_w_out = contract_rows(act_low, d_out_low)
    d_b_out = jnp.sum(d_out_low.astype(jnp.float32), axis=0)
    d_activ = contract_cols(d_out_low, w_out)
    (d_pre_up,) = activ_back(d_activ)
    d_up_low = d_pre_up.astype(jnp.bfloat16)
    d_w_in = contract_rows(hidden_low, d_up_low)
    d_b_in = jnp.sum(d_up_low.astype(jnp.float32), axis=0)
    d_hidden = grad_y + contract_cols(d_up_low, w_in)
    d_pre_conv, d_gain_one, d_bias_one = conv_back(d_hidden)
    d_conv_low = d_pre_conv.astype(jnp.bfloat16)
    d_conv_bias = jnp.sum(d_conv_low.astype(jnp.float32), axis=0)
    d_windows = d_conv_low.reshape(my_windows, WINDOW_LENGTH, chan_width)
    own_back = shift_stack(d_windows, slot_tap_table, False)
    other_back = shift_stack(d_windows, other_table, False)
    input_grad = (
        d_hidden
        + jnp.einsum("sto,sro->tr", own_back, conv_weight, preferred_element_type=jnp.float32)
        + jnp.einsum("sto,sro->tr", other_back, other_weight, preferred_element_type=jnp.float32)
    )
    own_terms = jnp.einsum("str,to->sro", own_stack, d_conv_low, preferred_element_type=jnp.float32)
    other_terms = jnp.einsum(
        "str,to->sro", other_stack, d_conv_low, preferred_element_type=jnp.float32
    )
    bits = [2] * dp_bits

    def by_tap(own, other):
        return jnp.where(my_index == 0, jnp.stack([own, other]), jnp.stack([other, own]))

    def conv_part(begin, end, order):
        own = own_terms[begin:end]
        other = other_terms[begin:end]
        both = by_tap(own, other)
        rows = chan_width >> dp_bits
        both = both.reshape([2, end - begin] + bits + [rows, chan_width])
        return halve(jnp.moveaxis(both, 1, 1 + dp_bits), order, jnp.bfloat16)

    cut = own_slots * 2 // 5
    conv_weight_grad = jnp.concatenate(
        [
            conv_part(0, cut, first),
            conv_part(cut, 2 * cut, second),
            conv_part(2 * cut, own_slots, third),
        ]
    )

    def spread(total, order, kind):
        rows = total.shape[0] >> (dp_bits + 1)
        split = total.reshape(bits + [2, rows] + list(total.shape[1:]))
        return halve(jnp.moveaxis(split, dp_bits, 0), order, kind)

    d_w_out_mine = spread(d_w_out, first, jnp.bfloat16)
    d_w_in_mine = spread(d_w_in, second, jnp.bfloat16)
    owners = 2 << dp_bits
    small = [d_b_in, d_b_out, d_conv_bias, d_gain_one, d_bias_one, d_gain_two, d_bias_two]
    joined = jnp.concatenate([v.reshape(owners, -1) for v in small], axis=1)
    joined_mine = spread(joined, third, jnp.float32).reshape(-1)
    vectors = []
    start = 0
    for v in small:
        size = v.shape[0] // owners
        vectors.append(joined_mine[start : start + size])
        start += size
    return (
        block_output,
        input_grad,
        conv_weight_grad,
        vectors[2],
        vectors[3],
        vectors[4],
        d_w_in_mine,
        vectors[0],
        d_w_out_mine,
        vectors[1],
        vectors[5],
        vectors[6],
    )


TILE = 512
COLS = 512
PAD = KERNEL_TAPS // 2 * DILATION_STEP
MIB = 2**20
TABLE_ROWS = 16
F32 = jnp.float32
BF16 = jnp.bfloat16
HBM = pl.BlockSpec(memory_space=pltpu.HBM)
VMEM = pl.BlockSpec(memory_space=pltpu.VMEM)
SMEM = pl.BlockSpec(memory_space=pltpu.SMEM)


def dot_plain(left, right):
    return lax.dot_general(left, right, (((1,), (0,)), ((), ())), preferred_element_type=F32)


def gelu_and_slope(value):
    cdf = 0.5 + 0.5 * lax.erf(value * 0.7071067811865476)
    density = jnp.exp2(value * value * -0.7213475204444817)
    return value * cdf, cdf + (value * 0.3989422804014327) * density


def norm_parts(value):
    center = value - jnp.mean(value, axis=-1, keepdims=True)
    spread = jnp.mean(center * center, axis=-1, keepdims=True)
    scale = lax.rsqrt(spread + 1e-05)
    return center * scale, scale


def norm_back(grad, unit):
    return grad - jnp.mean(grad, axis=-1, keepdims=True) - unit * jnp.mean(
        grad * unit, axis=-1, keepdims=True
    )


def fold_rows(value):
    return jnp.sum(value.reshape(value.shape[0] // 8, 8, value.shape[1]), axis=0)


def one_row(value):
    return jnp.sum(value, axis=0, keepdims=True)


def my_bits(dp_bits):
    place = lax.axis_index("dp")
    mine = {bit: (place >> bit) & 1 for bit in range(dp_bits)}
    mine["t"] = lax.axis_index("tap")
    return mine


def relative(order, owner, mine):
    spot = 0
    for label in order:
        spot = spot * 2 + (owner[label] ^ mine[label])
    return spot


def rows_at(start, size):
    return pl.ds(pl.multiple_of(start, 16), size)


def split_copy(source, target, sems, first):
    rows = target.shape[0] // 4
    return [
        pltpu.make_async_copy(
            source.at[at * rows : (at + 1) * rows, :],
            target.at[at * rows : (at + 1) * rows, :],
            sems.at[first + at],
        )
        for at in range(4)
    ]


def wait_all(copies):
    for copy in copies:
        copy.wait()


def clear_pads(pad_ref):
    zeros = jnp.zeros((PAD, pad_ref.shape[2]), pad_ref.dtype)
    for win in range(pad_ref.shape[0]):
        pad_ref[win, 0:PAD, :] = zeros
        pad_ref[win, PAD + WINDOW_LENGTH :, :] = zeros


def each_tile(rows, body, together=1):
    per = WINDOW_LENGTH // TILE

    @pl.loop(0, rows // TILE // together)
    def _(step):
        for member in range(together):
            number = step * together + member
            body(rows_at(number * TILE, TILE), number // per, (number % per) * TILE)


def window_weight(species, counts, win, windows, lanes):
    kind = species[lax.axis_index("tap") * windows + win]
    count = jnp.full((8, lanes), counts[kind], jnp.int32).astype(F32)
    return (4.0 / count)[0:1, :]


def load_kernel(
    table, x_hbm, weight_hbm, w_in_hbm, x_pad, weight, w_in, straight, sems
):
    windows = x_pad.shape[0]
    slots = weight.shape[0]
    rows = weight.shape[1] // 8
    base = lax.axis_index("tap") * windows * WINDOW_LENGTH
    start = ((lax.axis_index("dp") & 7) ^ 6) * rows
    copies = []
    for slot in range(slots):
        source = weight_hbm.at[slot, rows_at(start, rows), :]
        copies.append((source, straight.at[slot * rows : (slot + 1) * rows, :]))
    for win in range(windows):
        source = x_hbm.at[rows_at(base + win * WINDOW_LENGTH, WINDOW_LENGTH), :]
        copies.append((source, x_pad.at[win, PAD : PAD + WINDOW_LENGTH, :]))
    copies += [(weight_hbm.at[slot], weight.at[slot]) for slot in range(slots)]
    copies = [
        pltpu.make_async_copy(source, target, sems.at[at])
        for at, (source, target) in enumerate(copies)
    ]
    copies += split_copy(w_in_hbm, w_in, sems, len(copies))
    for copy in copies:
        copy.start()
    at = lax.broadcasted_iota(jnp.int32, (TABLE_ROWS, straight.shape[1]), 0)
    taps = jnp.zeros(at.shape, jnp.int32)
    for slot in range(slots):
        taps = jnp.where(at == slot, table[slot], taps)
    straight[slots * rows :, :] = taps.astype(F32).astype(BF16)
    clear_pads(x_pad)
    wait_all(copies)


def own_conv_kernel(table, x_pad, weight, _, part, token):
    token[...] = jnp.zeros(token.shape, token.dtype)

    def convolve(rows, win, begin):
        total = None
        for slot in range(weight.shape[0]):
            shifted = rows_at(table[slot] * DILATION_STEP + begin, TILE)
            term = dot_plain(x_pad[win, shifted, :], weight[slot])
            total = term if total is None else total + term
        part[rows, :] = total

    each_tile(part.shape[0], convolve, 2)


def join_pieces(plan, pieces, weight):
    slots = weight.shape[0]
    rows = weight.shape[1] // 8
    place = lax.axis_index("dp") & 7
    for turns, piece in zip(plan, pieces):
        flat = len(piece.shape) == 2
        for number, turn in enumerate(turns):
            there = rows_at((place ^ turn) * rows, rows)
            if flat:
                for slot in range(slots):
                    weight[slot, there, :] = piece[slot * rows : (slot + 1) * rows, :]
            else:
                weight[:, there, :] = piece[number * slots : (number + 1) * slots]


def main_kernel(orders, dp_bits, turns, *refs):
    species, counts = refs[:2]
    x_pad, part, grad_hbm, w_in, w_out_hbm = refs[2:7]
    conv_bias, gain_one, bias_one, b_in, b_out, gain_two, bias_two = refs[7:14]
    pieces = refs[14 : 14 + len(turns)]
    y_hbm, unit, slope, d_up, weight, keep, send, small, grad_in, table = refs[
        14 + len(turns) : 24 + len(turns)
    ]
    w_out, hidden, low, act, hid_slope, d_out, y_low, result, sums, sem, sems = refs[24 + len(turns) :]
    told = pieces[turns.index((6,))]
    told_at = told.shape[0] - TABLE_ROWS
    taps = []
    for slot in range(weight.shape[0]):
        line = told[told_at : told_at + TABLE_ROWS, 0:128].astype(F32)
        chosen = lax.broadcasted_iota(jnp.int32, line.shape, 0) == slot
        taps.append(jnp.max(jnp.where(chosen, line, 0.0)).astype(jnp.int32))
        table[slot] = taps[slot]
    mine = my_bits(dp_bits)
    rows_dev, chan = hidden.shape
    hid_width = w_in.shape[1]
    windows = x_pad.shape[0]
    out_copies = split_copy(w_out_hbm, w_out, sems, 4)
    grad_copies = split_copy(grad_hbm, grad_in, sems, 8)
    for copy in out_copies + grad_copies:
        copy.start()
    join_pieces(turns, pieces, weight)
    sums[...] = jnp.zeros(sums.shape, F32)

    def first_norm(rows, win, begin):
        total = part[rows, :] + conv_bias[...]
        for slot in range(weight.shape[0]):
            shifted = rows_at(taps[slot] * DILATION_STEP + begin, TILE)
            total = total + dot_plain(x_pad[win, shifted, :], weight[slot])
        value, steep = gelu_and_slope(total)
        normed, scale = norm_parts(value)
        unit[rows, :] = normed
        slope[rows, :] = scale * steep
        here = x_pad[win, rows_at(PAD + begin, TILE), :].astype(F32)
        summed = here + (normed * gain_one[...] + bias_one[...])
        hidden[rows, :] = summed
        low[rows, :] = summed.astype(BF16)

    each_tile(rows_dev, first_norm, 2)

    def go_up(rows, win, begin):
        for at in range(0, hid_width, COLS):
            cols = slice(at, at + COLS)
            up = dot_plain(low[rows, :], w_in[:, cols]) + b_in[:, cols]
            value, steep = gelu_and_slope(up)
            act[rows, cols] = value.astype(BF16)
            hid_slope[rows, cols] = steep

    each_tile(rows_dev, go_up, 2)
    wait_all(out_copies + grad_copies)

    def second_norm(rows, win, begin):
        pre_out = dot_plain(act[rows, :], w_out[...]) + b_out[...]
        normed, scale = norm_parts(pre_out)
        result_rows = hidden[rows, :] + (normed * gain_two[...] + bias_two[...])
        y_low[rows, :] = result_rows.astype(BF16)
        grad_y = grad_in[rows, :].astype(F32) * window_weight(species, counts, win, windows, chan)
        back = (norm_back(grad_y * gain_two[...], normed) * scale).astype(BF16)
        d_out[rows, :] = back
        sums[0] += fold_rows(back.astype(F32))
        sums[1] += fold_rows(grad_y * normed)
        sums[2] += fold_rows(grad_y)

    each_tile(rows_dev, second_norm, 2)
    y_copy = pltpu.make_async_copy(y_low, y_hbm, sem)
    y_copy.start()

    def go_down(rows, win, begin):
        for number, at in enumerate(range(0, hid_width, COLS)):
            cols = slice(at, at + COLS)
            d_act = contract_cols(d_out[rows, :], w_out[cols, :])
            back = (d_act * hid_slope[rows, cols]).astype(BF16)
            d_up[rows, cols] = back
            sums[3 + number] += fold_rows(back.astype(F32))

    each_tile(rows_dev, go_down, 2)
    for number in range(8):
        small[number : number + 1, :] = one_row(sums[number])
    core = mine[0]
    out_block = hid_width >> (dp_bits + 1)
    in_block = chan >> (dp_bits + 1)
    chunks = hid_width // COLS
    half = (out_block + chunks * in_block) // 2

    def hand_out(spot, first_row, block, targets):
        for start in range(0, result.shape[1], 4 * block):
            owner_at = first_row // block + start // block
            for tap in range(2):
                owner = {bit: (owner_at >> (bit + 1)) & 1 for bit in range(1, dp_bits)}
                owner["t"] = tap
                inner = start + tap * block
                for part_at, source, size, shift in targets:
                    spread = relative(orders[part_at], owner, mine) + (part_at << dp_bits)
                    place = rows_at(spread * half + shift, size)
                    mine_at = rows_at(inner + source + core * 2 * block, size)
                    other_at = rows_at(inner + source + (1 - core) * 2 * block, size)
                    keep[place, :] = result[spot, mine_at, :]
                    send[place, :] = result[spot, other_at, :].astype(BF16)

    size = out_block // 2

    @pl.loop(0, chunks // 2)
    def _(pair):
        for spot in range(2):
            at = pl.multiple_of((pair * 2 + spot) * COLS, COLS)
            result[spot] = contract_rows(act[:, pl.ds(at, COLS)], d_out[...])
            hand_out(spot, at, out_block, [(0, 0, size, 0), (1, size, size, 0)])

    @pl.loop(0, chunks // 2)
    def _(step):
        shift = size + step * in_block
        for spot in range(2):
            at = pl.multiple_of((spot * (chunks // 2) + step) * COLS, COLS)
            result[spot] = contract_rows(low[...], d_up[:, pl.ds(at, COLS)])
            hand_out(spot, 0, in_block, [(spot, 0, in_block, shift)])

    y_copy.wait()


def back_kernel(
    species,
    counts,
    grad_in,
    w_in,
    d_up,
    unit,
    slope,
    gain_one,
    small_in,
    d_pad,
    d_hidden,
    small,
    sums,
):
    windows = d_pad.shape[0]
    chan = d_hidden.shape[1]
    clear_pads(d_pad)
    sums[...] = jnp.zeros(sums.shape, F32)

    def through_norm(rows, win, begin):
        grad = grad_in[rows, :].astype(F32) * window_weight(species, counts, win, windows, chan)
        grad = grad + contract_cols(d_up[rows, :], w_in[...])
        d_hidden[rows, :] = grad
        normed = unit[rows, :]
        back = (norm_back(grad * gain_one[...], normed) * slope[rows, :]).astype(BF16)
        d_pad[win, rows_at(PAD + begin, TILE), :] = back
        sums[0] += fold_rows(back.astype(F32))
        sums[1] += fold_rows(grad * normed)
        sums[2] += fold_rows(grad)

    each_tile(d_hidden.shape[0], through_norm, 2)
    small[0:8, :] = small_in[...]
    for number in range(8):
        small[8 + number : 9 + number, :] = one_row(sums[number])


def store_small(total, ref, first):
    ref[first : first + total.shape[0], :] = total.astype(BF16)


def load_small(ref, first, count):
    return ref[first : first + count, :].astype(F32)


def terms_kernel(slots, orders, dp_bits, with_small, own_table, other_table, x_pad, d_pad, *refs):
    if with_small:
        small, _, keep, send, result = refs
        store_small(small[...], send, keep.shape[0])
    else:
        _, keep, send, result = refs
    mine = my_bits(dp_bits)
    rows = x_pad.shape[2] >> dp_bits
    core = mine[0]
    tables = (own_table, other_table)
    size = rows // 2

    @pl.loop(0, len(slots))
    def _(number):
        for near_tap in range(2):
            tap = tables[near_tap][slots[0] + number]
            shifted = rows_at((KERNEL_TAPS - 1 - tap) * DILATION_STEP, WINDOW_LENGTH)
            total = None
            for win in range(x_pad.shape[0]):
                term = contract_rows(
                    x_pad[win, PAD : PAD + WINDOW_LENGTH, :], d_pad[win, shifted, :]
                )
                total = term if total is None else total + term
            result[near_tap] = total
            for start in range(0, x_pad.shape[2], 2 * rows):
                owner_at = start // rows
                owner = {bit: (owner_at >> bit) & 1 for bit in range(1, dp_bits)}
                owner["t"] = mine["t"] ^ near_tap
                for part_at in range(2):
                    spread = relative(orders[part_at], owner, mine) + (part_at << dp_bits)
                    place = rows_at((spread * len(slots) + number) * size, size)
                    mine_at = rows_at(start + core * rows + part_at * size, size)
                    other_at = rows_at(start + (1 - core) * rows + part_at * size, size)
                    keep[place, :] = result[near_tap, mine_at, :]
                    send[place, :] = result[near_tap, other_at, :].astype(BF16)


def input_sum(table, d_pad, base, weight, rows, win, begin):
    total = base[rows, :]
    for slot in range(weight.shape[0]):
        shifted = rows_at((KERNEL_TAPS - 1 - table[slot]) * DILATION_STEP + begin, TILE)
        total = total + contract_cols(d_pad[win, shifted, :], weight[slot])
    return total


def input_near_kernel(table, d_pad, base, weight, _, out):
    def gather(rows, win, begin):
        out[rows, :] = input_sum(table, d_pad, base, weight, rows, win, begin)

    each_tile(out.shape[0], gather, 2)


def input_far_kernel(table, d_pad, base, weight, _, out_hbm, token, out, sems):
    token[...] = jnp.zeros(token.shape, token.dtype)

    def copy_of(rows):
        return pltpu.make_async_copy(out.at[rows, :], out_hbm.at[rows, :], sems.at[0])

    def gather(rows, win, begin):
        out[rows, :] = input_sum(table, d_pad, base, weight, rows, win, begin)
        copy_of(rows).start()

    each_tile(out.shape[0], gather, 2)
    pltpu.make_async_copy(out, out_hbm, sems.at[0]).wait()


def fused_kernel(got_count, plans, *refs):
    gots = refs[:got_count]
    at = got_count
    inputs = []
    for plan in plans:
        inputs.append(refs[at : at + 1 + plan["with_small"]])
        at += 1 + plan["with_small"]
    at += 1
    kept = []
    for plan in plans:
        kept.append(refs[at : at + 1 + plan["with_small"]])
        at += 1 + plan["with_small"]
    sent = refs[at:]
    for plan, source, target in zip(plans, inputs, kept):
        keep = source[0]
        rows = keep.shape[0] // 2
        half = rows // 2
        for part in range(2):
            which, base = plan["ins"][part]
            out, spot = plan["outs"][part]
            start = part * rows
            theirs = gots[which][base + half : base + rows, :].astype(F32)
            total = keep[start + half : start + rows, :] + theirs
            sent[out][spot : spot + half, :] = total.astype(BF16)
            ours = gots[which][base : base + half, :].astype(F32)
            target[0][part * half : (part + 1) * half, :] = keep[start : start + half, :] + ours
        if plan["with_small"]:
            which, base = plan["small_in"]
            count = source[1].shape[0]
            total = source[1][...] + load_small(gots[which], base, count)
            target[1][...] = total
            out, spot = plan["small_out"]
            store_small(total, sent[out], spot)


def sum_of(gots, keep, rows):
    total = keep[rows, :]
    for got in gots:
        total = total + got[rows, :].astype(F32)
    return total


def finish_ffn(got, keep, w_in_out, w_out_out):
    out_rows, chan = w_out_out.shape
    in_rows = w_in_out.shape[0]
    half = keep.shape[0] // 2
    steps = w_in_out.shape[1] // chan // 2
    for part in range(2):
        base = part * half
        size = out_rows // 2
        w_out_out[part * size : (part + 1) * size, :] = sum_of([got], keep, slice(base, base + size))
        for step in range(steps):
            at = base + size + step * in_rows
            cols = slice((part * steps + step) * chan, (part * steps + step + 1) * chan)
            w_in_out[:, cols] = sum_of([got], keep, slice(at, at + in_rows))


def last_conv_kernel(
    got,
    keep_a,
    small,
    keep_b,
    got_f,
    keep_f,
    out,
    total,
    conv_bias,
    gain_one,
    bias_one,
    b_out,
    gain_two,
    bias_two,
    b_in,
    w_in_out,
    w_out_out,
):
    finish_ffn(got_f, keep_f, w_in_out, w_out_out)
    size = out.shape[1] // 2
    first = keep_a.shape[0] // out.shape[1]
    rest = out.shape[0] - first
    shift = keep_a.shape[0]
    for slot in range(out.shape[0]):
        for part in range(2):
            if slot < first:
                at = (part * first + slot) * size
                kept, base = keep_a, 0
            else:
                at = (part * rest + slot - first) * size
                kept, base = keep_b, shift
            theirs = got[base + at : base + at + size, :].astype(F32)
            out[slot, part * size : (part + 1) * size, :] = kept[at : at + size, :] + theirs
    total[...] = small[...] + load_small(got, shift + keep_b.shape[0], small.shape[0])
    lanes = small.shape[1]
    owner = lax.axis_index("dp") * lax.axis_size("tap") + lax.axis_index("tap")
    width = b_out.shape[1]
    turned = pltpu.roll(total[...], (lanes - owner * width) % lanes, 1)
    for at, target in (
        (0, b_out),
        (1, gain_two),
        (2, bias_two),
        (8, conv_bias),
        (9, gain_one),
        (10, bias_one),
    ):
        target[...] = turned[at : at + 1, 0:width]
    width = b_in.shape[1]
    start = owner * width
    line = total[pl.ds(3 + start // lanes, 1), :]
    line = pltpu.roll(jnp.broadcast_to(line, (8, lanes)), (lanes - start % lanes) % lanes, 1)
    b_in[...] = line[0:1, 0:width]


def params(mib):
    return pltpu.CompilerParams(vmem_limit_bytes=mib * MIB)


def claim(micros):
    return pl.CostEstimate(flops=int(micros * 1.1e9), bytes_accessed=1, transcendentals=0)


def after_kernel(_, token, out):
    del token, out


def after(value, token, claimed=0):
    return pl.pallas_call(
        after_kernel,
        out_shape=pltpu.VMEM(value.shape, value.dtype),
        in_specs=[VMEM] * 2,
        out_specs=VMEM,
        input_output_aliases={0: 0},
        compiler_params=params(4),
        cost_estimate=claim(claimed),
        name="after",
    )(near(value), near(token))


def far(value):
    return pltpu.with_memory_space_constraint(value, pltpu.HBM)


def near(value):
    return pltpu.with_memory_space_constraint(value, pltpu.VMEM)


def fused_step(gots, flows, plans, sizes, token):
    lanes = flows[0]["keep"].shape[1]
    operands = [near(got) for got in gots]
    outs = []
    for flow, plan in zip(flows, plans):
        plan["with_small"] = "small_in" in plan
        operands.append(near(flow["keep"]))
        outs.append(pltpu.VMEM((flow["keep"].shape[0] // 2, lanes), F32))
        if plan["with_small"]:
            operands.append(near(flow["small"]))
            outs.append(pltpu.VMEM(flow["small"].shape, F32))
    operands.append(near(token))
    kept = len(outs)
    outs += [pltpu.VMEM((rows, lanes), BF16) for rows in sizes]
    out = pl.pallas_call(
        functools.partial(fused_kernel, len(gots), plans),
        out_shape=outs,
        in_specs=[VMEM] * len(operands),
        out_specs=[VMEM] * len(outs),
        compiler_params=params(4),
        cost_estimate=claim(0),
        name="step",
    )(*operands)
    at = 0
    for flow, plan in zip(flows, plans):
        flow["keep"] = out[at]
        at += 1
        if plan["with_small"]:
            flow["small"] = out[at]
            at += 1
    return out[kept:]


def swap(value, mask):
    count = lax.axis_size("dp") * lax.axis_size("tap")
    return lax.ppermute(value, ("dp", "tap"), [(i, i ^ mask) for i in range(count)])


def cut_kernel(weight_hbm, piece, sems):
    rows = piece.shape[1]
    start = (lax.axis_index("dp") & 7) * rows
    copies = [
        pltpu.make_async_copy(
            weight_hbm.at[slot, rows_at(start, rows), :], piece.at[slot], sems.at[slot]
        )
        for slot in range(piece.shape[0])
    ]
    for copy in copies:
        copy.start()
    wait_all(copies)


def cut_piece(conv_weight):
    slots, chan, width = conv_weight.shape
    return pl.pallas_call(
        cut_kernel,
        out_shape=pltpu.VMEM((slots, chan // 8, width), BF16),
        in_specs=[HBM],
        out_specs=VMEM,
        scratch_shapes=[pltpu.SemaphoreType.DMA((slots,))],
        compiler_params=params(4),
        cost_estimate=claim(0),
        name="cut_piece",
    )(far(conv_weight))


def both_kernel(over_one, over_two, _, both):
    slots = over_one.shape[0]
    both[0:slots] = over_one[...]
    both[slots:] = over_two[...]


def fetch_pieces(first, straight, token):
    over_one = swap_dp(first, 1)
    over_two = swap_dp(first, 2)
    straight = swap_tap(after(straight, first))
    slots = first.shape[0]
    both = pl.pallas_call(
        both_kernel,
        out_shape=pltpu.VMEM((2 * slots,) + first.shape[1:], BF16),
        in_specs=[VMEM] * 3,
        out_specs=VMEM,
        compiler_params=params(4),
        cost_estimate=claim(0),
        name="both",
    )(near(over_one), near(over_two), near(token))
    return [
        ((0,), first),
        ((2, 4), both),
        ((6,), straight),
        ((1,), swap_dp(first, 0)),
        ((3, 5), swap_dp(both, 0)),
        ((7,), swap_dp(straight, 0)),
    ]


def fast_shards(
    block_input,
    conv_weight,
    slot_tap_table,
    conv_bias,
    conv_norm_gain,
    conv_norm_bias,
    w_in,
    b_in,
    w_out,
    b_out,
    ffn_norm_gain,
    ffn_norm_bias,
    species_id,
    species_count,
    out_grad,
):
    tap_count = lax.axis_size("tap")
    dp_bits = (lax.axis_size("dp") - 1).bit_length()
    rows_dev = block_input.shape[0] // tap_count
    chan = block_input.shape[1]
    hid = w_in.shape[1]
    windows = rows_dev // WINDOW_LENGTH
    slots = conv_weight.shape[0]
    vmem = pltpu.VMEM
    line = list(range(2, dp_bits))
    orders = (["t", 1] + line, [1, "t"] + line)
    orders_b = ([2, "t", 1] + line[1:], [2, 1, "t"] + line[1:])
    over_x, over_y = 1, 4
    pad_shape = (windows, WINDOW_LENGTH + 2 * PAD, chan)
    rows_f = (rows_dev, chan)
    small_cost = claim(0)

    def row(vector):
        return vector.reshape(1, -1)

    piece = cut_piece(conv_weight)
    weight_shape = conv_weight.shape
    tiles = rows_dev // TILE
    dma = pltpu.SemaphoreType.DMA
    first = swap_tap(piece)
    x_pad, own_weight, w_in_near, straight = pl.pallas_call(
        load_kernel,
        out_shape=[
            vmem(pad_shape, BF16),
            vmem(weight_shape, BF16),
            vmem(w_in.shape, BF16),
            vmem((slots * chan // 8 + TABLE_ROWS, chan), BF16),
        ],
        in_specs=[SMEM] + [HBM] * 3,
        out_specs=[VMEM] * 4,
        scratch_shapes=[dma((windows + 2 * slots + 4,))],
        compiler_params=params(8),
        cost_estimate=claim(0),
        name="load",
    )(slot_tap_table, far(block_input), far(conv_weight), far(w_in))
    first = after(first, x_pad)
    part, token = pl.pallas_call(
        own_conv_kernel,
        out_shape=[vmem(rows_f, F32), vmem((8, 128), F32)],
        in_specs=[SMEM] + [VMEM] * 3,
        out_specs=[VMEM] * 2,
        compiler_params=params(8),
        cost_estimate=claim(0),
        name="own_conv",
    )(slot_tap_table, near(x_pad), near(own_weight), near(first))
    pieces = fetch_pieces(first, straight, token)

    block_f = (hid + chan * hid // COLS) >> (dp_bits + 1)
    half_f = block_f << dp_bits
    main = pl.pallas_call(
        functools.partial(main_kernel, orders, dp_bits, [turn for turn, _ in pieces]),
        out_shape=[
            pltpu.HBM(rows_f, BF16),
            vmem(rows_f, F32),
            vmem(rows_f, F32),
            vmem((rows_dev, hid), BF16),
            vmem(conv_weight.shape, BF16),
            vmem((half_f, chan), F32),
            vmem((half_f, chan), BF16),
            vmem((8, chan), F32),
            vmem(rows_f, BF16),
            jax.ShapeDtypeStruct((slots,), jnp.int32),
        ],
        in_specs=[SMEM] * 2 + [VMEM] * 2 + [HBM, VMEM, HBM] + [VMEM] * (7 + len(pieces)),
        out_specs=[HBM] + [VMEM] * 8 + [SMEM],
        scratch_shapes=[
            vmem(w_out.shape, BF16),
            vmem(rows_f, F32),
            vmem(rows_f, BF16),
            vmem((rows_dev, hid), BF16),
            vmem((rows_dev, hid), F32),
            vmem(rows_f, BF16),
            vmem(rows_f, BF16),
            vmem((2, COLS, chan), F32),
            vmem((8, 8, chan), F32),
            dma,
            dma((12,)),
        ],
        compiler_params=params(34),
        cost_estimate=small_cost,
        name="main_rows",
    )(
        species_id,
        species_count,
        near(x_pad),
        near(part),
        far(out_grad),
        near(w_in_near),
        far(w_out),
        row(conv_bias),
        row(conv_norm_gain),
        row(conv_norm_bias),
        row(b_in),
        row(b_out),
        row(ffn_norm_gain),
        row(ffn_norm_bias),
        *[near(piece) for _, piece in pieces],
    )
    block_output, unit, slope, d_up, other_weight, keep_f, send_f, small_ffn = main[:8]
    grad_in, other_table = main[8:]
    got_f = swap_dp(send_f, 0)

    d_pad, d_hidden, small = pl.pallas_call(
        back_kernel,
        out_shape=[vmem(pad_shape, BF16), vmem(rows_f, F32), vmem((16, chan), F32)],
        in_specs=[SMEM] * 2 + [VMEM] * 7,
        out_specs=[VMEM] * 3,
        scratch_shapes=[vmem((8, 8, chan), F32)],
        compiler_params=params(8),
        cost_estimate=small_cost,
        name="back_rows",
    )(
        species_id,
        species_count,
        near(grad_in),
        near(w_in_near),
        near(d_up),
        near(unit),
        near(slope),
        row(conv_norm_gain),
        near(small_ffn),
    )
    flow_f = dict(keep=keep_f)
    rows = keep_f.shape[0] // 2
    plan = dict(ins=[(0, 0), (0, rows)], outs=[(0, 0), (1, 0)])
    sends_f = fused_step([got_f], [flow_f], [plan], [rows // 2] * 2, small)
    gots_f = [swap(sends_f[0], over_x), swap(sends_f[1], over_y)]

    def terms(group, orders, token, small, name):
        count = len(group) * chan
        extra = 0 if small is None else small.shape[0]
        outs = [vmem((count, chan), F32), vmem((count + extra, chan), BF16)]
        scratch = [vmem((2, chan, chan), F32)]
        more = [] if small is None else [near(small)]
        return pl.pallas_call(
            functools.partial(terms_kernel, group, orders, dp_bits, small is not None),
            out_shape=outs,
            in_specs=[SMEM] * 2 + [VMEM] * (3 + len(more)),
            out_specs=[VMEM] * len(outs),
            scratch_shapes=scratch,
            compiler_params=params(8),
            cost_estimate=small_cost,
            name=name,
        )(slot_tap_table, other_table, near(x_pad), near(d_pad), *more, near(token))

    cut = (slots * 3 + 4) // 5
    keep_a, send_a = terms(range(0, cut), orders, sends_f[0], None, "terms_a")
    got_a = swap_dp(send_a, 0)
    keep_b, send_b = terms(range(cut, slots), orders_b, keep_a, small, "terms_b")
    got_b = swap_dp(send_b, 0)
    def spaced(token, claimed=1):
        return after(mark, token, claimed)

    mark = token
    flow_a = dict(keep=keep_a)
    flow_b = dict(keep=keep_b, small=small)
    extra = small.shape[0]
    over_z, over_zz = 2 << line[0], 2 << line[1]

    def half_of(flow):
        return flow["keep"].shape[0] // 4

    def joined(base, flow):
        return [(0, base), (0, base + 2 * half_of(flow))]

    size = half_of(flow_f)
    plan = dict(ins=[(0, 0), (1, 0)], outs=[(0, 0), (1, 0)])
    sends = fused_step(gots_f, [flow_f], [plan], [size] * 2, keep_b)
    gots_f = [swap(sends[0], over_y), swap(sends[1], over_x)]
    mark = spaced(flow_f["keep"], 100)
    size = half_of(flow_b)
    plan = dict(
        ins=joined(0, flow_b),
        small_in=(0, 4 * size),
        outs=[(0, 0), (0, size)],
        small_out=(0, 2 * size),
    )
    sends = fused_step([got_b], [flow_b], [plan], [2 * size + extra], mark)
    got_b = swap(sends[0], over_z)
    partial = pl.pallas_call(
        input_near_kernel,
        out_shape=vmem(rows_f, F32),
        in_specs=[SMEM] + [VMEM] * 4,
        out_specs=VMEM,
        compiler_params=params(8),
        cost_estimate=claim(0),
        name="input_near",
    )(slot_tap_table, near(d_pad), near(d_hidden), near(own_weight), near(flow_b["keep"]))
    size = half_of(flow_f)
    plan = dict(ins=[(0, 0), (1, 0)], outs=[(0, 0), (0, size)])
    sends = fused_step(gots_f, [flow_f], [plan], [2 * size], partial)
    got_f = swap(sends[0], over_z)
    mark = spaced(flow_f["keep"])
    size = half_of(flow_a)
    plan = dict(ins=joined(0, flow_a), outs=[(0, 0), (1, 0)])
    sends = fused_step([got_a], [flow_a], [plan], [size] * 2, mark)
    gots_a = [swap(sends[0], over_x), swap(sends[1], over_y)]
    input_grad, mark = pl.pallas_call(
        input_far_kernel,
        out_shape=[pltpu.HBM(rows_f, F32), vmem((8, 128), F32)],
        in_specs=[SMEM] + [VMEM] * 4,
        out_specs=[HBM, VMEM],
        scratch_shapes=[vmem(rows_f, F32), pltpu.SemaphoreType.DMA((rows_dev // TILE,))],
        compiler_params=params(8),
        cost_estimate=small_cost,
        name="input_far",
    )(other_table, near(d_pad), near(partial), near(other_weight), near(flow_a["keep"]))
    mark = spaced(mark)
    size, size_b = half_of(flow_a), half_of(flow_b)
    plan = dict(ins=[(0, 0), (1, 0)], outs=[(0, 0), (1, 0)])
    plan_b = dict(
        ins=[(2, 0), (2, 2 * size_b)],
        small_in=(2, 4 * size_b),
        outs=[(1, size), (0, size)],
        small_out=(1, size + size_b),
    )
    sends = fused_step(
        gots_a + [got_b],
        [flow_a, flow_b],
        [plan, plan_b],
        [size + size_b, size + size_b + extra],
        mark,
    )
    gots = [swap(sends[0], over_y), swap(sends[1], over_x)]
    shift = size
    mark = spaced(flow_a["keep"])
    size = half_of(flow_f)
    plan = dict(ins=joined(0, flow_f), outs=[(0, 0), (0, size)])
    sends = fused_step([got_f], [flow_f], [plan], [2 * size], mark)
    got_f = swap(sends[0], over_zz)
    mark = spaced(flow_f["keep"])
    size = half_of(flow_a)
    plan = dict(ins=[(0, 0), (1, 0)], outs=[(0, 0), (0, size)])
    sends = fused_step(gots, [flow_a], [plan], [2 * size], mark)
    got_a = swap(sends[0], over_z)
    size = half_of(flow_b)
    plan = dict(
        ins=[(1, shift), (0, shift)],
        small_in=(1, shift + 2 * size),
        outs=[(0, 0), (1, 0)],
        small_out=(0, size),
    )
    sends = fused_step(gots, [flow_b], [plan], [size + extra, size], flow_a["keep"])
    gots_b = [swap(sends[0], over_y), swap(sends[1], over_x)]
    mark = flow_b["keep"]
    got_f = after(got_f, mark)
    mark = spaced(got_f)
    size, size_b = half_of(flow_a), half_of(flow_b)
    plan = dict(ins=joined(0, flow_a), outs=[(0, 0), (0, size)])
    shift = 2 * size
    plan_b = dict(
        ins=[(1, 0), (2, 0)],
        small_in=(1, 2 * size_b),
        outs=[(0, shift), (0, shift + size_b)],
        small_out=(0, shift + 2 * size_b),
    )
    sends = fused_step(
        [got_a] + gots_b, [flow_a, flow_b], [plan, plan_b], [shift + 2 * size_b + extra], mark
    )
    got = swap(sends[0], over_zz)
    width = chan >> (dp_bits + 1)
    wide = hid >> (dp_bits + 1)
    small = flow_b["small"]
    conv_weight_grad, _, *vectors, w_in_mine, w_out_mine = pl.pallas_call(
        last_conv_kernel,
        out_shape=[
            jax.ShapeDtypeStruct((slots, chan >> dp_bits, chan), F32),
            vmem(small.shape, F32),
        ]
        + [jax.ShapeDtypeStruct((1, width), F32)] * 6
        + [
            jax.ShapeDtypeStruct((1, wide), F32),
            jax.ShapeDtypeStruct((chan >> (dp_bits + 1), hid), F32),
            jax.ShapeDtypeStruct((hid >> (dp_bits + 1), chan), F32),
        ],
        in_specs=[VMEM] * 6,
        out_specs=[VMEM] * 11,
        compiler_params=params(4),
        cost_estimate=claim(0),
        name="last_conv",
    )(
        near(got),
        near(flow_a["keep"]),
        near(small),
        near(flow_b["keep"]),
        near(got_f),
        near(flow_f["keep"]),
    )
    conv_bias_grad, gain_one_grad, bias_one_grad, b_out_grad, gain_two_grad, bias_two_grad, b_in_grad = [
        vector.reshape(-1) for vector in vectors
    ]
    return (
        block_output,
        input_grad,
        conv_weight_grad,
        conv_bias_grad,
        gain_one_grad,
        bias_one_grad,
        w_in_mine,
        b_in_grad,
        w_out_mine,
        b_out_grad,
        gain_two_grad,
        bias_two_grad,
    )


def narrow_enough(mesh):
    return mesh.shape["tap"] == 2 and mesh.shape["dp"] == 16


def solution(mesh):
    chosen = fast_shards if narrow_enough(mesh) else plain_shards
    return jax.shard_map(
        chosen,
        mesh=mesh,
        in_specs=(
            P("dp", None),
            P("tap", None, None),
            P("tap"),
            P(),
            P(),
            P(),
            P(),
            P(),
            P(),
            P(),
            P(),
            P(),
            P("dp"),
            P(),
            P(("dp", "tap"), None),
        ),
        out_specs=(
            P(("dp", "tap"), None),
            P(("dp", "tap"), None),
            P("tap", "dp", None),
            P(("dp", "tap")),
            P(("dp", "tap")),
            P(("dp", "tap")),
            P(("dp", "tap"), None),
            P(("dp", "tap")),
            P(("dp", "tap"), None),
            P(("dp", "tap")),
            P(("dp", "tap")),
            P(("dp", "tap")),
        ),
        check_vma=False,
    )
```

```python
import functools

import jax
import jax.numpy as jnp
from jax import lax
from jax.experimental import pallas as pl
from jax.experimental.pallas import tpu as pltpu
from jax.sharding import PartitionSpec as P

KERNEL_TAPS = 9
DILATION_STEP = 16
WINDOW_LENGTH = 512


def layer_norm(values):
    mean_val = jnp.mean(values, axis=-1, keepdims=True)
    center = values - mean_val
    spread = jnp.mean(center * center, axis=-1, keepdims=True)
    return center * lax.rsqrt(spread + 1e-05)


def exact_gelu(values):
    return jax.nn.gelu(values, approximate=False)


def conv_branch(pre_conv, gain_one, bias_one):
    return layer_norm(exact_gelu(pre_conv)) * gain_one + bias_one


def ffn_branch(pre_out, gain_two, bias_two):
    return layer_norm(pre_out) * gain_two + bias_two


def shift_stack(win_rows, tap_table, forward):
    tap_extent = KERNEL_TAPS // 2 * DILATION_STEP
    padded_input = jnp.pad(win_rows, ((0, 0), (tap_extent, tap_extent), (0, 0)))
    pieces = []
    for index_of_slot in range(tap_table.shape[0]):
        if forward:
            tap_offset = tap_table[index_of_slot]
        else:
            tap_offset = KERNEL_TAPS - 1 - tap_table[index_of_slot]
        shifted_input = lax.dynamic_slice_in_dim(
            padded_input, tap_offset * DILATION_STEP, WINDOW_LENGTH, 1
        )
        pieces.append(shifted_input.reshape(-1, win_rows.shape[2]))
    return jnp.stack(pieces)


def contract_rows(left, right):
    return lax.dot_general(
        left, right, (((0,), (0,)), ((), ())), preferred_element_type=jnp.float32
    )


def contract_cols(left, right):
    return lax.dot_general(
        left, right, (((1,), (1,)), ((), ())), preferred_element_type=jnp.float32
    )


def swap_dp(value, bit):
    count = lax.axis_size("dp")
    return lax.ppermute(value, "dp", [(i, i ^ (1 << bit)) for i in range(count)])


def swap_tap(value):
    return lax.ppermute(value, "tap", [(0, 1), (1, 0)])


def halve(part, order, kind):
    dp_bits = (lax.axis_size("dp") - 1).bit_length()
    place = lax.axis_index("dp")
    tap = lax.axis_index("tap")
    labels = ["t"] + list(range(dp_bits - 1, -1, -1))
    for step in order:
        axis = labels.index(step)
        labels.pop(axis)
        mine = tap if step == "t" else (place >> step) & 1
        keep = lax.dynamic_index_in_dim(part, mine, axis, keepdims=False)
        send = lax.dynamic_index_in_dim(part, 1 - mine, axis, keepdims=False).astype(kind)
        got = swap_tap(send) if step == "t" else swap_dp(send, step)
        part = keep + got.astype(jnp.float32)
    return part


def orders(dp_bits):
    rest = list(range(2, dp_bits))
    first = [0, "t", 1] + rest
    second = [0, 1] + rest[:1] + ["t"] + rest[1:]
    third = [0] + rest[:1] + ["t", 1] + rest[1:]
    return first, second, third


def plain_shards(
    block_input,
    conv_weight,
    slot_tap_table,
    conv_bias,
    conv_norm_gain,
    conv_norm_bias,
    w_in,
    b_in,
    w_out,
    b_out,
    ffn_norm_gain,
    ffn_norm_bias,
    species_id,
    species_count,
    out_grad,
):
    tap_count = lax.axis_size("tap")
    my_index = lax.axis_index("tap")
    core = lax.axis_index("dp") & 1
    dp_bits = (lax.axis_size("dp") - 1).bit_length()
    tok_dev, chan_width = block_input.shape
    hid_width = w_in.shape[1]
    half_rows = tok_dev // tap_count
    windows = tok_dev // WINDOW_LENGTH
    my_windows = windows // tap_count
    own_slots = conv_weight.shape[0]
    half_chan = chan_width // 2
    first, second, third = orders(dp_bits)

    other_table = swap_tap(slot_tap_table)
    part_send = lax.dynamic_slice_in_dim(conv_weight, core * half_chan, half_chan, 1)
    part_here = swap_tap(part_send)
    part_mate = swap_dp(part_here, 0)
    low_part = jnp.where(core == 0, part_here, part_mate)
    high_part = jnp.where(core == 0, part_mate, part_here)
    other_weight = jnp.concatenate([low_part, high_part], axis=1)

    my_x = lax.dynamic_slice_in_dim(block_input, my_index * half_rows, half_rows, 0)
    x_windows = my_x.reshape(my_windows, WINDOW_LENGTH, chan_width)
    mine_x = my_x.astype(jnp.float32)
    own_stack = shift_stack(x_windows, slot_tap_table, True)
    other_stack = shift_stack(x_windows, other_table, True)
    conv_out = jnp.einsum("str,sro->to", own_stack, conv_weight, preferred_element_type=jnp.float32)
    conv_out = conv_out + jnp.einsum(
        "str,sro->to", other_stack, other_weight, preferred_element_type=jnp.float32
    )
    pre_conv = conv_out + conv_bias
    norm_one, conv_back = jax.vjp(conv_branch, pre_conv, conv_norm_gain, conv_norm_bias)
    hidden = mine_x + norm_one
    hidden_low = hidden.astype(jnp.bfloat16)
    pre_up = jnp.dot(hidden_low, w_in, preferred_element_type=jnp.float32) + b_in
    activ, activ_back = jax.vjp(exact_gelu, pre_up)
    act_low = activ.astype(jnp.bfloat16)
    pre_out = jnp.dot(act_low, w_out, preferred_element_type=jnp.float32) + b_out
    norm_two, ffn_back = jax.vjp(ffn_branch, pre_out, ffn_norm_gain, ffn_norm_bias)
    block_output = (hidden + norm_two).astype(jnp.bfloat16)
    my_species = lax.dynamic_slice_in_dim(species_id, my_index * my_windows, my_windows, 0)
    species_range = jnp.arange(species_count.shape[0], dtype=jnp.int32)
    matches = my_species[:, None] == species_range[None, :]
    window_count = jnp.sum(jnp.where(matches, species_count[None, :], 0), axis=1)
    window_scale = 4.0 / window_count.astype(jnp.float32)
    grad_y = (
        out_grad.astype(jnp.float32).reshape(my_windows, WINDOW_LENGTH, chan_width)
        * window_scale[:, None, None]
    ).reshape(half_rows, chan_width)
    d_pre_out, d_gain_two, d_bias_two = ffn_back(grad_y)
    d_out_low = d_pre_out.astype(jnp.bfloat16)
    d_w_out = contract_rows(act_low, d_out_low)
    d_b_out = jnp.sum(d_out_low.astype(jnp.float32), axis=0)
    d_activ = contract_cols(d_out_low, w_out)
    (d_pre_up,) = activ_back(d_activ)
    d_up_low = d_pre_up.astype(jnp.bfloat16)
    d_w_in = contract_rows(hidden_low, d_up_low)
    d_b_in = jnp.sum(d_up_low.astype(jnp.float32), axis=0)
    d_hidden = grad_y + contract_cols(d_up_low, w_in)
    d_pre_conv, d_gain_one, d_bias_one = conv_back(d_hidden)
    d_conv_low = d_pre_conv.astype(jnp.bfloat16)
    d_conv_bias = jnp.sum(d_conv_low.astype(jnp.float32), axis=0)
    d_windows = d_conv_low.reshape(my_windows, WINDOW_LENGTH, chan_width)
    own_back = shift_stack(d_windows, slot_tap_table, False)
    other_back = shift_stack(d_windows, other_table, False)
    input_grad = (
        d_hidden
        + jnp.einsum("sto,sro->tr", own_back, conv_weight, preferred_element_type=jnp.float32)
        + jnp.einsum("sto,sro->tr", other_back, other_weight, preferred_element_type=jnp.float32)
    )
    own_terms = jnp.einsum("str,to->sro", own_stack, d_conv_low, preferred_element_type=jnp.float32)
    other_terms = jnp.einsum(
        "str,to->sro", other_stack, d_conv_low, preferred_element_type=jnp.float32
    )
    bits = [2] * dp_bits

    def by_tap(own, other):
        return jnp.where(my_index == 0, jnp.stack([own, other]), jnp.stack([other, own]))

    def conv_part(begin, end, order):
        own = own_terms[begin:end]
        other = other_terms[begin:end]
        both = by_tap(own, other)
        rows = chan_width >> dp_bits
        both = both.reshape([2, end - begin] + bits + [rows, chan_width])
        return halve(jnp.moveaxis(both, 1, 1 + dp_bits), order, jnp.bfloat16)

    cut = own_slots * 2 // 5
    conv_weight_grad = jnp.concatenate(
        [
            conv_part(0, cut, first),
            conv_part(cut, 2 * cut, second),
            conv_part(2 * cut, own_slots, third),
        ]
    )

    def spread(total, order, kind):
        rows = total.shape[0] >> (dp_bits + 1)
        split = total.reshape(bits + [2, rows] + list(total.shape[1:]))
        return halve(jnp.moveaxis(split, dp_bits, 0), order, kind)

    d_w_out_mine = spread(d_w_out, first, jnp.bfloat16)
    d_w_in_mine = spread(d_w_in, second, jnp.bfloat16)
    owners = 2 << dp_bits
    small = [d_b_in, d_b_out, d_conv_bias, d_gain_one, d_bias_one, d_gain_two, d_bias_two]
    joined = jnp.concatenate([v.reshape(owners, -1) for v in small], axis=1)
    joined_mine = spread(joined, third, jnp.float32).reshape(-1)
    vectors = []
    start = 0
    for v in small:
        size = v.shape[0] // owners
        vectors.append(joined_mine[start : start + size])
        start += size
    return (
        block_output,
        input_grad,
        conv_weight_grad,
        vectors[2],
        vectors[3],
        vectors[4],
        d_w_in_mine,
        vectors[0],
        d_w_out_mine,
        vectors[1],
        vectors[5],
        vectors[6],
    )


TILE = 512
COLS = 512
PAD = KERNEL_TAPS // 2 * DILATION_STEP
MIB = 2**20
TABLE_ROWS = 16
F32 = jnp.float32
BF16 = jnp.bfloat16
HBM = pl.BlockSpec(memory_space=pltpu.HBM)
VMEM = pl.BlockSpec(memory_space=pltpu.VMEM)
SMEM = pl.BlockSpec(memory_space=pltpu.SMEM)


def dot_plain(left, right):
    return lax.dot_general(left, right, (((1,), (0,)), ((), ())), preferred_element_type=F32)


def gelu_and_slope(value):
    cdf = 0.5 + 0.5 * lax.erf(value * 0.7071067811865476)
    density = jnp.exp2(value * value * -0.7213475204444817)
    return value * cdf, cdf + (value * 0.3989422804014327) * density


def norm_parts(value):
    center = value - jnp.mean(value, axis=-1, keepdims=True)
    spread = jnp.mean(center * center, axis=-1, keepdims=True)
    scale = lax.rsqrt(spread + 1e-05)
    return center * scale, scale


def norm_back(grad, unit):
    return grad - jnp.mean(grad, axis=-1, keepdims=True) - unit * jnp.mean(
        grad * unit, axis=-1, keepdims=True
    )


def fold_rows(value):
    return jnp.sum(value.reshape(value.shape[0] // 8, 8, value.shape[1]), axis=0)


def one_row(value):
    return jnp.sum(value, axis=0, keepdims=True)


def my_bits(dp_bits):
    place = lax.axis_index("dp")
    mine = {bit: (place >> bit) & 1 for bit in range(dp_bits)}
    mine["t"] = lax.axis_index("tap")
    return mine


def relative(order, owner, mine):
    spot = 0
    for label in order:
        spot = spot * 2 + (owner[label] ^ mine[label])
    return spot


def rows_at(start, size):
    return pl.ds(pl.multiple_of(start, 16), size)


def split_copy(source, target, sems, first):
    rows = target.shape[0] // 4
    return [
        pltpu.make_async_copy(
            source.at[at * rows : (at + 1) * rows, :],
            target.at[at * rows : (at + 1) * rows, :],
            sems.at[first + at],
        )
        for at in range(4)
    ]


def wait_all(copies):
    for copy in copies:
        copy.wait()


def clear_pads(pad_ref):
    zeros = jnp.zeros((PAD, pad_ref.shape[2]), pad_ref.dtype)
    for win in range(pad_ref.shape[0]):
        pad_ref[win, 0:PAD, :] = zeros
        pad_ref[win, PAD + WINDOW_LENGTH :, :] = zeros


def each_tile(rows, body, together=1):
    per = WINDOW_LENGTH // TILE

    @pl.loop(0, rows // TILE // together)
    def _(step):
        for member in range(together):
            number = step * together + member
            body(rows_at(number * TILE, TILE), number // per, (number % per) * TILE)


def window_weight(species, counts, win, windows, lanes):
    kind = species[lax.axis_index("tap") * windows + win]
    count = jnp.full((8, lanes), counts[kind], jnp.int32).astype(F32)
    return (4.0 / count)[0:1, :]


def load_kernel(
    table, x_hbm, weight_hbm, w_in_hbm, x_pad, weight, w_in, straight, sems
):
    windows = x_pad.shape[0]
    slots = weight.shape[0]
    rows = weight.shape[1] // 8
    base = lax.axis_index("tap") * windows * WINDOW_LENGTH
    start = ((lax.axis_index("dp") & 7) ^ 6) * rows
    copies = []
    for slot in range(slots):
        source = weight_hbm.at[slot, rows_at(start, rows), :]
        copies.append((source, straight.at[slot * rows : (slot + 1) * rows, :]))
    for win in range(windows):
        source = x_hbm.at[rows_at(base + win * WINDOW_LENGTH, WINDOW_LENGTH), :]
        copies.append((source, x_pad.at[win, PAD : PAD + WINDOW_LENGTH, :]))
    copies += [(weight_hbm.at[slot], weight.at[slot]) for slot in range(slots)]
    copies = [
        pltpu.make_async_copy(source, target, sems.at[at])
        for at, (source, target) in enumerate(copies)
    ]
    copies += split_copy(w_in_hbm, w_in, sems, len(copies))
    for copy in copies:
        copy.start()
    at = lax.broadcasted_iota(jnp.int32, (TABLE_ROWS, straight.shape[1]), 0)
    taps = jnp.zeros(at.shape, jnp.int32)
    for slot in range(slots):
        taps = jnp.where(at == slot, table[slot], taps)
    straight[slots * rows :, :] = taps.astype(F32).astype(BF16)
    clear_pads(x_pad)
    wait_all(copies)


def own_conv_kernel(table, x_pad, weight, _, part, token):
    token[...] = jnp.zeros(token.shape, token.dtype)

    def convolve(rows, win, begin):
        total = None
        for slot in range(weight.shape[0]):
            shifted = rows_at(table[slot] * DILATION_STEP + begin, TILE)
            term = dot_plain(x_pad[win, shifted, :], weight[slot])
            total = term if total is None else total + term
        part[rows, :] = total

    each_tile(part.shape[0], convolve, 2)


def join_pieces(plan, pieces, weight):
    slots = weight.shape[0]
    rows = weight.shape[1] // 8
    place = lax.axis_index("dp") & 7
    for turns, piece in zip(plan, pieces):
        flat = len(piece.shape) == 2
        for number, turn in enumerate(turns):
            there = rows_at((place ^ turn) * rows, rows)
            if flat:
                for slot in range(slots):
                    weight[slot, there, :] = piece[slot * rows : (slot + 1) * rows, :]
            else:
                weight[:, there, :] = piece[number * slots : (number + 1) * slots]


def main_kernel(orders, dp_bits, turns, *refs):
    species, counts = refs[:2]
    x_pad, part, grad_hbm, w_in, w_out_hbm = refs[2:7]
    conv_bias, gain_one, bias_one, b_in, b_out, gain_two, bias_two = refs[7:14]
    pieces = refs[14 : 14 + len(turns)]
    y_hbm, unit, slope, d_up, weight, keep, send, small, grad_in, table = refs[
        14 + len(turns) : 24 + len(turns)
    ]
    w_out, hidden, low, act, hid_slope, d_out, y_low, result, sums, sem, sems = refs[24 + len(turns) :]
    told = pieces[turns.index((6,))]
    told_at = told.shape[0] - TABLE_ROWS
    taps = []
    for slot in range(weight.shape[0]):
        line = told[told_at : told_at + TABLE_ROWS, 0:128].astype(F32)
        chosen = lax.broadcasted_iota(jnp.int32, line.shape, 0) == slot
        taps.append(jnp.max(jnp.where(chosen, line, 0.0)).astype(jnp.int32))
        table[slot] = taps[slot]
    mine = my_bits(dp_bits)
    rows_dev, chan = hidden.shape
    hid_width = w_in.shape[1]
    windows = x_pad.shape[0]
    out_copies = split_copy(w_out_hbm, w_out, sems, 4)
    grad_copies = split_copy(grad_hbm, grad_in, sems, 8)
    for copy in out_copies + grad_copies:
        copy.start()
    join_pieces(turns, pieces, weight)
    sums[...] = jnp.zeros(sums.shape, F32)

    def first_norm(rows, win, begin):
        total = part[rows, :] + conv_bias[...]
        for slot in range(weight.shape[0]):
            shifted = rows_at(taps[slot] * DILATION_STEP + begin, TILE)
            total = total + dot_plain(x_pad[win, shifted, :], weight[slot])
        value, steep = gelu_and_slope(total)
        normed, scale = norm_parts(value)
        unit[rows, :] = normed
        slope[rows, :] = scale * steep
        here = x_pad[win, rows_at(PAD + begin, TILE), :].astype(F32)
        summed = here + (normed * gain_one[...] + bias_one[...])
        hidden[rows, :] = summed
        low[rows, :] = summed.astype(BF16)

    each_tile(rows_dev, first_norm, 2)

    def go_up(rows, win, begin):
        for at in range(0, hid_width, COLS):
            cols = slice(at, at + COLS)
            up = dot_plain(low[rows, :], w_in[:, cols]) + b_in[:, cols]
            value, steep = gelu_and_slope(up)
            act[rows, cols] = value.astype(BF16)
            hid_slope[rows, cols] = steep

    each_tile(rows_dev, go_up, 2)
    wait_all(out_copies + grad_copies)

    def second_norm(rows, win, begin):
        pre_out = dot_plain(act[rows, :], w_out[...]) + b_out[...]
        normed, scale = norm_parts(pre_out)
        result_rows = hidden[rows, :] + (normed * gain_two[...] + bias_two[...])
        y_low[rows, :] = result_rows.astype(BF16)
        grad_y = grad_in[rows, :].astype(F32) * window_weight(species, counts, win, windows, chan)
        back = (norm_back(grad_y * gain_two[...], normed) * scale).astype(BF16)
        d_out[rows, :] = back
        sums[0] += fold_rows(back.astype(F32))
        sums[1] += fold_rows(grad_y * normed)
        sums[2] += fold_rows(grad_y)

    each_tile(rows_dev, second_norm, 2)
    y_copy = pltpu.make_async_copy(y_low, y_hbm, sem)
    y_copy.start()

    def go_down(rows, win, begin):
        for number, at in enumerate(range(0, hid_width, COLS)):
            cols = slice(at, at + COLS)
            d_act = contract_cols(d_out[rows, :], w_out[cols, :])
            back = (d_act * hid_slope[rows, cols]).astype(BF16)
            d_up[rows, cols] = back
            sums[3 + number] += fold_rows(back.astype(F32))

    each_tile(rows_dev, go_down, 2)
    for number in range(8):
        small[number : number + 1, :] = one_row(sums[number])
    core = mine[0]
    out_block = hid_width >> (dp_bits + 1)
    in_block = chan >> (dp_bits + 1)
    chunks = hid_width // COLS
    half = (out_block + chunks * in_block) // 2

    def hand_out(spot, first_row, block, targets):
        for start in range(0, result.shape[1], 4 * block):
            owner_at = first_row // block + start // block
            for tap in range(2):
                owner = {bit: (owner_at >> (bit + 1)) & 1 for bit in range(1, dp_bits)}
                owner["t"] = tap
                inner = start + tap * block
                for part_at, source, size, shift in targets:
                    spread = relative(orders[part_at], owner, mine) + (part_at << dp_bits)
                    place = rows_at(spread * half + shift, size)
                    mine_at = rows_at(inner + source + core * 2 * block, size)
                    other_at = rows_at(inner + source + (1 - core) * 2 * block, size)
                    keep[place, :] = result[spot, mine_at, :]
                    send[place, :] = result[spot, other_at, :].astype(BF16)

    size = out_block // 2

    for pair in range(chunks // 2):
        for spot in range(2):
            at = pl.multiple_of((pair * 2 + spot) * COLS, COLS)
            result[spot] = contract_rows(act[:, pl.ds(at, COLS)], d_out[...])
            hand_out(spot, at, out_block, [(0, 0, size, 0), (1, size, size, 0)])

    for step in range(chunks // 2):
        shift = size + step * in_block
        for spot in range(2):
            at = pl.multiple_of((spot * (chunks // 2) + step) * COLS, COLS)
            result[spot] = contract_rows(low[...], d_up[:, pl.ds(at, COLS)])
            hand_out(spot, 0, in_block, [(spot, 0, in_block, shift)])

    y_copy.wait()


def back_kernel(
    species,
    counts,
    grad_in,
    w_in,
    d_up,
    unit,
    slope,
    gain_one,
    small_in,
    d_pad,
    d_hidden,
    small,
    sums,
):
    windows = d_pad.shape[0]
    chan = d_hidden.shape[1]
    clear_pads(d_pad)
    sums[...] = jnp.zeros(sums.shape, F32)

    def through_norm(rows, win, begin):
        grad = grad_in[rows, :].astype(F32) * window_weight(species, counts, win, windows, chan)
        grad = grad + contract_cols(d_up[rows, :], w_in[...])
        d_hidden[rows, :] = grad
        normed = unit[rows, :]
        back = (norm_back(grad * gain_one[...], normed) * slope[rows, :]).astype(BF16)
        d_pad[win, rows_at(PAD + begin, TILE), :] = back
        sums[0] += fold_rows(back.astype(F32))
        sums[1] += fold_rows(grad * normed)
        sums[2] += fold_rows(grad)

    each_tile(d_hidden.shape[0], through_norm, 2)
    small[0:8, :] = small_in[...]
    for number in range(8):
        small[8 + number : 9 + number, :] = one_row(sums[number])


def store_small(total, ref, first):
    ref[first : first + total.shape[0], :] = total.astype(BF16)


def load_small(ref, first, count):
    return ref[first : first + count, :].astype(F32)


def terms_kernel(slots, orders, dp_bits, with_small, own_table, other_table, x_pad, d_pad, *refs):
    if with_small:
        small, _, keep, send, result = refs
        store_small(small[...], send, keep.shape[0])
    else:
        _, keep, send, result = refs
    mine = my_bits(dp_bits)
    rows = x_pad.shape[2] >> dp_bits
    core = mine[0]
    tables = (own_table, other_table)
    size = rows // 2

    @pl.loop(0, len(slots))
    def _(number):
        for near_tap in range(2):
            tap = tables[near_tap][slots[0] + number]
            shifted = rows_at((KERNEL_TAPS - 1 - tap) * DILATION_STEP, WINDOW_LENGTH)
            total = None
            for win in range(x_pad.shape[0]):
                term = contract_rows(
                    x_pad[win, PAD : PAD + WINDOW_LENGTH, :], d_pad[win, shifted, :]
                )
                total = term if total is None else total + term
            result[near_tap] = total
            for start in range(0, x_pad.shape[2], 2 * rows):
                owner_at = start // rows
                owner = {bit: (owner_at >> bit) & 1 for bit in range(1, dp_bits)}
                owner["t"] = mine["t"] ^ near_tap
                for part_at in range(2):
                    spread = relative(orders[part_at], owner, mine) + (part_at << dp_bits)
                    place = rows_at((spread * len(slots) + number) * size, size)
                    mine_at = rows_at(start + core * rows + part_at * size, size)
                    other_at = rows_at(start + (1 - core) * rows + part_at * size, size)
                    keep[place, :] = result[near_tap, mine_at, :]
                    send[place, :] = result[near_tap, other_at, :].astype(BF16)


def input_sum(table, d_pad, base, weight, rows, win, begin):
    total = base[rows, :]
    for slot in range(weight.shape[0]):
        shifted = rows_at((KERNEL_TAPS - 1 - table[slot]) * DILATION_STEP + begin, TILE)
        total = total + contract_cols(d_pad[win, shifted, :], weight[slot])
    return total


def input_near_kernel(table, d_pad, base, weight, _, out):
    def gather(rows, win, begin):
        out[rows, :] = input_sum(table, d_pad, base, weight, rows, win, begin)

    each_tile(out.shape[0], gather, 2)


def input_far_kernel(table, d_pad, base, weight, _, out_hbm, token, out, sems):
    token[...] = jnp.zeros(token.shape, token.dtype)

    def copy_of(rows):
        return pltpu.make_async_copy(out.at[rows, :], out_hbm.at[rows, :], sems.at[0])

    def gather(rows, win, begin):
        out[rows, :] = input_sum(table, d_pad, base, weight, rows, win, begin)
        copy_of(rows).start()

    each_tile(out.shape[0], gather, 2)
    pltpu.make_async_copy(out, out_hbm, sems.at[0]).wait()


def fused_kernel(got_count, plans, *refs):
    gots = refs[:got_count]
    at = got_count
    inputs = []
    for plan in plans:
        inputs.append(refs[at : at + 1 + plan["with_small"]])
        at += 1 + plan["with_small"]
    at += 1
    kept = []
    for plan in plans:
        kept.append(refs[at : at + 1 + plan["with_small"]])
        at += 1 + plan["with_small"]
    sent = refs[at:]
    for plan, source, target in zip(plans, inputs, kept):
        keep = source[0]
        rows = keep.shape[0] // 2
        half = rows // 2
        for part in range(2):
            which, base = plan["ins"][part]
            out, spot = plan["outs"][part]
            start = part * rows
            theirs = gots[which][base + half : base + rows, :].astype(F32)
            total = keep[start + half : start + rows, :] + theirs
            sent[out][spot : spot + half, :] = total.astype(BF16)
            ours = gots[which][base : base + half, :].astype(F32)
            target[0][part * half : (part + 1) * half, :] = keep[start : start + half, :] + ours
        if plan["with_small"]:
            which, base = plan["small_in"]
            count = source[1].shape[0]
            total = source[1][...] + load_small(gots[which], base, count)
            target[1][...] = total
            out, spot = plan["small_out"]
            store_small(total, sent[out], spot)


def sum_of(gots, keep, rows):
    total = keep[rows, :]
    for got in gots:
        total = total + got[rows, :].astype(F32)
    return total


def finish_ffn(got, keep, w_in_out, w_out_out):
    out_rows, chan = w_out_out.shape
    in_rows = w_in_out.shape[0]
    half = keep.shape[0] // 2
    steps = w_in_out.shape[1] // chan // 2
    for part in range(2):
        base = part * half
        size = out_rows // 2
        w_out_out[part * size : (part + 1) * size, :] = sum_of([got], keep, slice(base, base + size))
        for step in range(steps):
            at = base + size + step * in_rows
            cols = slice((part * steps + step) * chan, (part * steps + step + 1) * chan)
            w_in_out[:, cols] = sum_of([got], keep, slice(at, at + in_rows))


def last_conv_kernel(
    got,
    keep_a,
    small,
    keep_b,
    got_f,
    keep_f,
    out,
    total,
    conv_bias,
    gain_one,
    bias_one,
    b_out,
    gain_two,
    bias_two,
    b_in,
    w_in_out,
    w_out_out,
):
    finish_ffn(got_f, keep_f, w_in_out, w_out_out)
    size = out.shape[1] // 2
    first = keep_a.shape[0] // out.shape[1]
    rest = out.shape[0] - first
    shift = keep_a.shape[0]
    for slot in range(out.shape[0]):
        for part in range(2):
            if slot < first:
                at = (part * first + slot) * size
                kept, base = keep_a, 0
            else:
                at = (part * rest + slot - first) * size
                kept, base = keep_b, shift
            theirs = got[base + at : base + at + size, :].astype(F32)
            out[slot, part * size : (part + 1) * size, :] = kept[at : at + size, :] + theirs
    total[...] = small[...] + load_small(got, shift + keep_b.shape[0], small.shape[0])
    lanes = small.shape[1]
    owner = lax.axis_index("dp") * lax.axis_size("tap") + lax.axis_index("tap")
    width = b_out.shape[1]
    turned = pltpu.roll(total[...], (lanes - owner * width) % lanes, 1)
    for at, target in (
        (0, b_out),
        (1, gain_two),
        (2, bias_two),
        (8, conv_bias),
        (9, gain_one),
        (10, bias_one),
    ):
        target[...] = turned[at : at + 1, 0:width]
    width = b_in.shape[1]
    start = owner * width
    line = total[pl.ds(3 + start // lanes, 1), :]
    line = pltpu.roll(jnp.broadcast_to(line, (8, lanes)), (lanes - start % lanes) % lanes, 1)
    b_in[...] = line[0:1, 0:width]


def params(mib):
    return pltpu.CompilerParams(vmem_limit_bytes=mib * MIB)


def claim(micros):
    return pl.CostEstimate(flops=int(micros * 1.1e9), bytes_accessed=1, transcendentals=0)


def after_kernel(_, token, out):
    del token, out


def after(value, token, claimed=0):
    return pl.pallas_call(
        after_kernel,
        out_shape=pltpu.VMEM(value.shape, value.dtype),
        in_specs=[VMEM] * 2,
        out_specs=VMEM,
        input_output_aliases={0: 0},
        compiler_params=params(4),
        cost_estimate=claim(claimed),
        name="after",
    )(near(value), near(token))


def far(value):
    return pltpu.with_memory_space_constraint(value, pltpu.HBM)


def near(value):
    return pltpu.with_memory_space_constraint(value, pltpu.VMEM)


def fused_step(gots, flows, plans, sizes, token):
    lanes = flows[0]["keep"].shape[1]
    operands = [near(got) for got in gots]
    outs = []
    for flow, plan in zip(flows, plans):
        plan["with_small"] = "small_in" in plan
        operands.append(near(flow["keep"]))
        outs.append(pltpu.VMEM((flow["keep"].shape[0] // 2, lanes), F32))
        if plan["with_small"]:
            operands.append(near(flow["small"]))
            outs.append(pltpu.VMEM(flow["small"].shape, F32))
    operands.append(near(token))
    kept = len(outs)
    outs += [pltpu.VMEM((rows, lanes), BF16) for rows in sizes]
    out = pl.pallas_call(
        functools.partial(fused_kernel, len(gots), plans),
        out_shape=outs,
        in_specs=[VMEM] * len(operands),
        out_specs=[VMEM] * len(outs),
        compiler_params=params(4),
        cost_estimate=claim(0),
        name="step",
    )(*operands)
    at = 0
    for flow, plan in zip(flows, plans):
        flow["keep"] = out[at]
        at += 1
        if plan["with_small"]:
            flow["small"] = out[at]
            at += 1
    return out[kept:]


def swap(value, mask):
    count = lax.axis_size("dp") * lax.axis_size("tap")
    return lax.ppermute(value, ("dp", "tap"), [(i, i ^ mask) for i in range(count)])


def cut_kernel(weight_hbm, piece, sems):
    rows = piece.shape[1]
    start = (lax.axis_index("dp") & 7) * rows
    copies = [
        pltpu.make_async_copy(
            weight_hbm.at[slot, rows_at(start, rows), :], piece.at[slot], sems.at[slot]
        )
        for slot in range(piece.shape[0])
    ]
    for copy in copies:
        copy.start()
    wait_all(copies)


def cut_piece(conv_weight):
    slots, chan, width = conv_weight.shape
    return pl.pallas_call(
        cut_kernel,
        out_shape=pltpu.VMEM((slots, chan // 8, width), BF16),
        in_specs=[HBM],
        out_specs=VMEM,
        scratch_shapes=[pltpu.SemaphoreType.DMA((slots,))],
        compiler_params=params(4),
        cost_estimate=claim(0),
        name="cut_piece",
    )(far(conv_weight))


def both_kernel(over_one, over_two, _, both):
    slots = over_one.shape[0]
    both[0:slots] = over_one[...]
    both[slots:] = over_two[...]


def fetch_pieces(first, straight, token):
    over_one = swap_dp(first, 1)
    over_two = swap_dp(first, 2)
    straight = swap_tap(after(straight, first))
    slots = first.shape[0]
    both = pl.pallas_call(
        both_kernel,
        out_shape=pltpu.VMEM((2 * slots,) + first.shape[1:], BF16),
        in_specs=[VMEM] * 3,
        out_specs=VMEM,
        compiler_params=params(4),
        cost_estimate=claim(0),
        name="both",
    )(near(over_one), near(over_two), near(token))
    return [
        ((0,), first),
        ((2, 4), both),
        ((6,), straight),
        ((1,), swap_dp(first, 0)),
        ((3, 5), swap_dp(both, 0)),
        ((7,), swap_dp(straight, 0)),
    ]


def fast_shards(
    block_input,
    conv_weight,
    slot_tap_table,
    conv_bias,
    conv_norm_gain,
    conv_norm_bias,
    w_in,
    b_in,
    w_out,
    b_out,
    ffn_norm_gain,
    ffn_norm_bias,
    species_id,
    species_count,
    out_grad,
):
    tap_count = lax.axis_size("tap")
    dp_bits = (lax.axis_size("dp") - 1).bit_length()
    rows_dev = block_input.shape[0] // tap_count
    chan = block_input.shape[1]
    hid = w_in.shape[1]
    windows = rows_dev // WINDOW_LENGTH
    slots = conv_weight.shape[0]
    vmem = pltpu.VMEM
    line = list(range(2, dp_bits))
    orders = (["t", 1] + line, [1, "t"] + line)
    orders_b = ([2, "t", 1] + line[1:], [2, 1, "t"] + line[1:])
    over_x, over_y = 1, 4
    pad_shape = (windows, WINDOW_LENGTH + 2 * PAD, chan)
    rows_f = (rows_dev, chan)
    small_cost = claim(0)

    def row(vector):
        return vector.reshape(1, -1)

    piece = cut_piece(conv_weight)
    weight_shape = conv_weight.shape
    tiles = rows_dev // TILE
    dma = pltpu.SemaphoreType.DMA
    first = swap_tap(piece)
    x_pad, own_weight, w_in_near, straight = pl.pallas_call(
        load_kernel,
        out_shape=[
            vmem(pad_shape, BF16),
            vmem(weight_shape, BF16),
            vmem(w_in.shape, BF16),
            vmem((slots * chan // 8 + TABLE_ROWS, chan), BF16),
        ],
        in_specs=[SMEM] + [HBM] * 3,
        out_specs=[VMEM] * 4,
        scratch_shapes=[dma((windows + 2 * slots + 4,))],
        compiler_params=params(8),
        cost_estimate=claim(0),
        name="load",
    )(slot_tap_table, far(block_input), far(conv_weight), far(w_in))
    first = after(first, x_pad)
    part, token = pl.pallas_call(
        own_conv_kernel,
        out_shape=[vmem(rows_f, F32), vmem((8, 128), F32)],
        in_specs=[SMEM] + [VMEM] * 3,
        out_specs=[VMEM] * 2,
        compiler_params=params(8),
        cost_estimate=claim(0),
        name="own_conv",
    )(slot_tap_table, near(x_pad), near(own_weight), near(first))
    pieces = fetch_pieces(first, straight, token)

    block_f = (hid + chan * hid // COLS) >> (dp_bits + 1)
    half_f = block_f << dp_bits
    main = pl.pallas_call(
        functools.partial(main_kernel, orders, dp_bits, [turn for turn, _ in pieces]),
        out_shape=[
            pltpu.HBM(rows_f, BF16),
            vmem(rows_f, F32),
            vmem(rows_f, F32),
            vmem((rows_dev, hid), BF16),
            vmem(conv_weight.shape, BF16),
            vmem((half_f, chan), F32),
            vmem((half_f, chan), BF16),
            vmem((8, chan), F32),
            vmem(rows_f, BF16),
            jax.ShapeDtypeStruct((slots,), jnp.int32),
        ],
        in_specs=[SMEM] * 2 + [VMEM] * 2 + [HBM, VMEM, HBM] + [VMEM] * (7 + len(pieces)),
        out_specs=[HBM] + [VMEM] * 8 + [SMEM],
        scratch_shapes=[
            vmem(w_out.shape, BF16),
            vmem(rows_f, F32),
            vmem(rows_f, BF16),
            vmem((rows_dev, hid), BF16),
            vmem((rows_dev, hid), F32),
            vmem(rows_f, BF16),
            vmem(rows_f, BF16),
            vmem((2, COLS, chan), F32),
            vmem((8, 8, chan), F32),
            dma,
            dma((12,)),
        ],
        compiler_params=params(34),
        cost_estimate=small_cost,
        name="main_rows",
    )(
        species_id,
        species_count,
        near(x_pad),
        near(part),
        far(out_grad),
        near(w_in_near),
        far(w_out),
        row(conv_bias),
        row(conv_norm_gain),
        row(conv_norm_bias),
        row(b_in),
        row(b_out),
        row(ffn_norm_gain),
        row(ffn_norm_bias),
        *[near(piece) for _, piece in pieces],
    )
    block_output, unit, slope, d_up, other_weight, keep_f, send_f, small_ffn = main[:8]
    grad_in, other_table = main[8:]
    got_f = swap_dp(send_f, 0)

    d_pad, d_hidden, small = pl.pallas_call(
        back_kernel,
        out_shape=[vmem(pad_shape, BF16), vmem(rows_f, F32), vmem((16, chan), F32)],
        in_specs=[SMEM] * 2 + [VMEM] * 7,
        out_specs=[VMEM] * 3,
        scratch_shapes=[vmem((8, 8, chan), F32)],
        compiler_params=params(8),
        cost_estimate=small_cost,
        name="back_rows",
    )(
        species_id,
        species_count,
        near(grad_in),
        near(w_in_near),
        near(d_up),
        near(unit),
        near(slope),
        row(conv_norm_gain),
        near(small_ffn),
    )
    flow_f = dict(keep=keep_f)
    rows = keep_f.shape[0] // 2
    plan = dict(ins=[(0, 0), (0, rows)], outs=[(0, 0), (1, 0)])
    sends_f = fused_step([got_f], [flow_f], [plan], [rows // 2] * 2, small)
    gots_f = [swap(sends_f[0], over_x), swap(sends_f[1], over_y)]

    def terms(group, orders, token, small, name):
        count = len(group) * chan
        extra = 0 if small is None else small.shape[0]
        outs = [vmem((count, chan), F32), vmem((count + extra, chan), BF16)]
        scratch = [vmem((2, chan, chan), F32)]
        more = [] if small is None else [near(small)]
        return pl.pallas_call(
            functools.partial(terms_kernel, group, orders, dp_bits, small is not None),
            out_shape=outs,
            in_specs=[SMEM] * 2 + [VMEM] * (3 + len(more)),
            out_specs=[VMEM] * len(outs),
            scratch_shapes=scratch,
            compiler_params=params(8),
            cost_estimate=small_cost,
            name=name,
        )(slot_tap_table, other_table, near(x_pad), near(d_pad), *more, near(token))

    cut = (slots * 3 + 4) // 5
    keep_a, send_a = terms(range(0, cut), orders, sends_f[0], None, "terms_a")
    got_a = swap_dp(send_a, 0)
    keep_b, send_b = terms(range(cut, slots), orders_b, keep_a, small, "terms_b")
    got_b = swap_dp(send_b, 0)
    def spaced(token, claimed=1):
        return after(mark, token, claimed)

    mark = token
    flow_a = dict(keep=keep_a)
    flow_b = dict(keep=keep_b, small=small)
    extra = small.shape[0]
    over_z, over_zz = 2 << line[0], 2 << line[1]

    def half_of(flow):
        return flow["keep"].shape[0] // 4

    def joined(base, flow):
        return [(0, base), (0, base + 2 * half_of(flow))]

    size = half_of(flow_f)
    plan = dict(ins=[(0, 0), (1, 0)], outs=[(0, 0), (1, 0)])
    sends = fused_step(gots_f, [flow_f], [plan], [size] * 2, keep_b)
    gots_f = [swap(sends[0], over_y), swap(sends[1], over_x)]
    mark = spaced(flow_f["keep"], 100)
    size = half_of(flow_b)
    plan = dict(
        ins=joined(0, flow_b),
        small_in=(0, 4 * size),
        outs=[(0, 0), (0, size)],
        small_out=(0, 2 * size),
    )
    sends = fused_step([got_b], [flow_b], [plan], [2 * size + extra], mark)
    got_b = swap(sends[0], over_z)
    partial = pl.pallas_call(
        input_near_kernel,
        out_shape=vmem(rows_f, F32),
        in_specs=[SMEM] + [VMEM] * 4,
        out_specs=VMEM,
        compiler_params=params(8),
        cost_estimate=claim(0),
        name="input_near",
    )(slot_tap_table, near(d_pad), near(d_hidden), near(own_weight), near(flow_b["keep"]))
    size = half_of(flow_f)
    plan = dict(ins=[(0, 0), (1, 0)], outs=[(0, 0), (0, size)])
    sends = fused_step(gots_f, [flow_f], [plan], [2 * size], partial)
    got_f = swap(sends[0], over_z)
    mark = spaced(flow_f["keep"])
    size = half_of(flow_a)
    plan = dict(ins=joined(0, flow_a), outs=[(0, 0), (1, 0)])
    sends = fused_step([got_a], [flow_a], [plan], [size] * 2, mark)
    gots_a = [swap(sends[0], over_x), swap(sends[1], over_y)]
    input_grad, mark = pl.pallas_call(
        input_far_kernel,
        out_shape=[pltpu.HBM(rows_f, F32), vmem((8, 128), F32)],
        in_specs=[SMEM] + [VMEM] * 4,
        out_specs=[HBM, VMEM],
        scratch_shapes=[vmem(rows_f, F32), pltpu.SemaphoreType.DMA((rows_dev // TILE,))],
        compiler_params=params(8),
        cost_estimate=small_cost,
        name="input_far",
    )(other_table, near(d_pad), near(partial), near(other_weight), near(flow_a["keep"]))
    mark = spaced(mark)
    size, size_b = half_of(flow_a), half_of(flow_b)
    plan = dict(ins=[(0, 0), (1, 0)], outs=[(0, 0), (1, 0)])
    plan_b = dict(
        ins=[(2, 0), (2, 2 * size_b)],
        small_in=(2, 4 * size_b),
        outs=[(1, size), (0, size)],
        small_out=(1, size + size_b),
    )
    sends = fused_step(
        gots_a + [got_b],
        [flow_a, flow_b],
        [plan, plan_b],
        [size + size_b, size + size_b + extra],
        mark,
    )
    gots = [swap(sends[0], over_y), swap(sends[1], over_x)]
    shift = size
    mark = spaced(flow_a["keep"])
    size = half_of(flow_f)
    plan = dict(ins=joined(0, flow_f), outs=[(0, 0), (0, size)])
    sends = fused_step([got_f], [flow_f], [plan], [2 * size], mark)
    got_f = swap(sends[0], over_zz)
    mark = spaced(flow_f["keep"])
    size = half_of(flow_a)
    plan = dict(ins=[(0, 0), (1, 0)], outs=[(0, 0), (0, size)])
    sends = fused_step(gots, [flow_a], [plan], [2 * size], mark)
    got_a = swap(sends[0], over_z)
    size = half_of(flow_b)
    plan = dict(
        ins=[(1, shift), (0, shift)],
        small_in=(1, shift + 2 * size),
        outs=[(0, 0), (1, 0)],
        small_out=(0, size),
    )
    sends = fused_step(gots, [flow_b], [plan], [size + extra, size], flow_a["keep"])
    gots_b = [swap(sends[0], over_y), swap(sends[1], over_x)]
    mark = flow_b["keep"]
    got_f = after(got_f, mark)
    mark = spaced(got_f)
    size, size_b = half_of(flow_a), half_of(flow_b)
    plan = dict(ins=joined(0, flow_a), outs=[(0, 0), (0, size)])
    shift = 2 * size
    plan_b = dict(
        ins=[(1, 0), (2, 0)],
        small_in=(1, 2 * size_b),
        outs=[(0, shift), (0, shift + size_b)],
        small_out=(0, shift + 2 * size_b),
    )
    sends = fused_step(
        [got_a] + gots_b, [flow_a, flow_b], [plan, plan_b], [shift + 2 * size_b + extra], mark
    )
    got = swap(sends[0], over_zz)
    width = chan >> (dp_bits + 1)
    wide = hid >> (dp_bits + 1)
    small = flow_b["small"]
    conv_weight_grad, _, *vectors, w_in_mine, w_out_mine = pl.pallas_call(
        last_conv_kernel,
        out_shape=[
            jax.ShapeDtypeStruct((slots, chan >> dp_bits, chan), F32),
            vmem(small.shape, F32),
        ]
        + [jax.ShapeDtypeStruct((1, width), F32)] * 6
        + [
            jax.ShapeDtypeStruct((1, wide), F32),
            jax.ShapeDtypeStruct((chan >> (dp_bits + 1), hid), F32),
            jax.ShapeDtypeStruct((hid >> (dp_bits + 1), chan), F32),
        ],
        in_specs=[VMEM] * 6,
        out_specs=[VMEM] * 11,
        compiler_params=params(4),
        cost_estimate=claim(0),
        name="last_conv",
    )(
        near(got),
        near(flow_a["keep"]),
        near(small),
        near(flow_b["keep"]),
        near(got_f),
        near(flow_f["keep"]),
    )
    conv_bias_grad, gain_one_grad, bias_one_grad, b_out_grad, gain_two_grad, bias_two_grad, b_in_grad = [
        vector.reshape(-1) for vector in vectors
    ]
    return (
        block_output,
        input_grad,
        conv_weight_grad,
        conv_bias_grad,
        gain_one_grad,
        bias_one_grad,
        w_in_mine,
        b_in_grad,
        w_out_mine,
        b_out_grad,
        gain_two_grad,
        bias_two_grad,
    )


def narrow_enough(mesh):
    return mesh.shape["tap"] == 2 and mesh.shape["dp"] == 16


def solution(mesh):
    chosen = fast_shards if narrow_enough(mesh) else plain_shards
    return jax.shard_map(
        chosen,
        mesh=mesh,
        in_specs=(
            P("dp", None),
            P("tap", None, None),
            P("tap"),
            P(),
            P(),
            P(),
            P(),
            P(),
            P(),
            P(),
            P(),
            P(),
            P("dp"),
            P(),
            P(("dp", "tap"), None),
        ),
        out_specs=(
            P(("dp", "tap"), None),
            P(("dp", "tap"), None),
            P("tap", "dp", None),
            P(("dp", "tap")),
            P(("dp", "tap")),
            P(("dp", "tap")),
            P(("dp", "tap"), None),
            P(("dp", "tap")),
            P(("dp", "tap"), None),
            P(("dp", "tap")),
            P(("dp", "tap")),
            P(("dp", "tap")),
        ),
        check_vma=False,
    )
```
